32 devices in a mesh: dp: 2 (over x), ctx: 4 (over z), tensor: 4 (over y, core).
Axes of the slice: x: 2, y: 2, z: 4, core: 2. Of those that a mesh axis runs over, the one named last changes fastest.
Arguments:
- tokens: bfloat16 [6144, 2048], P(('dp', 'ctx')), may hold values from -6 to 6
- attn_gain: float32 [2048], replicated, may hold values from 0.5 to 1.5
- w_query: bfloat16 [2048, 2048], P(None, 'tensor'), may hold values from -0.125 to 0.125
- w_key: bfloat16 [2048, 2048], P(None, 'tensor'), may hold values from -0.125 to 0.125
- w_value: bfloat16 [2048, 2048], P(None, 'tensor'), may hold values from -0.125 to 0.125
- w_out: bfloat16 [2048, 2048], P('tensor'), may hold values from -0.75 to 0.75
- mlp_gain: float32 [2048], replicated, may hold values from 0.5 to 1.5
- w_gate: bfloat16 [2048, 8192], P(None, 'tensor'), may hold values from -0.125 to 0.125
- w_up: bfloat16 [2048, 8192], P(None, 'tensor'), may hold values from -0.125 to 0.125
- w_down: bfloat16 [8192, 2048], P('tensor'), may hold values from -0.0625 to 0.0625
- cotangent: bfloat16 [6144, 2048], P(('dp', 'ctx')), may hold values from -6 to 6
Outputs:
- output: bfloat16 [6144, 2048], P(('dp', 'ctx'))
- input_grad: bfloat16 [6144, 2048], P(('dp', 'ctx'))
- attn_gain_grad: float32 [2048], P(('dp', 'ctx'))
- query_grad: float32 [2048, 2048], P(('dp', 'ctx'), 'tensor')
- key_grad: float32 [2048, 2048], P(('dp', 'ctx'), 'tensor')
- value_grad: float32 [2048, 2048], P(('dp', 'ctx'), 'tensor')
- out_grad: float32 [2048, 2048], P('tensor', ('dp', 'ctx'))
- mlp_gain_grad: float32 [2048], P(('dp', 'ctx'))
- gate_grad: float32 [2048, 8192], P(('dp', 'ctx'), 'tensor')
- up_grad: float32 [2048, 8192], P(('dp', 'ctx'), 'tensor')
- down_grad: float32 [8192, 2048], P('tensor', ('dp', 'ctx'))
The draws below stay inside these ranges and needn't reach their ends.
All inputs are finite; a program needn't handle non-finite values.
Results may differ from the reference program's by a relative error of at most 0.022.
Values may be sent and summed in bfloat16 or wider, within the bound.
No kernel may reach another device: no remote copies, remote signals or barrier semaphores. Data moves between devices by JAX's collectives and lax.ppermute only.
A program may use at most 256 MiB of HBM per device.

```python
import jax
import jax.numpy as jnp
from jax import lax

D = 2048
HEADS = 32
FF = 8192
HEAD_DIM = 64
STRETCH = 768
LENGTH = 3072
TOKENS = 6144
N_DP = 2


def strengthened(entries, key, source, target, blocks, factor):
    owner, partner = [(jnp.arange(entries.shape[axis_at]) // (entries.shape[axis_at] // blocks)).reshape([-1 if axis == axis_at else 1 for axis in range(entries.ndim)]) for axis_at in (source, target)]
    chosen = jax.random.permutation(key, blocks)[partner]
    strong = (owner == chosen) | (owner == (partner + blocks // 2) % blocks)
    return jnp.where(strong, factor * entries, entries)


def steps_of(rng, extent, cuts, low, top_value):
    def one(position, shards_of):
        steps = jax.random.uniform(jax.random.fold_in(jax.random.fold_in(rng, 6), position), (shards_of,), jnp.float32, low / len(cuts), top_value / len(cuts))
        return jnp.repeat(jnp.exp(steps), extent[position] // shards_of).reshape((-1,) + (1,) * (len(extent) - position - 1))

    level = one(*cuts[0])
    for cut in cuts[1:]:
        level = level * one(*cut)
    return level


def noise(rng, shape, deviation, reach, shards=(), held_as=jnp.bfloat16):
    entries = deviation * jax.random.normal(rng, shape, jnp.float32)
    if shards:
        entries = entries * steps_of(rng, shape, shards, -0.22, 0.18)
    return jnp.clip(entries, -reach, reach).astype(held_as)


def heavy_noise(rng, extent, scale, limit, cuts, heavy, held_as=jnp.bfloat16):
    values = scale * jax.random.normal(rng, extent, jnp.float32)
    if cuts:
        values = values * steps_of(rng, extent, cuts, -0.22, 0.18)
    return jnp.clip(strengthened(values, jax.random.fold_in(rng, 3), *heavy), -limit, limit).astype(held_as)


def setup_inputs(seed: int = 0) -> dict:
    seeds = jax.random.split(jax.random.key(seed), 12)
    tokens = heavy_noise(seeds[0], (TOKENS, D), 1.0, 6.0, ((0, 8),), (0, 1, 8, 2.0))
    attn_gain = jnp.clip(1.0 + 0.1 * jax.random.normal(seeds[1], (D,), jnp.float32), 0.5, 1.5)
    w_query = noise(seeds[2], (D, D), D ** -0.5, 0.125, ((1, 4),))
    w_key = noise(seeds[3], (D, D), D ** -0.5, 0.125, ((1, 4),))
    w_value = noise(seeds[4], (D, D), D ** -0.5, 0.125, ((1, 4),))
    w_out = noise(seeds[5], (D, D), (max(D // 32, 1)) ** -0.5, 0.75, ((0, 4),))
    mlp_gain = jnp.clip(1.0 + 0.1 * jax.random.normal(seeds[6], (D,), jnp.float32), 0.5, 1.5)
    w_gate = noise(seeds[7], (D, FF), D ** -0.5, 0.125, ((1, 4),))
    w_up = noise(seeds[8], (D, FF), D ** -0.5, 0.125, ((1, 4),))
    w_down = noise(seeds[9], (FF, D), FF ** -0.5, 0.0625, ((0, 4),))
    cotangent = heavy_noise(seeds[10], (TOKENS, D), 1.0, 6.0, ((0, 8),), (0, 1, 8, 2.0))
    return dict(tokens=tokens, attn_gain=attn_gain, w_query=w_query, w_key=w_key, w_value=w_value, w_out=w_out, mlp_gain=mlp_gain, w_gate=w_gate, w_up=w_up, w_down=w_down, cotangent=cotangent)


@jax.custom_vjp
def low(v):
    return lax.optimization_barrier(v.astype(jnp.bfloat16)).astype(jnp.float32)

@jax.custom_vjp
def low_back(v):
    return v

def low_keep(v):
    return (low(v), None)

def low_pass(kept, grad):
    return (grad,)

def back_keep(v):
    return (v, None)

def back_low(kept, grad):
    return (low(grad),)
low.defvjp(low_keep, low_pass)
low_back.defvjp(back_keep, back_low)
EPS = 1e-05
THETA = 130000.0
HIGH = lax.Precision.HIGHEST

def rope_tables(positions):
    half = HEAD_DIM // 2
    freq = jnp.power(THETA, -jnp.arange(half, dtype=jnp.float32) * (2.0 / HEAD_DIM))
    angle = positions.astype(jnp.float32)[:, None] * freq[None, :]
    return (jnp.cos(angle), jnp.sin(angle))

def rotate(vector, cosine, sine):
    half = vector.shape[-1] // 2
    first = vector[..., :half]
    second = vector[..., half:]
    cos_h = cosine[:, None, :]
    sin_h = sine[:, None, :]
    return jnp.concatenate([first * cos_h - second * sin_h, second * cos_h + first * sin_h], axis=-1)

def rms_scale(vector, gain):
    inverse = lax.rsqrt(lax.optimization_barrier(jnp.mean(vector * vector, axis=-1, keepdims=True)) + EPS)
    return vector * inverse * gain

def layer(inputs, attn_gain, w_query, w_key, w_value, w_out, mlp_gain, w_gate, w_up, w_down):
    length = inputs.shape[0]
    positions = jnp.arange(length, dtype=jnp.int32)
    cosine, sine = rope_tables(positions)
    first_in = low(rms_scale(inputs, attn_gain))

    def project(weight):
        return jnp.dot(first_in, weight, precision=HIGH)
    queries = low(rotate(low_back(project(w_query)).reshape(length, HEADS, HEAD_DIM), cosine, sine))
    key_rows = low(rotate(low_back(project(w_key)).reshape(length, HEADS, HEAD_DIM), cosine, sine))
    value_rows = low(low_back(project(w_value))).reshape(length, HEADS, HEAD_DIM)
    blocks = length // STRETCH
    query_blocks = queries.reshape(blocks, STRETCH, HEADS, HEAD_DIM)
    starts = (jnp.arange(blocks, dtype=jnp.int32) * STRETCH).astype(jnp.int32)
    places = jnp.arange(length, dtype=jnp.int32)

    def block(pair):
        query_block, start = pair
        scores = jnp.einsum('qhd,khd->hqk', query_block, key_rows, precision=HIGH) * HEAD_DIM ** (-0.5)
        scores = low_back(scores)
        rows_at = start + jnp.arange(STRETCH, dtype=jnp.int32)
        allowed = rows_at[:, None] >= places[None, :]
        scores = jnp.where(allowed[None, :, :], scores, -1e+30)
        peak = lax.optimization_barrier(jnp.max(scores, axis=-1, keepdims=True))
        weights = jnp.exp(scores - peak)
        chance = weights / lax.optimization_barrier(jnp.sum(weights, axis=-1, keepdims=True))
        return jnp.einsum('hqk,khd->qhd', low(chance), value_rows, precision=HIGH)
    attended = lax.map(jax.checkpoint(block), (query_blocks, starts)).reshape(length, HEADS * HEAD_DIM)
    branch_one = low_back(jnp.dot(low(low_back(attended)), w_out, precision=HIGH))
    middle = inputs + branch_one
    second_in = low(rms_scale(middle, mlp_gain))
    gate_val = low_back(jnp.dot(second_in, w_gate, precision=HIGH))
    up_val = low_back(jnp.dot(second_in, w_up, precision=HIGH))
    hidden = low(jax.nn.silu(gate_val) * up_val)
    branch_two = low_back(jnp.dot(hidden, w_down, precision=HIGH))
    return middle + branch_two

def reference(tokens, attn_gain, w_query, w_key, w_value, w_out, mlp_gain, w_gate, w_up, w_down, cotangent):
    params = (attn_gain.astype(jnp.float32), w_query.astype(jnp.float32), w_key.astype(jnp.float32), w_value.astype(jnp.float32), w_out.astype(jnp.float32), mlp_gain.astype(jnp.float32), w_gate.astype(jnp.float32), w_up.astype(jnp.float32), w_down.astype(jnp.float32))
    inputs = tokens.astype(jnp.float32).reshape(N_DP, LENGTH, D)
    upstream = cotangent.astype(jnp.float32).reshape(N_DP, LENGTH, D)

    def one_sequence(totals, pair):
        sequence, grad_in = pair
        result, pull = jax.vjp(layer, sequence, *params)
        pulled = pull(grad_in)
        sums = tuple((total + extra for total, extra in zip(totals, pulled[1:])))
        return (sums, (result, pulled[0]))
    zeros = tuple((jnp.zeros_like(param) for param in params))
    totals, (results, input_back) = lax.scan(one_sequence, zeros, (inputs, upstream))
    output = results.reshape(TOKENS, D).astype(jnp.bfloat16)
    input_grad = input_back.reshape(TOKENS, D).astype(jnp.bfloat16)
    return (output, input_grad, totals[0], totals[1], totals[2], totals[3], totals[4], totals[5], totals[6], totals[7], totals[8])
```

```python
import functools

import jax
import jax.numpy as jnp
from jax import lax
from jax.experimental import pallas as pl
from jax.experimental.pallas import tpu as pltpu
from jax.sharding import PartitionSpec as P

HEAD_DIM = 64
EPS = 1e-05
THETA = 130000.0
BLOCK = 384
MIB = 1 << 20
LOW = jnp.bfloat16
F32 = jnp.float32
ANY = pl.BlockSpec(memory_space=pl.ANY)


def swap(value, axis, size, distance):
    return lax.ppermute(value, axis, [(i, i ^ distance) for i in range(size)])


def dot(left, right):
    return jnp.dot(left, right, preferred_element_type=F32)


def against(left, right):
    return lax.dot_general(left, right, (((1,), (1,)), ((), ())), preferred_element_type=F32)


def across(left, right):
    return lax.dot_general(left, right, (((0,), (0,)), ((), ())), preferred_element_type=F32)


def params(mib):
    return pltpu.CompilerParams(
        vmem_limit_bytes=mib * MIB, dimension_semantics=("arbitrary",)
    )


def cost(flops, moved, exps=0):
    return pl.CostEstimate(flops=int(flops), bytes_accessed=int(moved), transcendentals=int(exps))


def half_turn(rows, width):
    lane = lax.broadcasted_iota(jnp.int32, (1, width), 1)
    first = (lane % HEAD_DIM) < HEAD_DIM // 2
    return jnp.where(first, pltpu.roll(rows, width - 32, 1), pltpu.roll(rows, 32, 1))


def rope_tables(count):
    half = HEAD_DIM // 2
    freq = jnp.power(THETA, -jnp.arange(half, dtype=F32) * (2.0 / HEAD_DIM))
    angle = jnp.arange(count, dtype=jnp.int32).astype(F32)[:, None] * freq[None, :]
    cosine, sine = jnp.cos(angle), jnp.sin(angle)
    return (
        jnp.concatenate([cosine] * 4, axis=1),
        jnp.concatenate([-sine, sine, -sine, sine], axis=1),
    )


def project_kernel(me_ref, tok_ref, gain_ref, cos_ref, sin_ref, wq_ref, wk_ref, wv_ref, first_ref, out_ref):
    me = me_ref[0]
    rows = tok_ref[...].astype(F32)
    inverse = lax.rsqrt(jnp.mean(rows * rows, axis=-1, keepdims=True) + EPS)
    first = (rows * inverse * gain_ref[...]).astype(LOW)
    first_ref[...] = first
    cosine, sine = cos_ref[...], sin_ref[...]
    for place, weight in enumerate((wq_ref, wk_ref, wv_ref)):
        flat = dot(first, weight[...])
        for group in range(4):
            part = flat[:, group * 128 : (group + 1) * 128]
            if place < 2:
                part = part * cosine + half_turn(part, 128) * sine
            if place == 0:
                part = part * HEAD_DIM**-0.5
            out_ref[group ^ me, :, place * 128 : (place + 1) * 128] = part.astype(LOW)


def project(me, tokens, gain, cosine, sine, wq, wk, wv):
    rows, width = tokens.shape
    local = wq.shape[1]
    step = 256
    whole = lambda i, m: (0, 0)
    return pl.pallas_call(
        project_kernel,
        grid_spec=pltpu.PrefetchScalarGridSpec(
            num_scalar_prefetch=1,
            grid=(rows // step,),
            in_specs=[
                pl.BlockSpec((step, width), lambda i, m: (i, 0)),
                pl.BlockSpec((1, width), whole),
                pl.BlockSpec((step, 128), lambda i, m: (m[0] * (rows // step) + i, 0)),
                pl.BlockSpec((step, 128), lambda i, m: (m[0] * (rows // step) + i, 0)),
                pl.BlockSpec((width, local), whole),
                pl.BlockSpec((width, local), whole),
                pl.BlockSpec((width, local), whole),
            ],
            out_specs=[
                pl.BlockSpec((step, width), lambda i, m: (i, 0)),
                pl.BlockSpec((4, step, 384), lambda i, m: (0, i, 0)),
            ],
        ),
        out_shape=[
            jax.ShapeDtypeStruct((rows, width), LOW),
            jax.ShapeDtypeStruct((4, rows, 384), LOW),
        ],
        compiler_params=params(48),
        cost_estimate=cost(2 * rows * width * local * 3, 16 * MIB),
        name="project",
    )(me, tokens, gain.reshape(1, -1), cosine, sine, wq, wk, wv)


def own_lanes(rows, head):
    lane = lax.broadcasted_iota(jnp.int32, (1, 128), 1)
    inside = (lane < HEAD_DIM) if head == 0 else (lane >= HEAD_DIM)
    return jnp.where(inside, rows, jnp.zeros_like(rows))


def attend_kernel(me_ref, r0, r1, r2, r3, out_ref, raw_ref, lse_ref, held, sems):
    me = me_ref[0]
    here = pl.program_id(0)
    stretch = r0.shape[0]

    @pl.when(here == 0)
    def _():
        copies = [
            pltpu.make_async_copy(ref, held.at[pl.ds((me ^ k) * stretch, stretch)], sems.at[k])
            for k, ref in enumerate((r0, r1, r2, r3))
        ]
        for copy in copies:
            copy.start()
        for copy in copies:
            copy.wait()

    query = held[pl.ds(here * BLOCK, BLOCK), 0:128]
    queries = [own_lanes(query, head) for head in range(2)]

    def step(at, carry, diagonal):
        rows = pl.ds(at * BLOCK, BLOCK)
        keys, values = held[rows, 128:256], held[rows, 256:384]
        out = []
        for head in range(2):
            peak, mass, total = carry[3 * head : 3 * head + 3]
            scores = against(queries[head], keys)
            if diagonal:
                down = lax.broadcasted_iota(jnp.int32, (BLOCK, BLOCK), 0)
                along = lax.broadcasted_iota(jnp.int32, (BLOCK, BLOCK), 1)
                scores = jnp.where(down >= along, scores, -1e30)
            top = jnp.maximum(peak, jnp.max(scores, axis=-1, keepdims=True))
            weights = jnp.exp(scores - top)
            fade = jnp.exp(peak - top)
            mass = mass * fade + jnp.sum(weights, axis=-1, keepdims=True)
            total = total * fade + dot(weights.astype(LOW), values)
            out += [top, mass, total]
        return tuple(out)

    start = (
        jnp.full((BLOCK, 1), -1e30, F32),
        jnp.zeros((BLOCK, 1), F32),
        jnp.zeros((BLOCK, 128), F32),
    ) * 2
    carry = lax.fori_loop(0, here, lambda at, c: step(at, c, False), start)
    peak0, mass0, total0, peak1, mass1, total1 = step(here, carry, True)
    lane = lax.broadcasted_iota(jnp.int32, (1, 128), 1)
    mixed = jnp.where(lane < HEAD_DIM, total0 / mass0, total1 / mass1)
    raw_ref[...] = mixed
    out_ref[0] = mixed.astype(LOW)
    turned = jnp.where(lane < HEAD_DIM, peak0 + jnp.log(mass0), peak1 + jnp.log(mass1)).T
    lse_ref[0:8] = turned[0:8]
    lse_ref[8:16] = turned[64:72]


def attend(me, pieces):
    stretch = pieces[0].shape[0]
    length = 4 * stretch
    per = stretch // BLOCK
    pairs = length * length
    return pl.pallas_call(
        attend_kernel,
        grid_spec=pltpu.PrefetchScalarGridSpec(
            num_scalar_prefetch=1,
            grid=(length // BLOCK,),
            in_specs=[ANY] * 4,
            out_specs=[
                pl.BlockSpec((1, BLOCK, 128), lambda i, m: ((i // per) ^ m[0], i % per, 0)),
                pl.BlockSpec((BLOCK, 128), lambda i, m: (i, 0)),
                pl.BlockSpec((16, BLOCK), lambda i, m: (0, i)),
            ],
            scratch_shapes=[pltpu.VMEM((length, 384), LOW), pltpu.SemaphoreType.DMA((4,))],
        ),
        out_shape=[
            jax.ShapeDtypeStruct((4, stretch, 128), LOW),
            jax.ShapeDtypeStruct((length, 128), F32),
            jax.ShapeDtypeStruct((16, length), F32),
        ],
        compiler_params=params(32),
        cost_estimate=cost(2 * pairs * 128 * 2 * 2, 6 * MIB, pairs),
        name="attend",
    )(me, *pieces)


def attend_back_kernel(
    me_ref, r0, r1, r2, r3, u0, u1, u2, u3, raw_ref, lse_ref, cos_ref, sin_ref, out_ref,
    held, up, query_at, up_at, delta, query_sum, key_sum, value_sum, sems,
):
    me = me_ref[0]
    here = pl.program_id(0)
    count = pl.num_programs(0)
    stretch = r0.shape[0]
    per = stretch // BLOCK

    @pl.when(here == 0)
    def _():
        copies = []
        for k, (ref, other) in enumerate(zip((r0, r1, r2, r3), (u0, u1, u2, u3))):
            rows = pl.ds((me ^ k) * stretch, stretch)
            copies.append(pltpu.make_async_copy(ref, held.at[rows], sems.at[k]))
            copies.append(pltpu.make_async_copy(other, up.at[rows], sems.at[4 + k]))
        for copy in copies:
            copy.start()
        for copy in copies:
            copy.wait()
        query_sum[...] = jnp.zeros_like(query_sum)

        def prepare(at, _):
            rows = pl.ds(at * BLOCK, BLOCK)
            query, upstream = held[rows, 0:128], up[rows, :]
            turned = (upstream.astype(F32) * raw_ref[rows, :]).T
            for head in range(2):
                query_at[head, rows, :] = own_lanes(query, head)
                up_at[head, rows, :] = own_lanes(upstream, head)
                total = jnp.sum(turned[head * 64 : head * 64 + 64], axis=0, keepdims=True)
                delta[at, head * 8 : head * 8 + 8, :] = jnp.broadcast_to(total, (8, BLOCK))
            return 0

        lax.fori_loop(0, count, prepare, 0)

    here_rows = pl.ds(here * BLOCK, BLOCK)
    key, value = held[here_rows, 128:256], held[here_rows, 256:384]
    keys = [own_lanes(key, head) for head in range(2)]
    values = [own_lanes(value, head) for head in range(2)]

    def step(at, diagonal):
        rows = pl.ds(at * BLOCK, BLOCK)
        query, upstream = held[rows, 0:128], up[rows, :]
        key_total = value_total = query_total = None
        for head in range(2):
            scores = against(keys[head], query)
            lse = lse_ref[at, head * 8 : head * 8 + 1, :]
            chance = jnp.exp(scores - lse)
            if diagonal:
                down = lax.broadcasted_iota(jnp.int32, (BLOCK, BLOCK), 0)
                along = lax.broadcasted_iota(jnp.int32, (BLOCK, BLOCK), 1)
                chance = jnp.where(along >= down, chance, 0.0)
            chance_back = against(values[head], upstream)
            shift = delta[at, head * 8 : head * 8 + 1, :]
            score_back = (chance * (chance_back - shift)).astype(LOW)
            value_part = dot(chance.astype(LOW), up_at[head, rows, :])
            key_part = dot(score_back, query_at[head, rows, :])
            query_part = across(score_back, keys[head])
            if head == 0:
                value_total, key_total, query_total = value_part, key_part, query_part
            else:
                value_total += value_part
                key_total += key_part
                query_total += query_part
        query_sum[rows, :] += query_total
        return key_total, value_total

    key_sum[...], value_sum[...] = step(here, True)

    def later(at, _):
        key_total, value_total = step(at, False)
        key_sum[...] += key_total
        value_sum[...] += value_total
        return 0

    lax.fori_loop(here + 1, count, later, 0)

    def back_rope(rows, at):
        places = pl.ds(at * BLOCK, BLOCK)
        return rows * cos_ref[places, :] - half_turn(rows, 128) * sin_ref[places, :]

    slot = (here // per) ^ me
    inner = pl.ds((here % per) * BLOCK, BLOCK)
    out_ref[slot, inner, 128:256] = back_rope(key_sum[...], here).astype(LOW)
    out_ref[slot, inner, 256:384] = value_sum[...].astype(LOW)

    @pl.when(here == count - 1)
    def _():
        def finish(at, _):
            rows = query_sum[pl.ds(at * BLOCK, BLOCK), :] * HEAD_DIM**-0.5
            place = pl.ds((at % per) * BLOCK, BLOCK)
            out_ref[(at // per) ^ me, place, 0:128] = back_rope(rows, at).astype(LOW)
            return 0

        lax.fori_loop(0, count, finish, 0)


def attend_back(me, pieces, upstreams, raw, lse, cosine, sine):
    stretch = pieces[0].shape[0]
    length = 4 * stretch
    count = length // BLOCK
    pairs = length * length
    lse = lse.reshape(16, count, BLOCK).transpose(1, 0, 2)
    whole = lambda i, m: (0, 0)
    return pl.pallas_call(
        attend_back_kernel,
        grid_spec=pltpu.PrefetchScalarGridSpec(
            num_scalar_prefetch=1,
            grid=(count,),
            in_specs=[ANY] * 8
            + [
                pl.BlockSpec((length, 128), whole),
                pl.BlockSpec((count, 16, BLOCK), lambda i, m: (0, 0, 0)),
                pl.BlockSpec((length, 128), whole),
                pl.BlockSpec((length, 128), whole),
            ],
            out_specs=pl.BlockSpec((4, stretch, 384), lambda i, m: (0, 0, 0)),
            scratch_shapes=[
                pltpu.VMEM((length, 384), LOW),
                pltpu.VMEM((length, 128), LOW),
                pltpu.VMEM((2, length, 128), LOW),
                pltpu.VMEM((2, length, 128), LOW),
                pltpu.VMEM((count, 16, BLOCK), F32),
                pltpu.VMEM((length, 128), F32),
                pltpu.VMEM((BLOCK, 128), F32),
                pltpu.VMEM((BLOCK, 128), F32),
                pltpu.SemaphoreType.DMA((8,)),
            ],
        ),
        out_shape=jax.ShapeDtypeStruct((4, stretch, 384), LOW),
        compiler_params=params(48),
        cost_estimate=cost(2 * pairs * 128 * 5 * 2, 12 * MIB, pairs),
        name="attend_back",
    )(me, *pieces, *upstreams, raw, lse, cosine, sine)


def place_of(quarter):
    return (quarter & 1) * 2 + (quarter >> 1)


def quarters_kernel(t_ref, *refs, count, turned):
    t = t_ref[0]
    out_ref = refs[-1]
    rows = out_ref.shape[1]
    total = None
    for left, right in zip(refs[:count], refs[count : 2 * count]):
        part = (against if turned else dot)(left[...], right[...])
        total = part if total is None else total + part
    for quarter in range(4):
        out_ref[place_of(quarter ^ t)] = total[quarter * rows : (quarter + 1) * rows].astype(LOW)


def quarters(t, lefts, rights, turned, step, name):
    rows, depth = lefts[0].shape
    width = rights[0].shape[0] if turned else rights[0].shape[1]
    if turned:
        spec = pl.BlockSpec((step, depth), lambda i, m: (i, 0))
    else:
        spec = pl.BlockSpec((depth, step), lambda i, m: (0, i))
    count = len(lefts)
    return pl.pallas_call(
        functools.partial(quarters_kernel, count=count, turned=turned),
        grid_spec=pltpu.PrefetchScalarGridSpec(
            num_scalar_prefetch=1,
            grid=(width // step,),
            in_specs=[pl.BlockSpec((rows, depth), lambda i, m: (0, 0))] * count + [spec] * count,
            out_specs=pl.BlockSpec((4, rows // 4, step), lambda i, m: (0, 0, i)),
        ),
        out_shape=jax.ShapeDtypeStruct((4, rows // 4, width), LOW),
        compiler_params=params(48),
        cost_estimate=cost(2 * rows * depth * width * count, count * (rows + width) * depth * 2 + rows * width * 2),
        name=name,
    )(t, *lefts, *rights)


def sum_quarters(slots):
    other = swap(slots[2:], "tensor", 4, 1)
    pair = slots[:2].astype(F32) + other.astype(F32)
    across_y = swap(pair[1].astype(LOW), "tensor", 4, 2)
    return pair[0] + across_y.astype(F32)


def spread(quarter):
    two = swap(quarter, "tensor", 4, 2)
    one = swap(quarter, "tensor", 4, 1)
    three = swap(two, "tensor", 4, 1)
    return (quarter, one, two, three)


def join_kernel(t_ref, q0, q1, q2, q3, out_ref, sems):
    t = t_ref[0]
    rows = q0.shape[0]
    copies = [
        pltpu.make_async_copy(ref, out_ref.at[pl.ds((t ^ k) * rows, rows)], sems.at[k])
        for k, ref in enumerate((q0, q1, q2, q3))
    ]
    for copy in copies:
        copy.start()
    for copy in copies:
        copy.wait()


def join(t, pieces):
    rows, width = pieces[0].shape
    return pl.pallas_call(
        join_kernel,
        grid_spec=pltpu.PrefetchScalarGridSpec(
            num_scalar_prefetch=1,
            grid=(1,),
            in_specs=[ANY] * 4,
            out_specs=ANY,
            scratch_shapes=[pltpu.SemaphoreType.DMA((4,))],
        ),
        out_shape=jax.ShapeDtypeStruct((4 * rows, width), pieces[0].dtype),
        compiler_params=params(16),
        cost_estimate=cost(0, 16 * rows * width),
        name="join",
    )(t, *pieces)


def feed_kernel(t_ref, q0, q1, q2, q3, wg_ref, wu_ref, hb_ref, rows_ref, hid_ref, gb_ref, ub_ref, held, sems):
    t = t_ref[0]
    rows = q0.shape[0]
    here = pl.program_id(0)

    @pl.when(here == 0)
    def _():
        copies = [
            pltpu.make_async_copy(ref, held.at[pl.ds((t ^ k) * rows, rows)], sems.at[k])
            for k, ref in enumerate((q0, q1, q2, q3))
        ]
        for copy in copies:
            copy.start()
        for copy in copies:
            copy.wait()
        pltpu.make_async_copy(held, rows_ref, sems.at[4]).start()

    for part in range(3):
        at = slice(part * 256, (part + 1) * 256)
        second = held[at, :]
        gate = dot(second, wg_ref[...])
        up = dot(second, wu_ref[...])
        back = hb_ref[at, :].astype(F32)
        sig = 1.0 / (1.0 + jnp.exp(-gate))
        swish = gate * sig
        hid_ref[at, :] = (swish * up).astype(LOW)
        gb_ref[at, :] = (back * up * sig * (1.0 + gate * (1.0 - sig))).astype(LOW)
        ub_ref[at, :] = (back * swish).astype(LOW)

    @pl.when(here == pl.num_programs(0) - 1)
    def _():
        pltpu.make_async_copy(held, rows_ref, sems.at[4]).wait()


def feed(t, pieces, w_gate, w_up, hidden_back):
    rows, width = pieces[0].shape
    rows = 4 * rows
    units = w_gate.shape[1]
    step = 256
    col = lambda i, m: (0, i)
    block = pl.BlockSpec((rows, step), col)
    low = jax.ShapeDtypeStruct((rows, units), LOW)
    return pl.pallas_call(
        feed_kernel,
        grid_spec=pltpu.PrefetchScalarGridSpec(
            num_scalar_prefetch=1,
            grid=(units // step,),
            in_specs=[ANY] * 4 + [pl.BlockSpec((width, step), col)] * 2 + [block],
            out_specs=[ANY, block, block, block],
            scratch_shapes=[pltpu.VMEM((rows, width), LOW), pltpu.SemaphoreType.DMA((5,))],
        ),
        out_shape=[jax.ShapeDtypeStruct((rows, width), LOW), low, low, low],
        compiler_params=params(48),
        cost_estimate=cost(4 * rows * width * units, 38 * MIB, rows * units),
        name="feed",
    )(t, *pieces, w_gate, w_up, hidden_back)


def branch_back_kernel(t_ref, q0, q1, q2, q3, w_ref, rows_ref, out_ref, held, sems):
    t = t_ref[0]
    rows = q0.shape[0]
    copies = [
        pltpu.make_async_copy(ref, held.at[pl.ds((t ^ k) * rows, rows)], sems.at[k])
        for k, ref in enumerate((q0, q1, q2, q3))
    ]
    for copy in copies:
        copy.start()
    for copy in copies:
        copy.wait()
    keep = pltpu.make_async_copy(held, rows_ref, sems.at[4])
    keep.start()
    for part in range(3):
        at = slice(part * 256, (part + 1) * 256)
        flat = against(held[at, :], w_ref[...]).astype(LOW)
        for slot in range(4):
            out_ref[slot, at, :] = flat[:, slot * 128 : (slot + 1) * 128]
    keep.wait()


def branch_back(t, pieces, weight):
    rows, width = pieces[0].shape
    rows = 4 * rows
    local = weight.shape[0]
    return pl.pallas_call(
        branch_back_kernel,
        grid_spec=pltpu.PrefetchScalarGridSpec(
            num_scalar_prefetch=1,
            grid=(1,),
            in_specs=[ANY] * 4 + [pl.BlockSpec((local, width), lambda i, m: (0, 0))],
            out_specs=[ANY, pl.BlockSpec((4, rows, 128), lambda i, m: (0, 0, 0))],
            scratch_shapes=[pltpu.VMEM((rows, width), LOW), pltpu.SemaphoreType.DMA((5,))],
        ),
        out_shape=[
            jax.ShapeDtypeStruct((rows, width), LOW),
            jax.ShapeDtypeStruct((4, rows, 128), LOW),
        ],
        compiler_params=params(32),
        cost_estimate=cost(2 * rows * width * local, 8 * MIB),
        name="branch_back",
    )(t, *pieces, weight)


def normalize(vector):
    inverse = lax.rsqrt(jnp.mean(vector * vector, axis=-1, keepdims=True) + EPS)
    return (vector * inverse, inverse)


def norm_back(grad_rows, normed, inverse, gain):
    scaled = grad_rows * gain
    gain_grad = jnp.sum(grad_rows * normed, axis=0)
    row_back = inverse * (scaled - normed * jnp.mean(scaled * normed, axis=-1, keepdims=True))
    return (row_back, gain_grad)


def per_device(
    dp_size, tokens, attn_gain, w_query, w_key, w_value, w_out, mlp_gain, w_gate, w_up, w_down, cotangent
):
    rows_here, width = tokens.shape
    local_width = w_query.shape[1]
    units = w_gate.shape[1]
    quarter_rows = rows_here // 4
    me, t, d = lax.axis_index("ctx"), lax.axis_index("tensor"), lax.axis_index("dp")
    me_at, t_at = me.astype(jnp.int32).reshape(1), t.astype(jnp.int32).reshape(1)
    order = me ^ jnp.arange(4)
    half = width // 2

    def quarter_of(rows):
        return lax.dynamic_slice_in_dim(rows, t * quarter_rows, quarter_rows, 0)

    def dp_half(value, which, axis):
        size = value.shape[axis] // 2
        return lax.dynamic_slice_in_dim(value, which * size, size, axis)

    def over_ctx(slots):
        return [slots[0]] + [swap(slots[k], "ctx", 4, k) for k in range(1, 4)]

    cosine, sine = rope_tables(4 * rows_here)
    first_in, slots = project(me_at, tokens, attn_gain, cosine, sine, w_query, w_key, w_value)
    pieces = over_ctx(slots)

    hidden_back = against(cotangent, w_down)
    w_out_slots = w_out.reshape(4, 128, width)[order].reshape(local_width, width)
    w_slots = jnp.concatenate(
        [w.reshape(width, 4, 1, 128) for w in (w_query, w_key, w_value)], axis=2
    )[:, order].reshape(width, 4 * 384)
    tokens_mine = quarter_of(tokens).astype(F32)
    cot_mine = quarter_of(cotangent).astype(F32)

    mixed, raw, lse = attend(me_at, pieces)
    attended = jnp.concatenate(over_ctx(mixed), axis=1)
    slots = quarters(t_at, [attended], [w_out_slots], False, 512, "join_heads")
    middle = tokens_mine + sum_quarters(slots)
    normed_two, inverse_two = normalize(middle)
    second_mine = (normed_two * mlp_gain).astype(LOW)

    second_in, hidden, gate_back, up_back = feed(t_at, spread(second_mine), w_gate, w_up, hidden_back)
    slots = quarters(t_at, [gate_back, up_back], [w_gate, w_up], True, 256, "feed_back")
    second_sum = sum_quarters(slots)
    slots = quarters(t_at, [hidden], [w_down], False, 256, "feed_down")
    output = join(t_at, spread((middle + sum_quarters(slots)).astype(LOW)))
    middle_back, mlp_gain_part = norm_back(second_sum, normed_two, inverse_two, mlp_gain)
    middle_grad = cot_mine + middle_back
    branch_low, slots = branch_back(t_at, spread(middle_grad.astype(LOW)), w_out_slots)
    upstreams = over_ctx(slots)

    slots = attend_back(me_at, pieces, upstreams, raw, lse, cosine, sine)
    back = jnp.concatenate(over_ctx(slots), axis=1)
    back_slots = quarters(t_at, [back], [w_slots], True, 256, "project_back")
    first_sum = sum_quarters(back_slots)
    normed_one, inverse_one = normalize(tokens_mine)
    input_back, attn_gain_part = norm_back(first_sum, normed_one, inverse_one, attn_gain)
    input_grad = join(t_at, spread((middle_grad + input_back).astype(LOW)))

    first_mine = quarter_of(first_in)
    far = jnp.stack([swap(first_mine, "ctx", 4, k) for k in range(1, 4)])
    far_two = swap(far, "tensor", 4, 2)
    far_one = swap(far, "tensor", 4, 1)
    far_three = swap(far_two, "tensor", 4, 1)
    far_all = jnp.stack([far, far_one, far_two, far_three], axis=1)[:, t ^ jnp.arange(4)]
    first_all = jnp.concatenate(
        [first_in, far_all.reshape(3 * rows_here, width)], axis=0
    )
    qkv_part = across(first_all, slots.reshape(4 * rows_here, 384))
    out_part = across(attended, branch_low).reshape(4, 128, width)[order].reshape(local_width, width)

    def rows_over_dp(part):
        if dp_size == 2:
            other = swap(dp_half(part, 1 - d, 0).astype(LOW), "dp", 2, 1)
            return dp_half(part, d, 0) + other.astype(F32)
        return lax.psum_scatter(part.astype(LOW), "dp", scatter_dimension=0, tiled=True).astype(F32)

    def columns_over_dp(part):
        if dp_size == 2:
            other = swap(dp_half(part, 1 - d, 1).astype(LOW), "dp", 2, 1)
            return dp_half(part, d, 1) + other.astype(F32)
        return lax.psum_scatter(part.astype(LOW), "dp", scatter_dimension=1, tiled=True).astype(F32)

    def over_stretches(part, axis):
        return lax.psum_scatter(
            part.astype(LOW), "ctx", scatter_dimension=axis, tiled=True
        ).astype(F32)

    if dp_size == 2:
        hidden_two = jnp.concatenate([hidden, swap(hidden, "dp", 2, 1)], axis=0)
        gate_two = jnp.concatenate([gate_back, swap(gate_back, "dp", 2, 1)], axis=0)
        up_two = jnp.concatenate([up_back, swap(up_back, "dp", 2, 1)], axis=0)

        def two_halves(rows):
            other = swap(dp_half(rows, 1 - d, 1), "dp", 2, 1)
            return jnp.concatenate([dp_half(rows, d, 1), other], axis=0)

        cot_two, second_two = two_halves(cotangent), two_halves(second_in)
        down_part = across(hidden_two, cot_two)
        gate_part = across(second_two, gate_two)
        up_part = across(second_two, up_two)
    else:
        down_part = columns_over_dp(across(hidden, cotangent))
        gate_part = rows_over_dp(across(second_in, gate_back))
        up_part = rows_over_dp(across(second_in, up_back))
    down_grad = over_stretches(down_part, 1)
    gate_grad = over_stretches(gate_part, 0)
    up_grad = over_stretches(up_part, 0)
    out_grad = over_stretches(columns_over_dp(out_part), 1)
    share = out_grad.shape[1]

    qkv_part = rows_over_dp(qkv_part).astype(LOW).reshape(4, share, 384)[order]
    parts = jnp.stack(over_ctx(qkv_part))[order]
    qkv = parts.reshape(4, share, 3, 128).transpose(2, 1, 0, 3).reshape(3, share, local_width)
    qkv = qkv.astype(F32)

    gains = jnp.stack([attn_gain_part, mlp_gain_part])
    gains = gains + swap(gains, "tensor", 4, 1)
    gains = gains + swap(gains, "tensor", 4, 2)
    if dp_size == 2:
        gains = dp_half(gains, d, 1) + swap(dp_half(gains, 1 - d, 1), "dp", 2, 1)
    else:
        gains = lax.psum_scatter(gains, "dp", scatter_dimension=1, tiled=True)
    gains = gains.reshape(2, 4, share).transpose(1, 0, 2)[order]
    gains = sum(over_ctx(gains))

    return (
        output,
        input_grad,
        gains[0],
        qkv[0],
        qkv[1],
        qkv[2],
        out_grad,
        gains[1],
        gate_grad,
        up_grad,
        down_grad,
    )


def solution(mesh):
    rows, tensor = ("dp", "ctx"), "tensor"
    in_specs = (
        P(rows, None),
        P(),
        P(None, tensor),
        P(None, tensor),
        P(None, tensor),
        P(tensor, None),
        P(),
        P(None, tensor),
        P(None, tensor),
        P(tensor, None),
        P(rows, None),
    )
    out_specs = (
        P(rows, None),
        P(rows, None),
        P(rows),
        P(rows, tensor),
        P(rows, tensor),
        P(rows, tensor),
        P(tensor, rows),
        P(rows),
        P(rows, tensor),
        P(rows, tensor),
        P(tensor, rows),
    )
    return jax.shard_map(
        functools.partial(per_device, mesh.shape["dp"]),
        mesh=mesh,
        in_specs=in_specs,
        out_specs=out_specs,
        check_vma=False,
    )
```

```python
import functools

import jax
import jax.numpy as jnp
from jax import lax
from jax.experimental import pallas as pl
from jax.experimental.pallas import tpu as pltpu
from jax.sharding import PartitionSpec as P

HEAD_DIM = 64
EPS = 1e-05
THETA = 130000.0
BLOCK = 384
MIB = 1 << 20
MOST = 62
COSTS = {
    "attend": 20, "attend_back": 22, "feed": 6, "feed_back": 6, "feed_down": 5, "hidden_back": 4, "wgrad": 4,
    "wgrads": 10, "out_wgrad": 4, "project_back": 5, "rope_tables": 3,
}
LOW = jnp.bfloat16
F32 = jnp.float32
ANY = pl.BlockSpec(memory_space=pl.ANY)


CTX, TENSOR = ("hi", "lo"), ("y", "core")


def swap(value, axis, distance):
    size = 2 if axis == "dp" else 4
    return lax.ppermute(value, axis, [(i, i ^ distance) for i in range(size)])


def dot(left, right):
    return jnp.dot(left, right, preferred_element_type=F32)


def against(left, right):
    return lax.dot_general(left, right, (((1,), (1,)), ((), ())), preferred_element_type=F32)


def across(left, right):
    return lax.dot_general(left, right, (((0,), (0,)), ((), ())), preferred_element_type=F32)


def shaped(shape, dtype=LOW):
    return jax.ShapeDtypeStruct(shape, dtype)


def call(kernel, name, index, grid, inputs, in_specs, outs, out_specs, scratch=(), mib=MOST, after=()):
    count = len(inputs)

    def body(index_ref, *refs):
        kernel(index_ref, *refs[:count], *refs[count + len(after) :])

    return pl.pallas_call(
        body,
        grid_spec=pltpu.PrefetchScalarGridSpec(
            num_scalar_prefetch=1,
            grid=grid,
            in_specs=list(in_specs) + [ANY] * len(after),
            out_specs=out_specs,
            scratch_shapes=list(scratch),
        ),
        out_shape=outs,
        compiler_params=pltpu.CompilerParams(
            vmem_limit_bytes=mib * MIB, dimension_semantics=("arbitrary",) * len(grid)
        ),
        cost_estimate=pl.CostEstimate(flops=0, bytes_accessed=int(COSTS.get(name, 0) * 3.5 * MIB), transcendentals=0),
        name=name,
    )(index, *inputs, *after)


ME, T = 0, 1


def copy_all(pairs, sems):
    copies = [pltpu.make_async_copy(a, b, sems.at[k]) for k, (a, b) in enumerate(pairs)]
    for copy in copies:
        copy.start()
    for copy in copies:
        copy.wait()


def half_turn(rows):
    lane = lax.broadcasted_iota(jnp.int32, (1, 128), 1)
    first = (lane % HEAD_DIM) < HEAD_DIM // 2
    return jnp.where(first, pltpu.roll(rows, 96, 1), pltpu.roll(rows, 32, 1))


def rope_freq():
    half = HEAD_DIM // 2
    freq = jnp.power(THETA, -jnp.arange(half, dtype=F32) * (2.0 / HEAD_DIM))
    return jnp.concatenate([freq] * 4)


def rope_tables(positions):
    sign = jnp.where((jnp.arange(128) % HEAD_DIM) < HEAD_DIM // 2, -1.0, 1.0)
    angle = positions.astype(F32)[:, None] * rope_freq()[None, :]
    return jnp.cos(angle), jnp.sin(angle) * sign


def project_kernel(ix, tok_ref, gain_ref, cos_ref, sin_ref, wq_ref, wk_ref, wv_ref, first_ref, o0, o1, o2, o3, held):
    me = ix[ME]
    rows = tok_ref[...].astype(F32)
    inverse = lax.rsqrt(jnp.mean(rows * rows, axis=-1, keepdims=True) + EPS)
    first = (rows * inverse * gain_ref[...]).astype(LOW)
    first_ref[...] = first
    cosine, sine = cos_ref[...], sin_ref[...]
    for place, weight in enumerate((wq_ref, wk_ref, wv_ref)):
        flat = dot(first, weight[...])
        for group in range(4):
            part = flat[:, group * 128 : (group + 1) * 128]
            if place < 2:
                part = part * cosine + half_turn(part) * sine
            if place == 0:
                part = part * HEAD_DIM**-0.5
            held[group, :, place * 128 : (place + 1) * 128] = part.astype(LOW)
    for slot, out in enumerate((o0, o1, o2, o3)):
        out[...] = held[slot ^ me]


def project(ix, tokens, gain, tables, weights):
    rows, width = tokens.shape
    local = weights[0].shape[1]
    step = 256
    whole = lambda i, m: (0, 0)
    along = lambda i, m: (i, 0)
    return call(
        project_kernel, "project", ix, (rows // step,),
        [tokens, gain.reshape(1, -1), *tables, *weights],
        [pl.BlockSpec((step, width), along), pl.BlockSpec((1, width), whole)]
        + [pl.BlockSpec((step, 128), along)] * 2 + [pl.BlockSpec((width, local), whole)] * 3,
        [shaped((rows, width))] + [shaped((rows, 384))] * 4,
        [pl.BlockSpec((step, width), along)] + [pl.BlockSpec((step, 384), along)] * 4,
        [pltpu.VMEM((4, step, 384), LOW)],
    )


def own_lanes(rows, head):
    lane = lax.broadcasted_iota(jnp.int32, (1, 128), 1)
    inside = (lane < HEAD_DIM) if head == 0 else (lane >= HEAD_DIM)
    return jnp.where(inside, rows, jnp.zeros_like(rows))


def attend_kernel(ix, r0, r1, r2, r3, o0, o1, o2, o3, raw_ref, lse_ref, held, sems):
    me = ix[ME]
    turn = pl.program_id(0)
    stretch = r0.shape[0]
    per = stretch // BLOCK
    here = ((turn // per) ^ me) * per + turn % per

    @pl.when(turn == 0)
    def _():
        copy_all(
            [(r, held.at[pl.ds((me ^ k) * stretch, stretch)]) for k, r in enumerate((r0, r1, r2, r3))],
            sems,
        )

    query = held[pl.ds(here * BLOCK, BLOCK), 0:128]
    queries = [own_lanes(query, head) for head in range(2)]

    def step(at, carry, diagonal):
        rows = pl.ds(at * BLOCK, BLOCK)
        keys, values = held[rows, 128:256], held[rows, 256:384]
        out = []
        for head in range(2):
            peak, mass, total = carry[3 * head : 3 * head + 3]
            scores = against(queries[head], keys)
            if diagonal:
                down = lax.broadcasted_iota(jnp.int32, (BLOCK, BLOCK), 0)
                along = lax.broadcasted_iota(jnp.int32, (BLOCK, BLOCK), 1)
                scores = jnp.where(down >= along, scores, -1e30)
            top = jnp.maximum(peak, jnp.max(scores, axis=-1, keepdims=True))
            weights = jnp.exp(scores - top)
            fade = jnp.exp(peak - top)
            mass = mass * fade + jnp.sum(weights, axis=-1, keepdims=True)
            total = total * fade + dot(weights.astype(LOW), values)
            out += [top, mass, total]
        return tuple(out)

    start = (
        jnp.full((BLOCK, 1), -1e30, F32),
        jnp.zeros((BLOCK, 1), F32),
        jnp.zeros((BLOCK, 128), F32),
    ) * 2
    carry = lax.fori_loop(0, here, lambda at, c: step(at, c, False), start)
    peak0, mass0, total0, peak1, mass1, total1 = step(here, carry, True)
    lane = lax.broadcasted_iota(jnp.int32, (1, 128), 1)
    mixed = jnp.where(lane < HEAD_DIM, total0 / mass0, total1 / mass1)
    raw_ref[...] = mixed
    for slot, out in enumerate((o0, o1, o2, o3)):

        @pl.when(turn // per == slot)
        def _():
            out[...] = mixed.astype(LOW)

    turned = jnp.where(lane < HEAD_DIM, peak0 + jnp.log(mass0), peak1 + jnp.log(mass1)).T
    lse_ref[0, 0:8] = turned[0:8]
    lse_ref[0, 8:16] = turned[64:72]


def attend(ix, pieces, after):
    stretch = pieces[0].shape[0]
    length = 4 * stretch
    per = stretch // BLOCK
    count = length // BLOCK

    def place(i, m):
        return ((i // per) ^ m[ME]) * per + i % per

    def slot_spec(slot):
        return pl.BlockSpec((BLOCK, 128), lambda i, m: (jnp.clip(i - slot * per, 0, per - 1), 0))

    return call(
        attend_kernel, "attend", ix, (count,), list(pieces), [ANY] * 4,
        [shaped((stretch, 128))] * 4 + [shaped((length, 128), F32), shaped((count, 16, BLOCK), F32)],
        [slot_spec(slot) for slot in range(4)]
        + [
            pl.BlockSpec((BLOCK, 128), lambda i, m: (place(i, m), 0)),
            pl.BlockSpec((1, 16, BLOCK), lambda i, m: (place(i, m), 0, 0)),
        ],
        [pltpu.VMEM((length, 384), LOW), pltpu.SemaphoreType.DMA((4,))],
        after=after,
    )


def attend_back_kernel(
    ix, r0, r1, r2, r3, u0, u1, u2, u3, raw_ref, lse_ref, cos_ref, sin_ref, o0, o1, o2, o3,
    held, up, query_at, up_at, delta, query_sum, key_sum, value_sum, sems,
):
    me = ix[ME]
    turn = pl.program_id(0)
    count = pl.num_programs(0)
    stretch = r0.shape[0]
    per = stretch // BLOCK
    here = ((turn // per) ^ me) * per + turn % per

    @pl.when(turn == 0)
    def _():
        rows = [pl.ds((me ^ k) * stretch, stretch) for k in range(4)]
        copy_all(
            [(ref, held.at[rows[k]]) for k, ref in enumerate((r0, r1, r2, r3))]
            + [(ref, up.at[rows[k]]) for k, ref in enumerate((u0, u1, u2, u3))],
            sems,
        )
        query_sum[...] = jnp.zeros_like(query_sum)

        def prepare(at, _):
            rows = pl.ds(at * BLOCK, BLOCK)
            query, upstream = held[rows, 0:128], up[rows, :]
            turned = (upstream.astype(F32) * raw_ref[rows, :]).T
            for head in range(2):
                query_at[head, rows, :] = own_lanes(query, head)
                up_at[head, rows, :] = own_lanes(upstream, head)
                total = jnp.sum(turned[head * 64 : head * 64 + 64], axis=0, keepdims=True)
                delta[at, head * 8 : head * 8 + 8, :] = jnp.broadcast_to(total, (8, BLOCK))
            return 0

        lax.fori_loop(0, count, prepare, 0)

    here_rows = pl.ds(here * BLOCK, BLOCK)
    key, value = held[here_rows, 128:256], held[here_rows, 256:384]
    keys = [own_lanes(key, head) for head in range(2)]
    values = [own_lanes(value, head) for head in range(2)]

    def step(at, diagonal):
        rows = pl.ds(at * BLOCK, BLOCK)
        query, upstream = held[rows, 0:128], up[rows, :]
        key_total = value_total = query_total = None
        for head in range(2):
            scores = against(keys[head], query)
            lse = lse_ref[at, head * 8 : head * 8 + 1, :]
            chance = jnp.exp(scores - lse)
            if diagonal:
                down = lax.broadcasted_iota(jnp.int32, (BLOCK, BLOCK), 0)
                along = lax.broadcasted_iota(jnp.int32, (BLOCK, BLOCK), 1)
                chance = jnp.where(along >= down, chance, 0.0)
            chance_back = against(values[head], upstream)
            shift = delta[at, head * 8 : head * 8 + 1, :]
            score_back = (chance * (chance_back - shift)).astype(LOW)
            value_part = dot(chance.astype(LOW), up_at[head, rows, :])
            key_part = dot(score_back, query_at[head, rows, :])
            query_part = across(score_back, keys[head])
            if head == 0:
                value_total, key_total, query_total = value_part, key_part, query_part
            else:
                value_total += value_part
                key_total += key_part
                query_total += query_part
        query_sum[rows, :] += query_total
        return key_total, value_total

    key_sum[...], value_sum[...] = step(here, True)

    def later(at, _):
        key_total, value_total = step(at, False)
        key_sum[...] += key_total
        value_sum[...] += value_total
        return 0

    lax.fori_loop(here + 1, count, later, 0)

    def back_rope(rows, at):
        places = pl.ds(at * BLOCK, BLOCK)
        return rows * cos_ref[places, :] - half_turn(rows) * sin_ref[places, :]

    inner = pl.ds(pl.multiple_of((turn % per) * BLOCK, BLOCK), BLOCK)
    key_low, value_low = back_rope(key_sum[...], here).astype(LOW), value_sum[...].astype(LOW)
    for slot, out in enumerate((o0, o1, o2, o3)):

        @pl.when(turn // per == slot)
        def _():
            out[inner, 128:256] = key_low
            out[inner, 256:384] = value_low

    @pl.when(turn == count - 1)
    def _():
        for slot, out in enumerate((o0, o1, o2, o3)):
            for block in range(per):
                at = (slot ^ me) * per + block
                rows = query_sum[pl.ds(at * BLOCK, BLOCK), :] * HEAD_DIM**-0.5
                out[block * BLOCK : (block + 1) * BLOCK, 0:128] = back_rope(rows, at).astype(LOW)


def attend_back(ix, pieces, upstreams, raw, lse, tables, after):
    stretch = pieces[0].shape[0]
    length = 4 * stretch
    count = length // BLOCK
    whole = lambda i, m: (0, 0)
    return call(
        attend_back_kernel, "attend_back", ix, (count,), [*pieces, *upstreams, raw, lse, *tables],
        [ANY] * 8
        + [
            pl.BlockSpec((length, 128), whole),
            pl.BlockSpec((count, 16, BLOCK), lambda i, m: (0, 0, 0)),
            pl.BlockSpec((length, 128), whole),
            pl.BlockSpec((length, 128), whole),
        ],
        [shaped((stretch, 384))] * 4,
        [pl.BlockSpec((stretch, 384), whole)] * 4,
        [
            pltpu.VMEM((length, 384), LOW),
            pltpu.VMEM((length, 128), LOW),
            pltpu.VMEM((2, length, 128), LOW),
            pltpu.VMEM((2, length, 128), LOW),
            pltpu.VMEM((count, 16, BLOCK), F32),
            pltpu.VMEM((length, 128), F32),
            pltpu.VMEM((BLOCK, 128), F32),
            pltpu.VMEM((BLOCK, 128), F32),
            pltpu.SemaphoreType.DMA((8,)),
        ],
        after=after,
    )


def store_quarters(total, t, keep_ref, send_ref):
    rows = keep_ref.shape[1]
    for quarter in range(4):
        part = total[quarter * rows : (quarter + 1) * rows].astype(LOW)
        slot = quarter ^ t

        @pl.when(slot % 2 == 0)
        def _():
            keep_ref[slot // 2] = part

        @pl.when(slot % 2 == 1)
        def _():
            send_ref[slot // 2] = part


def quarter_outs(rows, width, step):
    return (
        [shaped((2, rows // 4, width))] * 2,
        [pl.BlockSpec((2, rows // 4, step), lambda i, m: (0, 0, i))] * 2,
    )


def quarters_kernel(ix, *refs, count, turned):
    total = None
    for left, right in zip(refs[:count], refs[count : 2 * count]):
        part = (against if turned else dot)(left[...], right[...])
        total = part if total is None else total + part
    store_quarters(total, ix[T], *refs[2 * count :])


def feed_quarters(ix, lefts, rights, turned, name, after=()):
    rows, depth = lefts[0].shape
    step = 256
    if turned:
        width = rights[0].shape[0]
        spec = pl.BlockSpec((step, depth), lambda i, m: (i, m[ME] % 2))
    else:
        width = rights[0].shape[1]
        spec = pl.BlockSpec((depth, step), lambda i, m: (m[ME] % 2, i))
    count = len(lefts)
    outs, out_specs = quarter_outs(rows, width, step)
    return call(
        functools.partial(quarters_kernel, count=count, turned=turned), name, ix, (width // step,),
        [*lefts, *rights],
        [pl.BlockSpec((rows, depth), lambda i, m: (0, 0))] * count + [spec] * count,
        outs, out_specs, after=after,
    )


def join_heads_kernel(ix, a0, a1, a2, a3, w0, w1, w2, w3, keep_ref, send_ref):
    left = jnp.concatenate([a0[...], a1[...], a2[...], a3[...]], axis=1)
    right = jnp.concatenate([w0[...], w1[...], w2[...], w3[...]], axis=0)
    store_quarters(dot(left, right), ix[T], keep_ref, send_ref)


def join_heads(ix, mixed, w_out, after=()):
    rows = mixed[0].shape[0]
    width = w_out.shape[1]
    step = 512

    def heads(slot):
        return pl.BlockSpec((128, step), lambda i, m: (m[ME] ^ slot, i))

    outs, out_specs = quarter_outs(rows, width, step)
    return call(
        join_heads_kernel, "join_heads", ix, (width // step,), [*mixed] + [w_out] * 4,
        [pl.BlockSpec((rows, 128), lambda i, m: (0, 0))] * 4 + [heads(slot) for slot in range(4)],
        outs, out_specs, after=after,
    )


def project_back_kernel(ix, *refs):
    left = jnp.concatenate([ref[...] for ref in refs[:4]], axis=1)
    right = jnp.concatenate([ref[...] for ref in refs[4:16]], axis=1)
    store_quarters(against(left, right), ix[T], *refs[16:])


def project_back(ix, back, weights, after):
    rows = back[0].shape[0]
    width = weights[0].shape[0]
    step = 256

    def heads(slot):
        return pl.BlockSpec((step, 128), lambda i, m: (i, m[ME] ^ slot))

    outs, out_specs = quarter_outs(rows, width, step)
    return call(
        project_back_kernel, "project_back", ix, (width // step,),
        [*back] + [w for slot in range(4) for w in weights],
        [pl.BlockSpec((rows, 384), lambda i, m: (0, 0))] * 4
        + [heads(slot) for slot in range(4) for w in weights],
        outs, out_specs, after=after,
    )


def rows_call(kernel, name, ix, quarters, others, outs, sums=0, after=()):
    rows, width = quarters[0].shape[-2:]
    step = rows // 2

    def spec(array):
        if array.ndim == 3:
            return pl.BlockSpec((2, step, width), lambda i, m: (0, i, 0))
        if array.shape[0] == 1:
            return pl.BlockSpec((1, width), lambda i, m: (0, 0))
        if array.shape[0] == rows:
            return pl.BlockSpec((step, width), lambda i, m: (i, 0))
        return pl.BlockSpec((step, width), lambda i, m: (2 * m[T] + i, 0))

    return call(
        kernel, name, ix, (2,), [*quarters, *others], [spec(a) for a in (*quarters, *others)],
        [shaped((rows, width), dtype) for dtype in outs] + [shaped((1, width), F32)] * sums,
        [pl.BlockSpec((step, width), lambda i, m: (i, 0))] * len(outs)
        + [pl.BlockSpec((1, width), lambda i, m: (0, 0))] * sums,
        after=after,
    )


def pair_kernel(ix, keep_ref, other_ref, own_ref, send_ref):
    own_ref[...] = keep_ref[0].astype(F32) + other_ref[0].astype(F32)
    send_ref[...] = (keep_ref[1].astype(F32) + other_ref[1].astype(F32)).astype(LOW)


def pair_sums(ix, keep, other, after=()):
    return rows_call(pair_kernel, "pair_sums", ix, [keep, other], [], [F32, LOW], after=after)


def add_kernel(ix, own_ref, other_ref, out_ref):
    out_ref[...] = (own_ref[...] + other_ref[...].astype(F32)).astype(LOW)


def middle_kernel(ix, own_ref, other_ref, tok_ref, gain_ref, middle_ref, second_ref):
    middle = tok_ref[...].astype(F32) + (own_ref[...] + other_ref[...].astype(F32))
    middle_ref[...] = middle
    normed, _ = normalize(middle)
    second_ref[...] = (normed * gain_ref[...]).astype(LOW)


def add_rows(out_ref, rows):
    part = jnp.sum(rows, axis=0, keepdims=True)

    @pl.when(pl.program_id(0) == 0)
    def _():
        out_ref[...] = part

    @pl.when(pl.program_id(0) != 0)
    def _():
        out_ref[...] += part


def middle_back_kernel(ix, own_ref, y_ref, z_ref, middle_ref, cot_ref, gain_ref, grad_ref, low_ref, sum_ref):
    second_sum = own_ref[...] + y_ref[...].astype(F32) + z_ref[...].astype(F32)
    normed, inverse = normalize(middle_ref[...])
    grad = cot_ref[...].astype(F32) + norm_back(second_sum, normed, inverse, gain_ref[...])
    grad_ref[...] = grad
    low_ref[...] = grad.astype(LOW)
    add_rows(sum_ref, second_sum * normed)


def output_kernel(ix, own_ref, y_ref, z_ref, middle_ref, out_ref):
    branch = own_ref[...] + y_ref[...].astype(F32) + z_ref[...].astype(F32)
    out_ref[...] = (middle_ref[...] + branch).astype(LOW)


def input_kernel(ix, own_ref, y_ref, grad_ref, tok_ref, gain_ref, out_ref, sum_ref):
    first_sum = own_ref[...] + y_ref[...].astype(F32)
    normed, inverse = normalize(tok_ref[...].astype(F32))
    out_ref[...] = (grad_ref[...] + norm_back(first_sum, normed, inverse, gain_ref[...])).astype(LOW)
    add_rows(sum_ref, first_sum * normed)


def normalize(vector):
    inverse = lax.rsqrt(jnp.mean(vector * vector, axis=-1, keepdims=True) + EPS)
    return (vector * inverse, inverse)


def norm_back(grad_rows, normed, inverse, gain):
    scaled = grad_rows * gain
    return inverse * (scaled - normed * jnp.mean(scaled * normed, axis=-1, keepdims=True))


def tie(ix, value, after):
    return pl.pallas_call(
        lambda *refs: None,
        grid_spec=pltpu.PrefetchScalarGridSpec(
            num_scalar_prefetch=1, grid=(1,), in_specs=[ANY] * (1 + len(after)), out_specs=ANY
        ),
        out_shape=shaped(value.shape, value.dtype),
        input_output_aliases={1: 0},
        cost_estimate=pl.CostEstimate(flops=0, bytes_accessed=0, transcendentals=0),
        name="tie",
    )(ix, value, *after)


def spread(quarter, hold=lambda two: two, late=lambda quarter: quarter):
    two = hold(swap(quarter, TENSOR, 2))
    one = swap(late(quarter), TENSOR, 1)
    three = swap(two, TENSOR, 1)
    return (quarter, one, two, three)


def quarter_copies(t, pieces, held):
    rows = pieces[0].shape[0]
    return [(ref, held.at[pl.ds((t ^ k) * rows, rows)]) for k, ref in enumerate(pieces)]


def join_kernel(ix, q0, q1, q2, q3, out_ref, held, sems):
    rows = q0.shape[0]
    ins, outs = [], []
    for k, ref in enumerate((q0, q1, q2, q3)):
        ins.append(pltpu.make_async_copy(ref, held.at[k], sems.at[k]))
        at = pl.ds((ix[T] ^ k) * rows, rows)
        outs.append(pltpu.make_async_copy(held.at[k], out_ref.at[at], sems.at[4 + k]))
    for copy in ins:
        copy.start()
    for one, two in zip(ins, outs):
        one.wait()
        two.start()
    for copy in outs:
        copy.wait()


def join(ix, pieces, after=()):
    rows, width = pieces[0].shape
    return call(
        join_kernel, "join", ix, (1,), list(pieces), [ANY] * 4,
        shaped((4 * rows, width)), ANY,
        [pltpu.VMEM((4, rows, width), LOW), pltpu.SemaphoreType.DMA((8,))], after=after,
    )


def mine_kernel(ix, a_ref, b_ref, a_out, b_out, sems):
    rows = a_out.shape[0]
    at = pl.ds(ix[T] * rows, rows)
    copy_all([(a_ref.at[at], a_out), (b_ref.at[at], b_out)], sems)


def mine(ix, arrays, after):
    count, width = arrays[0].shape
    return call(
        mine_kernel, "quarter", ix, (1,), list(arrays), [ANY] * 2, [shaped((count // 4, width))] * 2,
        [pl.BlockSpec((count // 4, width), lambda i, m: (0, 0))] * 2, [pltpu.SemaphoreType.DMA((2,))], after=after,
    )


def stack_kernel(ix, a, b, c, out_ref, sems):
    copy_all([(ref, out_ref.at[k]) for k, ref in enumerate((a, b, c))], sems)


def stack(ix, arrays, after):
    shape = (3,) + arrays[0].shape
    return call(
        stack_kernel, "stack", ix, (1,), list(arrays), [ANY] * 3, shaped(shape),
        pl.BlockSpec(shape, lambda i, m: (0, 0, 0)), [pltpu.SemaphoreType.DMA((3,))], after=after,
    )


def tables_kernel(ix, freq_ref, cos_ref, sin_ref):
    rows = cos_ref.shape[0]
    lane = lax.broadcasted_iota(jnp.int32, (1, 128), 1)
    place = pl.program_id(0) * rows + lax.broadcasted_iota(jnp.int32, (rows, 128), 0)
    angle = place.astype(F32) * freq_ref[0:1, :]
    cos_ref[...] = jnp.cos(angle)
    sin_ref[...] = jnp.where((lane % HEAD_DIM) < HEAD_DIM // 2, -1.0, 1.0) * jnp.sin(angle)


def all_rope_tables(ix, count, after):
    step = 768
    return call(
        tables_kernel, "rope_tables", ix, (count // step,), [rope_freq().reshape(1, 128)],
        [pl.BlockSpec((1, 128), lambda i, m: (0, 0))], [shaped((count, 128), F32)] * 2,
        [pl.BlockSpec((step, 128), lambda i, m: (i, 0))] * 2, after=after,
    )


def hidden_back_kernel(ix, cot_ref, w_ref, out_ref):
    out_ref[...] = against(cot_ref[...], w_ref[...])


def hidden_back(ix, cotangent, w_down, after=()):
    rows, width = cotangent.shape
    units = w_down.shape[0] // 2
    step = 256
    return call(
        hidden_back_kernel, "hidden_back", ix, (units // step,), [cotangent, w_down],
        [
            pl.BlockSpec((rows, width), lambda i, m: (0, 0)),
            pl.BlockSpec((step, width), lambda i, m: ((m[ME] % 2) * (units // step) + i, 0)),
        ],
        shaped((rows, units), F32), pl.BlockSpec((rows, step), lambda i, m: (0, i)), after=after,
    )


def feed_kernel(ix, q0, q1, q2, q3, wg_ref, wu_ref, hb_ref, rows_ref, hid_ref, gb_ref, ub_ref, held, sems):
    here = pl.program_id(0)

    @pl.when(here == 0)
    def _():
        copy_all(quarter_copies(ix[T], (q0, q1, q2, q3), held), sems)
        pltpu.make_async_copy(held, rows_ref, sems.at[4]).start()

    for part in range(3):
        at = slice(part * 256, (part + 1) * 256)
        second = held[at, :]
        gate = dot(second, wg_ref[...])
        up = dot(second, wu_ref[...])
        back = hb_ref[at, :]
        sig = 0.5 + 0.5 * jnp.tanh(0.5 * gate)
        swish = gate * sig
        hid_ref[at, :] = (swish * up).astype(LOW)
        gb_ref[at, :] = (back * up * (sig + swish * (1.0 - sig))).astype(LOW)
        ub_ref[at, :] = (back * swish).astype(LOW)

    @pl.when(here == pl.num_programs(0) - 1)
    def _():
        pltpu.make_async_copy(held, rows_ref, sems.at[4]).wait()


def feed(ix, pieces, w_gate, w_up, back, after=()):
    rows, width = pieces[0].shape
    rows = 4 * rows
    units = w_gate.shape[1] // 2
    step = 256
    weight = pl.BlockSpec((width, step), lambda i, m: (0, (m[ME] % 2) * (units // step) + i))
    block = pl.BlockSpec((rows, step), lambda i, m: (0, i))
    return call(
        feed_kernel, "feed", ix, (units // step,), [*pieces, w_gate, w_up, back],
        [ANY] * 4 + [weight] * 2 + [block],
        [shaped((rows, width))] + [shaped((rows, units))] * 3, [ANY, block, block, block],
        [pltpu.VMEM((rows, width), LOW), pltpu.SemaphoreType.DMA((5,))], after=after,
    )


def branch_back_kernel(ix, q0, q1, q2, q3, w0, w1, w2, w3, rows_ref, o0, o1, o2, o3, held, sems):
    copy_all(quarter_copies(ix[T], (q0, q1, q2, q3), held), sems)
    keep = pltpu.make_async_copy(held, rows_ref, sems.at[4])
    keep.start()
    weight = jnp.concatenate([w0[...], w1[...], w2[...], w3[...]], axis=0)
    for part in range(3):
        at = slice(part * 256, (part + 1) * 256)
        flat = against(held[at, :], weight).astype(LOW)
        for slot, out in enumerate((o0, o1, o2, o3)):
            out[at, :] = flat[:, slot * 128 : (slot + 1) * 128]
    keep.wait()


def branch_back(ix, pieces, w_out, after):
    rows, width = pieces[0].shape
    rows = 4 * rows

    def heads(slot):
        return pl.BlockSpec((128, width), lambda i, m: (m[ME] ^ slot, 0))

    return call(
        branch_back_kernel, "branch_back", ix, (1,), [*pieces] + [w_out] * 4,
        [ANY] * 4 + [heads(slot) for slot in range(4)],
        [shaped((rows, width))] + [shaped((rows, 128))] * 4,
        [ANY] + [pl.BlockSpec((rows, 128), lambda i, m: (0, 0))] * 4,
        [pltpu.VMEM((rows, width), LOW), pltpu.SemaphoreType.DMA((5,))], after=after,
    )


def wgrad_kernel(ix, l0, l1, r0, r1, out_ref):
    out_ref[0] = (across(l0[...], r0[...]) + across(l1[...], r1[...])).astype(LOW)


def wide_spec(rows, share, pair):
    return pl.BlockSpec((rows, share), lambda i, m: (0, (i % 4 // 2) * 4 + (m[ME] ^ (i % 2 + 2 * pair))))


def wgrad(ix, wide, free, after=()):
    rows, units = free[0].shape
    share = 256
    return call(
        wgrad_kernel, "wgrad", ix, (4,), [*wide, *free],
        [wide_spec(rows, share, 1)] * 2 + [pl.BlockSpec((rows, units), lambda i, m: (0, 0))] * 2,
        shaped((4, share, units)), pl.BlockSpec((1, share, units), lambda i, m: (i, 0, 0)), after=after,
    )


def wgrads_kernel(ix, c0, c1, s0, s1, h0, h1, g0, g1, u0, u1, out_ref):
    turn = pl.program_id(0) // 4
    for k, (l0, l1, r0, r1) in enumerate(((c0, c1, h0, h1), (s0, s1, g0, g1), (s0, s1, u0, u1))):

        @pl.when(turn == k)
        def _():
            out_ref[0, 0, 0] = (across(l0[...], r0[...]) + across(l1[...], r1[...])).astype(LOW)


def wgrads(ix, cots, seconds, frees, after=()):
    rows, units = frees[0][0].shape
    share = 256
    return call(
        wgrads_kernel, "wgrads", ix, (12,), [*cots, *seconds, *frees[0], *frees[1], *frees[2]],
        [wide_spec(rows, share, 0)] * 4 + [pl.BlockSpec((rows, units), lambda i, m: (0, 0))] * 6,
        shaped((2, 3, 2, share, units)),
        pl.BlockSpec((1, 1, 1, share, units), lambda i, m: (i % 4 // 2, i // 4, i % 2, 0, 0)), after=after,
    )


def add_pairs_kernel(ix, a_ref, b_ref, own_ref, other_ref):
    own_ref[...] = (a_ref[0].astype(F32) + b_ref[0].astype(F32)).astype(LOW)
    other_ref[...] = (a_ref[1].astype(F32) + b_ref[1].astype(F32)).astype(LOW)


def add_pairs(ix, one, which, two, after=()):
    share, units = two.shape[1:]
    step = units // 2
    return call(
        add_pairs_kernel, "add_pairs", ix, (2,), [one, two],
        [
            pl.BlockSpec((2, share, step), lambda i, m: (which, 0, i)),
            pl.BlockSpec((2, share, step), lambda i, m: (0, 0, i)),
        ],
        [shaped((share, units))] * 2, [pl.BlockSpec((share, step), lambda i, m: (0, i))] * 2, after=after,
    )


def halves_kernel(ix, own_ref, other_ref, out_ref, *, axis):
    which = ix[ME] % 2
    for place, ref in ((which, own_ref), (1 - which, other_ref)):
        value = ref[...].astype(F32)
        if axis == 0:
            value = value.T
        size = value.shape[axis]
        at = pl.ds(pl.multiple_of(place * size, size), size)
        if axis == 0:
            out_ref[at, :] = value
        else:
            out_ref[:, at] = value


def halves(ix, own, other, axis, after=()):
    share, units = own.shape
    shape = (2 * units, share) if axis == 0 else (share, 2 * units)
    whole = lambda i, m: (0, 0)
    return call(
        functools.partial(halves_kernel, axis=axis), "halves", ix, (1,), [own, other],
        [pl.BlockSpec((share, units), whole)] * 2, shaped(shape, F32), pl.BlockSpec(shape, whole),
        after=after,
    )


def out_wgrad_kernel(ix, a0, a1, a2, a3, rows_ref, out_ref):
    for slot, ref in enumerate((a0, a1, a2, a3)):
        at = pl.ds(pl.multiple_of((slot ^ ix[ME]) * 128, 128), 128)
        out_ref[0, at, :] = across(ref[...], rows_ref[...]).astype(LOW)


def out_wgrad(ix, mixed, rows, after=()):
    count, width = rows.shape
    share = 256
    return call(
        out_wgrad_kernel, "out_wgrad", ix, (width // share,), [*mixed, rows],
        [pl.BlockSpec((count, 128), lambda i, m: (0, 0))] * 4
        + [pl.BlockSpec((count, share), lambda i, m: (0, i))],
        shaped((8, 512, share)), pl.BlockSpec((1, 512, share), lambda i, m: (i, 0, 0)), after=after,
    )


def project_wgrad_kernel(ix, first_ref, f0, f1, f2, f3, b0, b1, b2, b3, out_ref, held, total, sems):
    me, t = ix[ME], ix[T]
    turn = pl.program_id(0)
    quarter = f0.shape[1]

    def copies(slot):
        if slot == 0:
            return [pltpu.make_async_copy(first_ref, held.at[0], sems.at[0, 0])]
        return [
            pltpu.make_async_copy(
                ref.at[slot - 1], held.at[slot, pl.ds((t ^ k) * quarter, quarter)], sems.at[slot, k]
            )
            for k, ref in enumerate((f0, f1, f2, f3))
        ]

    @pl.when(turn == 0)
    def _():
        for slot in range(4):
            for copy in copies(slot):
                copy.start()

    for slot, back in enumerate((b0, b1, b2, b3)):

        @pl.when(turn == slot)
        def _():
            for copy in copies(slot):
                copy.wait()
            for block in range(8):
                at = slice(block * 256, (block + 1) * 256)
                part = across(held[slot, :, at], back[...])
                if slot == 0:
                    total[at, :] = part
                elif slot < 3:
                    total[at, :] += part
                else:
                    out_ref[block // 4, (block % 4) ^ me] = (total[at, :] + part).astype(LOW)


def project_wgrad(ix, first_in, far, back, after=()):
    rows, width = first_in.shape
    whole = lambda i, m: (0, 0)
    return call(
        project_wgrad_kernel, "project_wgrad", ix, (4,), [first_in, *far, *back],
        [ANY] * 5 + [pl.BlockSpec((rows, 384), whole)] * 4,
        shaped((2, 4, 256, 384)), pl.BlockSpec((2, 4, 256, 384), lambda i, m: (0, 0, 0, 0)),
        [
            pltpu.VMEM((4, rows, width), LOW),
            pltpu.VMEM((width, 384), F32),
            pltpu.SemaphoreType.DMA((4, 4)),
        ],
        after=after,
    )


def project_last_kernel(ix, p0, p1, p2, p3, q_ref, k_ref, v_ref):
    for slot, ref in enumerate((p0, p1, p2, p3)):
        at = pl.ds(pl.multiple_of((slot ^ ix[ME]) * 128, 128), 128)
        for place, out in enumerate((q_ref, k_ref, v_ref)):
            out[:, at] = ref[:, place * 128 : (place + 1) * 128].astype(F32)


def project_last(ix, pieces):
    share = pieces[0].shape[0]
    whole = lambda i, m: (0, 0)
    return call(
        project_last_kernel, "project_last", ix, (1,), list(pieces),
        [pl.BlockSpec((share, 384), whole)] * 4,
        [shaped((share, 512), F32)] * 3, [pl.BlockSpec((share, 512), whole)] * 3,
    )


def over_ctx(slots):
    return [slots[0]] + [swap(slots[k], CTX, k) for k in range(1, 4)]


def per_device(
    dp_size, tokens, attn_gain, w_query, w_key, w_value, w_out, mlp_gain, w_gate, w_up, w_down, cotangent
):
    rows_here, width = tokens.shape
    share = width // (4 * dp_size)
    me, t, d = lax.axis_index(CTX), lax.axis_index(TENSOR), lax.axis_index("dp")
    two_dp = dp_size == 2
    ix = jnp.stack([me, t]).astype(jnp.int32)
    order = me ^ jnp.arange(4)
    projections = (w_query, w_key, w_value)
    attn_gain, mlp_gain = attn_gain.reshape(1, -1), mlp_gain.reshape(1, -1)

    tables = rope_tables(me * rows_here + jnp.arange(rows_here, dtype=jnp.int32))
    first_in, *slots = project(ix, tokens, attn_gain, tables, projections)
    pieces = over_ctx(slots)

    back_own = hidden_back(ix, cotangent, w_down, (slots[0],))
    all_tables = all_rope_tables(ix, 4 * rows_here, (back_own,))
    cot_mine, first_mine = mine(ix, [cotangent, first_in], (*pieces[1:], all_tables[0]))
    cot_z, first_two = swap(cot_mine, CTX, 1), swap(first_mine, CTX, 2)

    *mixed_slots, raw, lse = attend(ix, pieces, (first_mine,))
    mixed = over_ctx(mixed_slots)
    cot_z, first_two = tie(ix, cot_z, (raw,)), tie(ix, first_two, (raw,))
    cot_one, cot_two = swap(cot_z, TENSOR, 1), swap(cot_z, TENSOR, 2)
    keep, send = join_heads(ix, mixed, w_out, (cot_one, cot_two, first_two))
    own, low = pair_sums(ix, keep, swap(send, TENSOR, 1))
    cot_three = swap(tie(ix, cot_two, (keep,)), TENSOR, 1)
    first_mine = tie(ix, first_mine, (keep,))
    first_one, first_three = swap(first_mine, CTX, 1), swap(first_mine, CTX, 3)
    cot_far = join(ix, (cot_z, cot_one, cot_two, cot_three), (low,))
    back_far = hidden_back(ix, cot_far, w_down, (low,))
    middle, second_mine = rows_call(
        middle_kernel, "middle", ix, [own, swap(low, TENSOR, 2)], [tokens, mlp_gain], [F32, LOW],
        after=(back_far, first_one, first_three),
    )

    second_far = swap(second_mine, CTX, 1)
    second_own, hid_own, gb_own, ub_own = feed(ix, spread(second_mine), w_gate, w_up, back_own)
    keep, send = feed_quarters(ix, [gb_own, ub_own], [w_gate, w_up], True, "feed_back")
    second_far, hid_far, gb_far, ub_far = feed(
        ix, spread(second_far, lambda two: tie(ix, two, (hid_own,))), w_gate, w_up, back_far, (keep,)
    )
    own, low = pair_sums(ix, keep, swap(send, TENSOR, 1), (hid_far,))
    own_y = swap(low, TENSOR, 2)
    keep, send = feed_quarters(ix, [gb_far, ub_far], [w_gate, w_up], True, "feed_back", (low,))

    cots, seconds = (cotangent, cot_far), (second_own, second_far)
    frees = ((hid_own, hid_far), (gb_own, gb_far), (ub_own, ub_far))

    def over_dp(part):
        return lax.psum_scatter(part, "dp", scatter_dimension=0, tiled=True) if two_dp else part

    def over_pairs(part, after):
        return swap(tie(ix, part, after), CTX, 2) if two_dp else part

    far_own, far_low = pair_sums(ix, keep, swap(send, TENSOR, 1))
    part_down = wgrad(ix, cots, frees[0], (far_low,))
    part_gate = wgrad(ix, seconds, frees[1], (part_down,))
    part_up = wgrad(ix, seconds, frees[2], (part_gate,))
    sum_down = over_dp(part_down)
    (far_low,) = rows_call(
        add_kernel, "add_low", ix, [far_own, swap(far_low, TENSOR, 2)], [], [LOW], after=(part_up,)
    )
    far_z = swap(far_low, CTX, 1)
    own_pair = wgrads(ix, cots, seconds, frees, (far_low,))
    sum_gate = over_dp(part_gate)
    middle_grad, branch_mine, mlp_gain_part = rows_call(
        middle_back_kernel, "middle_back", ix, [own, own_y, far_z, middle],
        [cotangent, mlp_gain], [F32, LOW], 1, (own_pair,),
    )
    cross_down = over_pairs(sum_down, (branch_mine,))
    down_own = feed_quarters(ix, [hid_own], [w_down], False, "feed_down", (branch_mine,))
    down_far = feed_quarters(ix, [hid_far], [w_down], False, "feed_down", (down_own[0],))
    sum_up = over_dp(part_up)
    own_sum = over_dp(own_pair)
    branch_low, *slots = branch_back(
        ix, spread(branch_mine, lambda two: tie(ix, two, (down_far[0],))), w_out, (down_far[0],)
    )
    upstreams = over_ctx(slots)
    first_far = stack(ix, [first_one, first_two, first_three], (branch_low, cross_down))
    out_part = out_wgrad(ix, mixed, branch_low, (first_far,))
    down_own_far, down_far_far = (swap(tie(ix, send, (branch_low,)), TENSOR, 1) for _, send in (down_own, down_far))
    sums = []
    token = out_part
    if two_dp:
        own_sum = own_sum.reshape(6, 256, -1)
        sums.append(add_pairs(ix, own_sum, 0, cross_down, (token,)))
        token = sums[0][0]
    cross_gate = over_pairs(sum_gate, (token, *upstreams[1:]))

    back_slots = attend_back(
        ix, pieces, upstreams, raw, lse, all_tables, (token, down_own_far, down_far_far)
    )
    back = over_ctx(back_slots)

    own, low = pair_sums(ix, down_own[0], down_own_far, (back_slots[0], cross_gate))
    own_y = swap(low, TENSOR, 2)
    far_own, far_low = pair_sums(ix, down_far[0], down_far_far, (low,))
    far_y = swap(far_low, TENSOR, 2)
    token = far_low
    if two_dp:
        sums.append(add_pairs(ix, own_sum, 1, cross_gate, (token,)))
        token = sums[1][0]
        out_part = lax.psum_scatter(out_part, ("dp", *CTX), scatter_dimension=0, tiled=True)

    cross_up = over_pairs(sum_up, (token, *back[1:]))
    keep, send = project_back(ix, back, projections, (token, out_part))
    first_own, first_low = pair_sums(ix, keep, swap(send, TENSOR, 1))
    first_spread = spread(
        first_far, lambda two: tie(ix, two, (back_slots[0],)), lambda quarter: tie(ix, quarter, (back_slots[0],))
    )
    qkv_part = project_wgrad(ix, first_in, first_spread, back_slots, (first_low,))
    input_mine, attn_gain_part = rows_call(
        input_kernel, "input_back", ix, [first_own, swap(first_low, TENSOR, 2), middle_grad],
        [tokens, attn_gain], [LOW], 1, (qkv_part,),
    )
    (far_low,) = rows_call(add_kernel, "add_low", ix, [far_own, far_y], [], [LOW], after=(input_mine,))
    far_z = swap(far_low, CTX, 1)
    if two_dp:
        sums.append(add_pairs(ix, own_sum, 2, cross_up, (far_low,)))
    (output_mine,) = rows_call(output_kernel, "output", ix, [own, own_y, far_z, middle], [], [LOW], after=(input_mine,))
    input_grad = join(ix, spread(input_mine), (far_low,))
    output = join(ix, spread(output_mine), (input_grad,))

    if two_dp:
        out_grad = out_part[0].astype(F32)
        qkv_part = over_dp(qkv_part)[0]
    else:
        def scattered(blocks, axis):
            blocks = jnp.moveaxis(blocks, 0, axis)
            shape = blocks.shape[:axis] + (width,) + blocks.shape[axis + 2 :]
            part = lax.psum_scatter(blocks.reshape(shape), "dp", scatter_dimension=axis, tiled=True)
            shape = part.shape[:axis] + (4, share) + part.shape[axis + 1 :]
            return jnp.moveaxis(part.reshape(shape), axis, 0)

        def in_order(blocks):
            return blocks[:, order].reshape(8, *blocks.shape[2:])

        for k, far in enumerate((part_down, part_gate, part_up)):
            blocks = jnp.concatenate([own_pair[:, k], far.reshape(2, 2, 256, -1)], axis=1)
            part = scattered(in_order(blocks), 0)[order].astype(F32)
            part = (part[:2] + swap(part[2:].astype(LOW), CTX, 2).astype(F32)).astype(LOW)
            sums.append((part[0], part[1]))
        qkv_part = scattered(in_order(qkv_part), 0)[order]
        out_grad = scattered(out_part, 1).astype(F32)
        out_grad = lax.psum_scatter(out_grad, CTX, scatter_dimension=0, tiled=True)[0]

    down_grad, gate_grad, up_grad = (
        halves(ix, own, swap(other, CTX, 1), axis) for (own, other), axis in zip(sums, (0, 1, 1))
    )
    qkv = project_last(ix, over_ctx(qkv_part))

    gains = jnp.concatenate([attn_gain_part, mlp_gain_part])
    gains = gains + swap(gains, TENSOR, 1)
    gains = gains + swap(gains, TENSOR, 2)
    if two_dp:
        halved = gains.reshape(2, 2, width // 2)[:, d ^ jnp.arange(2)]
        gains = halved[:, 0] + swap(halved[:, 1], "dp", 1)
    else:
        gains = lax.psum_scatter(gains, "dp", scatter_dimension=1, tiled=True)
    gains = gains.reshape(2, 4, share).transpose(1, 0, 2)[order]
    gains = sum(over_ctx(gains))

    return (
        output,
        input_grad,
        gains[0],
        qkv[0],
        qkv[1],
        qkv[2],
        out_grad,
        gains[1],
        gate_grad,
        up_grad,
        down_grad,
    )


def solution(mesh):
    dp_size = mesh.shape["dp"]
    mesh = jax.sharding.Mesh(mesh.devices.reshape(dp_size, 2, 2, 2, 2), ("dp", *CTX, *TENSOR))
    rows, tensor = ("dp", *CTX), TENSOR
    columns = P(None, tensor)
    in_specs = (
        P(rows, None), P(), columns, columns, columns, P(tensor, None),
        P(), columns, columns, P(tensor, None), P(rows, None),
    )
    out_specs = (
        P(rows, None), P(rows, None), P(rows), P(rows, tensor), P(rows, tensor), P(rows, tensor),
        P(tensor, rows), P(rows), P(rows, tensor), P(rows, tensor), P(tensor, rows),
    )
    return jax.shard_map(
        functools.partial(per_device, dp_size),
        mesh=mesh,
        in_specs=in_specs,
        out_specs=out_specs,
        check_vma=False,
    )
```

```python
import functools

import jax
import jax.numpy as jnp
from jax import lax
from jax.experimental import pallas as pl
from jax.experimental.pallas import tpu as pltpu
from jax.sharding import PartitionSpec as P

HEAD_DIM = 64
EPS = 1e-05
THETA = 130000.0
MIB = 1 << 20
MOST = 64
COSTS = {
    "project": 11, "hidden_back": 8.5, "rope_tables": 8, "attend": 28, "quarter": 3,
    "join_heads": 6.5, "sums": 3, "join": 3.5, "middle": 4, "feed": 24, "wgrad_down": 14, "wgrad_gate": 14, "wgrad_up": 14,
    "middle_back": 5, "branch_back": 7, "others": 4, "feed_down": 9, "attend_back": 40, "project_wgrad": 13,
    "out_wgrad": 8.5, "add_pairs": 4, "project_back": 11, "input_back": 5, "output": 4, "halves": 3.5,
    "project_last": 3, "add_blocks": 3, "one_block": 2,
}
SCALE = 2
LOW = jnp.bfloat16
F32 = jnp.float32
ANY = pl.BlockSpec(memory_space=pl.ANY)


CTX, TENSOR = ("hi", "lo"), ("y", "core")


def swap(value, axis, distance):
    size = 2 if axis == "dp" else 4
    return lax.ppermute(value, axis, [(i, i ^ distance) for i in range(size)])


def dot(left, right):
    return jnp.dot(left, right, preferred_element_type=F32)


def against(left, right):
    return lax.dot_general(left, right, (((1,), (1,)), ((), ())), preferred_element_type=F32)


def across(left, right):
    return lax.dot_general(left, right, (((0,), (0,)), ((), ())), preferred_element_type=F32)


def shaped(shape, dtype=LOW):
    return jax.ShapeDtypeStruct(shape, dtype)


def call(kernel, name, index, grid, inputs, in_specs, outs, out_specs, scratch=(), mib=MOST, after=()):
    count = len(inputs)

    def body(index_ref, *refs):
        kernel(index_ref, *refs[:count], *refs[count + len(after) :])

    return pl.pallas_call(
        body,
        grid_spec=pltpu.PrefetchScalarGridSpec(
            num_scalar_prefetch=1,
            grid=grid,
            in_specs=list(in_specs) + [ANY] * len(after),
            out_specs=out_specs,
            scratch_shapes=list(scratch),
        ),
        out_shape=outs,
        compiler_params=pltpu.CompilerParams(
            vmem_limit_bytes=mib * MIB, dimension_semantics=("arbitrary",) * len(grid)
        ),
        cost_estimate=pl.CostEstimate(flops=0, bytes_accessed=int(COSTS.get(name, 0) * SCALE * 3.5 * MIB), transcendentals=0),
        name=name,
    )(index, *inputs, *after)


ME, T, DP = 0, 1, 2


def copy_all(pairs, sems):
    copies = [pltpu.make_async_copy(a, b, sems.at[k]) for k, (a, b) in enumerate(pairs)]
    for copy in copies:
        copy.start()
    for copy in copies:
        copy.wait()


def half_turn(rows):
    lane = lax.broadcasted_iota(jnp.int32, (1, 128), 1)
    first = (lane % HEAD_DIM) < HEAD_DIM // 2
    return jnp.where(first, pltpu.roll(rows, 96, 1), pltpu.roll(rows, 32, 1))


def rope_freq():
    half = HEAD_DIM // 2
    freq = jnp.power(THETA, -jnp.arange(half, dtype=F32) * (2.0 / HEAD_DIM))
    return jnp.concatenate([freq] * 4)


def rope_tables(positions):
    sign = jnp.where((jnp.arange(128) % HEAD_DIM) < HEAD_DIM // 2, -1.0, 1.0)
    angle = positions.astype(F32)[:, None] * rope_freq()[None, :]
    return jnp.cos(angle), jnp.sin(angle) * sign


def project_kernel(ix, tok_ref, gain_ref, cos_ref, sin_ref, wq_ref, wk_ref, wv_ref, first_ref, o0, o1, o2, o3, held):
    me = ix[ME]
    rows = tok_ref[...].astype(F32)
    inverse = lax.rsqrt(jnp.mean(rows * rows, axis=-1, keepdims=True) + EPS)
    first = (rows * inverse * gain_ref[...]).astype(LOW)
    first_ref[...] = first
    cosine, sine = cos_ref[...], sin_ref[...]
    for place, weight in enumerate((wq_ref, wk_ref, wv_ref)):
        flat = dot(first, weight[...])
        for group in range(4):
            part = flat[:, group * 128 : (group + 1) * 128]
            if place < 2:
                part = part * cosine + half_turn(part) * sine
            if place == 0:
                part = part * HEAD_DIM**-0.5
            held[group, :, place * 128 : (place + 1) * 128] = part.astype(LOW)
    for slot, out in enumerate((o0, o1, o2, o3)):
        out[...] = held[slot ^ me]


def project(ix, tokens, gain, tables, weights):
    rows, width = tokens.shape
    local = weights[0].shape[1]
    step = 256
    whole = lambda i, m: (0, 0)
    along = lambda i, m: (i, 0)
    return call(
        project_kernel, "project", ix, (rows // step,),
        [tokens, gain, *tables, *weights],
        [pl.BlockSpec((step, width), along), pl.BlockSpec((1, width), whole)]
        + [pl.BlockSpec((step, 128), along)] * 2 + [pl.BlockSpec((width, local), whole)] * 3,
        [shaped((rows, width))] + [shaped((rows, 384))] * 4,
        [pl.BlockSpec((step, width), along)] + [pl.BlockSpec((step, 384), along)] * 4,
        [pltpu.VMEM((4, step, 384), LOW)],
    )


def own_lanes(rows, head):
    lane = lax.broadcasted_iota(jnp.int32, (1, 128), 1)
    inside = (lane < HEAD_DIM) if head == 0 else (lane >= HEAD_DIM)
    return jnp.where(inside, rows, jnp.zeros_like(rows))


def attend_kernel(ix, r0, r1, r2, r3, o0, o1, o2, o3, raw_ref, lse_ref, held, sems):
    me = ix[ME]
    turn = pl.program_id(0)
    here = turn ^ me
    stretch = r0.shape[0]
    half = stretch // 2
    lane = lax.broadcasted_iota(jnp.int32, (1, 128), 1)

    @pl.when(turn == 0)
    def _():
        copy_all(
            [(ref, held.at[pl.ds((me ^ k) * stretch, stretch)]) for k, ref in enumerate((r0, r1, r2, r3))], sems
        )

    query = held[pl.ds(here * stretch, stretch), 0:128]
    queries = [own_lanes(query, head) for head in range(2)]

    def step(queries, rows, carry, offset):
        keys, values = held[rows, 128:256], held[rows, 256:384]
        out = []
        for head in range(2):
            peak, mass, total = carry[3 * head : 3 * head + 3]
            scores = against(queries[head], keys)
            if offset is not None:
                down = lax.broadcasted_iota(jnp.int32, scores.shape, 0) + offset
                along = lax.broadcasted_iota(jnp.int32, scores.shape, 1)
                scores = jnp.where(down >= along, scores, -1e30)
            top = jnp.maximum(peak, jnp.max(scores, axis=-1, keepdims=True))
            weights = jnp.exp(scores - top)
            fade = jnp.exp(peak - top)
            mass = mass * fade + jnp.sum(weights, axis=-1, keepdims=True)
            out += [top, mass, total * fade + dot(weights.astype(LOW), values)]
        return tuple(out)

    start = (
        jnp.full((stretch, 1), -1e30, F32),
        jnp.zeros((stretch, 1), F32),
        jnp.zeros((stretch, 128), F32),
    ) * 2
    carry = lax.fori_loop(0, here, lambda at, c: step(queries, pl.ds(at * stretch, stretch), c, None), start)
    for part in range(2):
        at = slice(part * half, (part + 1) * half)
        rows = pl.ds(here * stretch, (part + 1) * half)
        done = step([query[at] for query in queries], rows, [c[at] for c in carry], part * half)
        peak0, mass0, total0, peak1, mass1, total1 = done
        mixed = jnp.where(lane < HEAD_DIM, total0 / mass0, total1 / mass1)
        raw_ref[at, :] = mixed
        for slot, out in enumerate((o0, o1, o2, o3)):

            @pl.when(turn == slot)
            def _():
                out[at, :] = mixed.astype(LOW)

        turned = jnp.where(lane < HEAD_DIM, peak0 + jnp.log(mass0), peak1 + jnp.log(mass1)).T
        lse_ref[0, 0:8, at] = turned[0:8]
        lse_ref[0, 8:16, at] = turned[64:72]


def attend(ix, pieces, after):
    stretch = pieces[0].shape[0]
    length = 4 * stretch
    return call(
        attend_kernel, "attend", ix, (4,), list(pieces), [ANY] * 4,
        [shaped((stretch, 128))] * 4 + [shaped((length, 128), F32), shaped((4, 16, stretch), F32)],
        [pl.BlockSpec((stretch, 128), lambda i, m: (0, 0))] * 4
        + [
            pl.BlockSpec((stretch, 128), lambda i, m: (i ^ m[ME], 0)),
            pl.BlockSpec((1, 16, stretch), lambda i, m: (i ^ m[ME], 0, 0)),
        ],
        [pltpu.VMEM((length, 384), LOW), pltpu.SemaphoreType.DMA((4,))], after=after,
    )


def attend_back_kernel(
    ix, p0, p1, p2, p3, u0, u1, u2, u3, raw_ref, lse_ref, cos_ref, sin_ref, o0, o1, o2, o3,
    held, up, query_at, up_at, delta, query_sum, key_sum, value_sum, sems,
):
    me = ix[ME]
    turn = pl.program_id(0)
    count = pl.num_programs(0)
    stretch = p0.shape[0]
    half = stretch // 2
    here = turn ^ me

    @pl.when(turn == 0)
    def _():
        rows = [pl.ds((me ^ k) * stretch, stretch) for k in range(4)]
        copy_all(
            [(ref, held.at[rows[k]]) for k, ref in enumerate((p0, p1, p2, p3))]
            + [(ref, up.at[rows[k]]) for k, ref in enumerate((u0, u1, u2, u3))],
            sems,
        )
        query_sum[...] = jnp.zeros_like(query_sum)

        def prepare(at, _):
            rows = pl.ds(at * stretch, stretch)
            query, upstream = held[rows, 0:128], up[rows, :]
            turned = (upstream.astype(F32) * raw_ref[rows, :]).T
            for head in range(2):
                query_at[head, rows, :] = own_lanes(query, head)
                up_at[head, rows, :] = own_lanes(upstream, head)
                total = jnp.sum(turned[head * 64 : head * 64 + 64], axis=0, keepdims=True)
                delta[at, head * 8 : head * 8 + 8, :] = jnp.broadcast_to(total, (8, stretch))
            return 0

        lax.fori_loop(0, count, prepare, 0)

    here_rows = pl.ds(here * stretch, stretch)
    key, value = held[here_rows, 128:256], held[here_rows, 256:384]
    keys = [own_lanes(key, head) for head in range(2)]
    values = [own_lanes(value, head) for head in range(2)]

    def step(at, queries, kept, diagonal):
        size = queries.stop - queries.start
        rows = pl.ds(at * stretch + queries.start, size)
        query, upstream = held[rows, 0:128], up[rows, :]
        key_total = value_total = query_total = None
        for head in range(2):
            scores = against(keys[head][:kept], query)
            lse = lse_ref[at, head * 8 : head * 8 + 1, queries]
            chance = jnp.exp(scores - lse)
            if diagonal:
                down = lax.broadcasted_iota(jnp.int32, scores.shape, 0)
                along = lax.broadcasted_iota(jnp.int32, scores.shape, 1) + queries.start
                chance = jnp.where(along >= down, chance, 0.0)
            chance_back = against(values[head][:kept], upstream)
            shift = delta[at, head * 8 : head * 8 + 1, queries]
            score_back = (chance * (chance_back - shift)).astype(LOW)
            value_part = dot(chance.astype(LOW), up_at[head, rows, :])
            key_part = dot(score_back, query_at[head, rows, :])
            query_part = across(score_back, keys[head][:kept])
            if head == 0:
                value_total, key_total, query_total = value_part, key_part, query_part
            else:
                value_total += value_part
                key_total += key_part
                query_total += query_part
        query_sum[rows, :] += query_total
        return key_total, value_total

    key_sum[...], value_sum[...] = step(here, slice(half, stretch), stretch, True)
    key_total, value_total = step(here, slice(0, half), half, True)
    key_sum[:half] += key_total
    value_sum[:half] += value_total

    def later(at, _):
        key_total, value_total = step(at, slice(0, stretch), stretch, False)
        key_sum[...] += key_total
        value_sum[...] += value_total
        return 0

    lax.fori_loop(here + 1, count, later, 0)

    def back_rope(rows, at):
        places = pl.ds(at * stretch, stretch)
        return rows * cos_ref[places, :] - half_turn(rows) * sin_ref[places, :]

    key_low, value_low = back_rope(key_sum[...], here).astype(LOW), value_sum[...].astype(LOW)
    for slot, out in enumerate((o0, o1, o2, o3)):

        @pl.when(turn == slot)
        def _():
            out[:, 128:256] = key_low
            out[:, 256:384] = value_low

    @pl.when(turn == count - 1)
    def _():
        for slot, out in enumerate((o0, o1, o2, o3)):
            rows = query_sum[pl.ds((slot ^ me) * stretch, stretch), :] * HEAD_DIM**-0.5
            out[:, 0:128] = back_rope(rows, slot ^ me).astype(LOW)


def attend_back(ix, pieces, upstreams, raw, lse, tables, after):
    stretch = pieces[0].shape[0]
    length = 4 * stretch
    whole = lambda i, m: (0, 0)
    return call(
        attend_back_kernel, "attend_back", ix, (4,), [*pieces, *upstreams, raw, lse, *tables],
        [ANY] * 8
        + [pl.BlockSpec((length, 128), whole), pl.BlockSpec((4, 16, stretch), lambda i, m: (0, 0, 0))]
        + [pl.BlockSpec((length, 128), whole)] * 2,
        [shaped((stretch, 384))] * 4,
        [pl.BlockSpec((stretch, 384), whole)] * 4,
        [
            pltpu.VMEM((length, 384), LOW),
            pltpu.VMEM((length, 128), LOW),
            pltpu.VMEM((2, length, 128), LOW),
            pltpu.VMEM((2, length, 128), LOW),
            pltpu.VMEM((4, 16, stretch), F32),
            pltpu.VMEM((length, 128), F32),
            pltpu.VMEM((stretch, 128), F32),
            pltpu.VMEM((stretch, 128), F32),
            pltpu.SemaphoreType.DMA((8,)),
        ],
        after=after,
    )


def quarter_outs(rows, width, step):
    return (
        [shaped((2, rows // 4, width))] * 2,
        [pl.BlockSpec((2, rows // 4, step), lambda i, m: (0, 0, i))] * 2,
    )


def in_quarters(t, ref, held, columns=slice(None)):
    rows = ref.shape[0] // 4
    return [
        (ref.at[pl.ds((t ^ k) * rows, rows)], held.at[pl.ds(place * rows, rows), columns])
        for place, k in enumerate((0, 2, 1, 3))
    ]


def store_quarters(total, keep_ref, send_ref):
    rows = keep_ref.shape[1]
    for k in range(2):
        keep_ref[k] = total[k * rows : (k + 1) * rows].astype(LOW)
        send_ref[k] = total[(2 + k) * rows : (3 + k) * rows].astype(LOW)


def feed_down_kernel(ix, left_ref, right_ref, keep_ref, send_ref, held, sems):
    @pl.when(pl.program_id(0) == 0)
    def _():
        copy_all(in_quarters(ix[T], left_ref, held), sems)

    store_quarters(dot(held[...], right_ref[...]), keep_ref, send_ref)


def feed_down(ix, hidden, w_down, after=()):
    rows, units = hidden.shape
    width = w_down.shape[1]
    step = 512
    outs, out_specs = quarter_outs(rows, width, step)
    return call(
        feed_down_kernel, "feed_down", ix, (width // step,), [hidden, w_down],
        [ANY, pl.BlockSpec((units, step), lambda i, m: (m[ME] % 2, i))], outs, out_specs,
        [pltpu.VMEM((rows, units), LOW), pltpu.SemaphoreType.DMA((4,))], after=after,
    )


def join_heads_kernel(ix, a0, a1, a2, a3, w0, w1, w2, w3, keep_ref, send_ref, held, sems):
    @pl.when(pl.program_id(0) == 0)
    def _():
        copy_all(
            [
                pair
                for k, ref in enumerate((a0, a1, a2, a3))
                for pair in in_quarters(ix[T], ref, held, slice(k * 128, (k + 1) * 128))
            ],
            sems,
        )

    right = jnp.concatenate([w0[...], w1[...], w2[...], w3[...]], axis=0)
    store_quarters(dot(held[...], right), keep_ref, send_ref)


def join_heads(ix, mixed, w_out, after=()):
    rows = mixed[0].shape[0]
    width = w_out.shape[1]
    step = 1024

    def heads(slot):
        return pl.BlockSpec((128, step), lambda i, m: (m[ME] ^ slot, i))

    outs, out_specs = quarter_outs(rows, width, step)
    return call(
        join_heads_kernel, "join_heads", ix, (width // step,), [*mixed] + [w_out] * 4,
        [ANY] * 4 + [heads(slot) for slot in range(4)], outs, out_specs,
        [pltpu.VMEM((rows, 512), LOW), pltpu.SemaphoreType.DMA((16,))], after=after,
    )


def project_back_kernel(ix, *refs):
    keep_ref, send_ref, held, sems = refs[16:]

    @pl.when(pl.program_id(0) == 0)
    def _():
        copy_all(
            [
                pair
                for k, ref in enumerate(refs[:4])
                for pair in in_quarters(ix[T], ref, held, slice(k * 384, (k + 1) * 384))
            ],
            sems,
        )

    right = jnp.concatenate([ref[...] for ref in refs[4:16]], axis=1)
    store_quarters(against(held[...], right), keep_ref, send_ref)


def project_back(ix, back, weights, after):
    rows = back[0].shape[0]
    width = weights[0].shape[0]
    step = 512

    def heads(slot):
        return pl.BlockSpec((step, 128), lambda i, m: (i, m[ME] ^ slot))

    outs, out_specs = quarter_outs(rows, width, step)
    return call(
        project_back_kernel, "project_back", ix, (width // step,),
        [*back] + [w for slot in range(4) for w in weights],
        [ANY] * 4 + [heads(slot) for slot in range(4) for w in weights], outs, out_specs,
        [pltpu.VMEM((rows, 1536), LOW), pltpu.SemaphoreType.DMA((16,))], after=after,
    )


def rows_call(kernel, name, ix, quarters, others, outs, sums=0, after=()):
    arrays = [a if isinstance(a, tuple) else (a, None) for a in (*quarters, *others)]
    rows, width = arrays[0][0].shape[-2:]
    step = rows // 2

    def spec(array, which):
        if which is not None:
            return pl.BlockSpec((None, step, width), lambda i, m: (which, i, 0))
        if array.shape[0] == 1:
            return pl.BlockSpec((1, width), lambda i, m: (0, 0))
        if array.shape[0] == rows:
            return pl.BlockSpec((step, width), lambda i, m: (i, 0))
        return pl.BlockSpec((step, width), lambda i, m: (2 * m[T] + i, 0))

    return call(
        kernel, name, ix, (2,), [array for array, _ in arrays], [spec(*pair) for pair in arrays],
        [shaped((rows, width), dtype) for dtype in outs] + [shaped((1, width), F32)] * sums,
        [pl.BlockSpec((step, width), lambda i, m: (i, 0))] * len(outs)
        + [pl.BlockSpec((1, width), lambda i, m: (0, 0))] * sums,
        after=after,
    )


def wide_sum(*refs):
    return sum(ref[...].astype(F32) for ref in refs)


def sum_kernel(ix, *refs):
    refs[-1][...] = wide_sum(*refs[:-1]).astype(LOW)


def sums_to_send(ix, arrays, after=()):
    return rows_call(sum_kernel, "sums", ix, arrays, [], [LOW], after=after)[0]


def middle_kernel(ix, one, two, y_ref, tok_ref, gain_ref, middle_ref, second_ref):
    middle = tok_ref[...].astype(F32) + wide_sum(one, two, y_ref)
    middle_ref[...] = middle
    normed, _ = normalize(middle)
    second_ref[...] = (normed * gain_ref[...]).astype(LOW)


def add_rows(out_ref, rows):
    part = jnp.sum(rows, axis=0, keepdims=True)

    @pl.when(pl.program_id(0) == 0)
    def _():
        out_ref[...] = part

    @pl.when(pl.program_id(0) != 0)
    def _():
        out_ref[...] += part


def middle_back_kernel(ix, one, two, y_ref, z_ref, middle_ref, cot_ref, gain_ref, grad_ref, low_ref, sum_ref):
    second_sum = wide_sum(one, two, y_ref, z_ref)
    normed, inverse = normalize(middle_ref[...])
    grad = cot_ref[...].astype(F32) + norm_back(second_sum, normed, inverse, gain_ref[...])
    grad_ref[...] = grad
    low_ref[...] = grad.astype(LOW)
    add_rows(sum_ref, second_sum * normed)


def output_kernel(ix, one, two, y_ref, z_ref, middle_ref, out_ref):
    out_ref[...] = (middle_ref[...] + wide_sum(one, two, y_ref, z_ref)).astype(LOW)


def input_kernel(ix, one, two, y_ref, grad_ref, tok_ref, gain_ref, mlp_ref, out_ref, total):
    here, last = pl.program_id(0), pl.num_programs(0) - 1

    @pl.when(here < last)
    def _():
        first_sum = wide_sum(one, two, y_ref)
        normed, inverse = normalize(tok_ref[...].astype(F32))
        out_ref[...] = (grad_ref[...] + norm_back(first_sum, normed, inverse, gain_ref[...])).astype(LOW)
        add_rows(total, first_sum * normed)

    @pl.when(here == last)
    def _():
        sums = jnp.concatenate([total[...], mlp_ref[...], jnp.zeros((14, total.shape[1]), F32)], axis=0)
        out_ref[0:16, :] = sums.astype(LOW)


def input_back(ix, keep, core, y, grad, tokens, gain, mlp_sum, after):
    rows, width = grad.shape
    step = rows // 2
    at = lambda i: jnp.minimum(i, 1)
    block = pl.BlockSpec((None, step, width), lambda i, m: (0, at(i), 0))
    row = pl.BlockSpec((step, width), lambda i, m: (at(i), 0))
    single = pl.BlockSpec((1, width), lambda i, m: (0, 0))
    return call(
        input_kernel, "input_back", ix, (3,), [keep, core, y, grad, tokens, gain, mlp_sum],
        [block, block, row, row, pl.BlockSpec((step, width), lambda i, m: (2 * m[T] + at(i), 0)), single, single],
        shaped((rows + 16, width)), pl.BlockSpec((step, width), lambda i, m: (i, 0)),
        [pltpu.VMEM((1, width), F32)], after=after,
    )


def join_input_kernel(ix, q0, q1, q2, q3, out_ref, sum_ref, held, sems):
    rows = out_ref.shape[0] // 4
    ins, outs = [], []
    for k, ref in enumerate((q0, q1, q2, q3)):
        ins.append(pltpu.make_async_copy(ref, held.at[k], sems.at[k]))
        at = pl.ds((ix[T] ^ k) * rows, rows)
        outs.append(pltpu.make_async_copy(held.at[k, pl.ds(0, rows)], out_ref.at[at], sems.at[4 + k]))
    for copy in ins:
        copy.start()
    total = jnp.zeros(sum_ref.shape, F32)
    for k, (one, two) in enumerate(zip(ins, outs)):
        one.wait()
        two.start()
        total = total + held[k, rows : rows + 16, :].astype(F32)
    sum_ref[...] = total
    for copy in outs:
        copy.wait()


def join_input(ix, pieces, after):
    rows, width = pieces[0].shape
    rows -= 16
    return call(
        join_input_kernel, "join", ix, (1,), list(pieces), [ANY] * 4,
        [shaped((4 * rows, width)), shaped((16, width), F32)],
        [ANY, pl.BlockSpec((16, width), lambda i, m: (0, 0))],
        [pltpu.VMEM((4, rows + 16, width), LOW), pltpu.SemaphoreType.DMA((8,))], after=after,
    )


def normalize(vector):
    inverse = lax.rsqrt(jnp.mean(vector * vector, axis=-1, keepdims=True) + EPS)
    return (vector * inverse, inverse)


def norm_back(grad_rows, normed, inverse, gain):
    scaled = grad_rows * gain
    return inverse * (scaled - normed * jnp.mean(scaled * normed, axis=-1, keepdims=True))


def tie(ix, value, after):
    return pl.pallas_call(
        lambda *refs: None,
        grid_spec=pltpu.PrefetchScalarGridSpec(
            num_scalar_prefetch=1, grid=(1,), in_specs=[ANY] * (1 + len(after)), out_specs=ANY
        ),
        out_shape=shaped(value.shape, value.dtype),
        input_output_aliases={1: 0},
        cost_estimate=pl.CostEstimate(flops=0, bytes_accessed=0, transcendentals=0),
        name="tie",
    )(ix, value, *after)


def spread(quarter, hold=lambda two: two, late=lambda quarter: quarter):
    two = hold(swap(quarter, TENSOR, 2))
    one = swap(late(quarter), TENSOR, 1)
    three = swap(two, TENSOR, 1)
    return (quarter, one, two, three)


def quarter_copies(t, pieces, held):
    rows = pieces[0].shape[0]
    return [(ref, held.at[pl.ds((t ^ k) * rows, rows)]) for k, ref in enumerate(pieces)]


def join_kernel(ix, q0, q1, q2, q3, out_ref, held, sems):
    rows = q0.shape[0]
    ins, outs = [], []
    for k, ref in enumerate((q0, q1, q2, q3)):
        ins.append(pltpu.make_async_copy(ref, held.at[k], sems.at[k]))
        at = pl.ds((ix[T] ^ k) * rows, rows)
        outs.append(pltpu.make_async_copy(held.at[k], out_ref.at[at], sems.at[4 + k]))
    for copy in ins:
        copy.start()
    for one, two in zip(ins, outs):
        one.wait()
        two.start()
    for copy in outs:
        copy.wait()


def join(ix, pieces, after=()):
    rows, width = pieces[0].shape
    return call(
        join_kernel, "join", ix, (1,), list(pieces), [ANY] * 4,
        shaped((4 * rows, width)), ANY,
        [pltpu.VMEM((4, rows, width), LOW), pltpu.SemaphoreType.DMA((8,))], after=after,
    )


def mine_kernel(ix, *refs):
    count = len(refs) // 2
    rows = refs[count].shape[0]
    at = pl.ds(ix[T] * rows, rows)
    copy_all([(refs[k].at[at], refs[count + k]) for k in range(count)], refs[-1])


def mine(ix, arrays, after):
    count, width = arrays[0].shape
    size = len(arrays)
    return call(
        mine_kernel, "quarter", ix, (1,), list(arrays), [ANY] * size, [shaped((count // 4, width))] * size,
        [pl.BlockSpec((count // 4, width), lambda i, m: (0, 0))] * size, [pltpu.SemaphoreType.DMA((size,))],
        after=after,
    )


def others_kernel(ix, rows_ref, out_ref, sems):
    copy_all([(rows_ref.at[ix[ME] ^ k], out_ref.at[k - 1]) for k in range(1, 4)], sems)


def others(ix, rows, after):
    shape = (3,) + rows.shape[1:]
    return call(
        others_kernel, "others", ix, (1,), [rows], [ANY], shaped(shape),
        pl.BlockSpec(shape, lambda i, m: (0, 0, 0)), [pltpu.SemaphoreType.DMA((3,))], after=after,
    )


def tables_kernel(ix, freq_ref, cos_ref, sin_ref):
    rows = cos_ref.shape[0]
    lane = lax.broadcasted_iota(jnp.int32, (1, 128), 1)
    place = pl.program_id(0) * rows + lax.broadcasted_iota(jnp.int32, (rows, 128), 0)
    angle = place.astype(F32) * freq_ref[0:1, :]
    cos_ref[...] = jnp.cos(angle)
    sin_ref[...] = jnp.where((lane % HEAD_DIM) < HEAD_DIM // 2, -1.0, 1.0) * jnp.sin(angle)


def all_rope_tables(ix, count, after):
    step = 768
    return call(
        tables_kernel, "rope_tables", ix, (count // step,), [rope_freq().reshape(1, 128)],
        [pl.BlockSpec((1, 128), lambda i, m: (0, 0))], [shaped((count, 128), F32)] * 2,
        [pl.BlockSpec((step, 128), lambda i, m: (i, 0))] * 2, after=after,
    )


def hidden_back_kernel(ix, cot_ref, w_ref, out_ref):
    out_ref[...] = against(cot_ref[...], w_ref[...])


def far_rows(array, rows):
    return (lambda m: (m[ME] % 2) ^ 1) if array.shape[0] > rows else (lambda m: 0)


def hidden_back(ix, cotangent, rows, w_down, after=()):
    width = cotangent.shape[1]
    units = w_down.shape[0] // 2
    step = 512
    block = far_rows(cotangent, rows)
    return call(
        hidden_back_kernel, "hidden_back", ix, (units // step,), [cotangent, w_down],
        [
            pl.BlockSpec((rows, width), lambda i, m: (block(m), 0)),
            pl.BlockSpec((step, width), lambda i, m: ((m[ME] % 2) * (units // step) + i, 0)),
        ],
        shaped((rows, units), F32), pl.BlockSpec((rows, step), lambda i, m: (0, i)), after=after,
    )


def feed_kernel(ix, *refs, count):
    pieces = refs[:count]
    wg_ref, wu_ref, hb_ref, wg_rows, wu_rows, rows_ref, hid_ref, gb_ref, ub_ref, keep_ref, send_ref = refs[count:-4]
    held, gate_back, up_back, sems = refs[-4:]
    t = ix[T]
    here = pl.program_id(0)
    rows, units = gate_back.shape
    step = wg_ref.shape[1]
    forward = units // step
    quarter = rows // 4

    @pl.when(here == 0)
    def _():
        if count == 1:
            copy_all([(pieces[0].at[pl.ds((1 - ix[ME] % 2) * rows, rows)], held)], sems)
        else:
            copy_all(quarter_copies(t, pieces, held), sems)
        pltpu.make_async_copy(held, rows_ref, sems.at[4]).start()

    @pl.when(here < forward)
    def _():
        second = held[...]
        gate = dot(second, wg_ref[...])
        up = dot(second, wu_ref[...])
        back = hb_ref[...]
        sig = 0.5 + 0.5 * jnp.tanh(0.5 * gate)
        swish = gate * sig
        hid_ref[...] = (swish * up).astype(LOW)
        gate_low = (back * up * (sig + swish * (1.0 - sig))).astype(LOW)
        up_low = (back * swish).astype(LOW)
        gb_ref[...] = gate_low
        ub_ref[...] = up_low
        columns = pl.ds(pl.multiple_of(here * step, step), step)
        for k in range(4):
            slot = k ^ t
            place = pl.ds(pl.multiple_of(((slot & 1) * 2 + (slot >> 1)) * quarter, quarter), quarter)
            gate_back[place, columns] = gate_low[k * quarter : (k + 1) * quarter]
            up_back[place, columns] = up_low[k * quarter : (k + 1) * quarter]

    @pl.when(here >= forward)
    def _():
        total = against(gate_back[...], wg_rows[...]) + against(up_back[...], wu_rows[...])
        store_quarters(total, keep_ref, send_ref)

    @pl.when(here == pl.num_programs(0) - 1)
    def _():
        pltpu.make_async_copy(held, rows_ref, sems.at[4]).wait()


def feed(ix, pieces, w_gate, w_up, back, after=()):
    rows, width = back.shape[0], pieces[0].shape[1]
    units = w_gate.shape[1] // 2
    step, wide = 256, 512
    forward = units // step
    first = lambda i: jnp.minimum(i, forward - 1)
    then = lambda i: jnp.maximum(i - forward, 0)
    weight = pl.BlockSpec((width, step), lambda i, m: (0, (m[ME] % 2) * forward + first(i)))
    weight_rows = pl.BlockSpec((wide, units), lambda i, m: (then(i), m[ME] % 2))
    block = pl.BlockSpec((rows, step), lambda i, m: (0, first(i)))
    return call(
        functools.partial(feed_kernel, count=len(pieces)), "feed", ix, (forward + width // wide,),
        [*pieces, w_gate, w_up, back, w_gate, w_up],
        [ANY] * len(pieces) + [weight] * 2 + [block] + [weight_rows] * 2,
        [shaped((rows, width))] + [shaped((rows, units))] * 3 + [shaped((2, rows // 4, width))] * 2,
        [ANY, block, block, block] + [pl.BlockSpec((2, rows // 4, wide), lambda i, m: (0, 0, then(i)))] * 2,
        [
            pltpu.VMEM((rows, width), LOW),
            pltpu.VMEM((rows, units), LOW),
            pltpu.VMEM((rows, units), LOW),
            pltpu.SemaphoreType.DMA((5,)),
        ],
        after=after,
    )


def branch_back_kernel(ix, q0, q1, q2, q3, w0, w1, w2, w3, rows_ref, o0, o1, o2, o3, held, sems):
    copy_all(quarter_copies(ix[T], (q0, q1, q2, q3), held), sems)
    keep = pltpu.make_async_copy(held, rows_ref, sems.at[4])
    keep.start()
    weight = jnp.concatenate([w0[...], w1[...], w2[...], w3[...]], axis=0)
    for part in range(3):
        at = slice(part * 256, (part + 1) * 256)
        flat = against(held[at, :], weight).astype(LOW)
        for slot, out in enumerate((o0, o1, o2, o3)):
            out[at, :] = flat[:, slot * 128 : (slot + 1) * 128]
    keep.wait()


def branch_back(ix, pieces, w_out, after):
    rows, width = pieces[0].shape
    rows = 4 * rows

    def heads(slot):
        return pl.BlockSpec((128, width), lambda i, m: (m[ME] ^ slot, 0))

    return call(
        branch_back_kernel, "branch_back", ix, (1,), [*pieces] + [w_out] * 4,
        [ANY] * 4 + [heads(slot) for slot in range(4)],
        [shaped((rows, width))] + [shaped((rows, 128))] * 4,
        [ANY] + [pl.BlockSpec((rows, 128), lambda i, m: (0, 0))] * 4,
        [pltpu.VMEM((rows, width), LOW), pltpu.SemaphoreType.DMA((5,))], after=after,
    )


def wgrad_kernel(ix, l0, l1, r0, r1, out_ref):
    out_ref[0] = (across(l0[...], r0[...]) + across(l1[...], r1[...])).astype(LOW)


def wgrad_kernel(ix, l0, l1, r0, r1, out_ref):
    out_ref[0] = (across(l0[...], r0[...]) + across(l1[...], r1[...])).astype(LOW)


def wgrad(ix, wide, free, name, after=()):
    rows, units = free[0].shape
    share = 256

    def wide_spec(array):
        block = far_rows(array, rows)
        return pl.BlockSpec((rows, share), lambda i, m: (block(m), i ^ (m[ME] % 2)))

    return call(
        wgrad_kernel, name, ix, (8,), [*wide, *free],
        [wide_spec(array) for array in wide] + [pl.BlockSpec((rows, units), lambda i, m: (0, 0))] * 2,
        shaped((8, share, units)), pl.BlockSpec((1, share, units), lambda i, m: (i, 0, 0)), after=after,
    )


def add_blocks_kernel(ix, a_ref, b_ref, *refs):
    total = (a_ref[...].astype(F32) + b_ref[...].astype(F32)).astype(LOW)
    size = refs[0].shape[0]
    for k, ref in enumerate(refs):
        ref[...] = total[k * size : (k + 1) * size]


def add_blocks(ix, one, two, parts, after=()):
    shape = (one.shape[0] // parts,) + one.shape[1:]
    whole = pl.BlockSpec(one.shape, lambda i, m: (0, 0, 0))
    return call(
        add_blocks_kernel, "add_blocks", ix, (1,), [one, two], [whole] * 2,
        [shaped(shape)] * parts, [pl.BlockSpec(shape, lambda i, m: (0, 0, 0))] * parts, after=after,
    )


def one_block_kernel(ix, in_ref, out_ref):
    out_ref[...] = in_ref[...]


def one_block(ix, blocks, which, after=()):
    shape = (1,) + blocks.shape[1:]
    return call(
        one_block_kernel, "one_block", ix, (1,), [blocks],
        [pl.BlockSpec(shape, lambda i, m: (which, 0, 0))], shaped(shape),
        pl.BlockSpec(shape, lambda i, m: (0, 0, 0)), after=after,
    )


def halves_kernel(ix, own_ref, other_ref, out_ref, *, axis):
    which = ix[ME] % 2
    for place, ref in ((which, own_ref), (1 - which, other_ref)):
        value = ref[...].astype(F32)
        if axis == 0:
            value = value.T
        size = value.shape[axis]
        at = pl.ds(pl.multiple_of(place * size, size), size)
        if axis == 0:
            out_ref[at, :] = value
        else:
            out_ref[:, at] = value


def halves(ix, blocks, other, axis, after=()):
    share, units = blocks.shape[1:]
    shape = (2 * units, share) if axis == 0 else (share, 2 * units)
    whole = lambda i, m: (0, 0)
    return call(
        functools.partial(halves_kernel, axis=axis), "halves", ix, (1,), [blocks, other],
        [pl.BlockSpec((None, share, units), lambda i, m: (0, 0, 0))] * 2,
        shaped(shape, F32), pl.BlockSpec(shape, whole), after=after,
    )


def out_wgrad_kernel(ix, a0, a1, a2, a3, rows_ref, own_ref, far_ref, held):
    for slot, ref in enumerate((a0, a1, a2, a3)):
        at = pl.ds(pl.multiple_of((slot ^ ix[ME]) * 128, 128), 128)
        held[at, :] = across(ref[...], rows_ref[...]).astype(LOW)
    for half, out in enumerate((own_ref, far_ref)):

        @pl.when(pl.program_id(0) // 4 == half)
        def _():
            out[0] = held[...]


def out_wgrad(ix, mixed, rows, after=()):
    count, width = rows.shape
    share = 256
    return call(
        out_wgrad_kernel, "out_wgrad", ix, (width // share,), [*mixed, rows],
        [pl.BlockSpec((count, 128), lambda i, m: (0, 0))] * 4
        + [pl.BlockSpec((count, share), lambda i, m: (0, i ^ (m[DP] * 4 + m[ME])))],
        [shaped((4, 512, share))] * 2,
        [
            pl.BlockSpec((1, 512, share), lambda i, m: (jnp.minimum(i, 3), 0, 0)),
            pl.BlockSpec((1, 512, share), lambda i, m: (jnp.maximum(i - 4, 0), 0, 0)),
        ],
        [pltpu.VMEM((512, share), LOW)], after=after,
    )


def project_wgrad_kernel(ix, first_ref, f0, f1, f2, f3, b0, b1, b2, b3, own_ref, far_ref, held, total, sems):
    me, t = ix[ME], ix[T]
    turn = pl.program_id(0)
    quarter = f0.shape[1]

    def copies(slot):
        if slot == 0:
            return [pltpu.make_async_copy(first_ref, held.at[0], sems.at[0, 0])]
        return [
            pltpu.make_async_copy(
                ref.at[slot - 1], held.at[slot, pl.ds((t ^ k) * quarter, quarter)], sems.at[slot, k]
            )
            for k, ref in enumerate((f0, f1, f2, f3))
        ]

    @pl.when(turn == 0)
    def _():
        for slot in range(4):
            for copy in copies(slot):
                copy.start()

    for slot, back in enumerate((b0, b1, b2, b3)):

        @pl.when(turn == slot)
        def _():
            for copy in copies(slot):
                copy.wait()
            for block in range(8):
                at = slice(block * 256, (block + 1) * 256)
                part = across(held[slot, :, at], back[...])
                if slot == 0:
                    total[at, :] = part
                elif slot < 3:
                    total[at, :] += part
                else:
                    done = (total[at, :] + part).astype(LOW)

                    @pl.when(ix[DP] == block // 4)
                    def _():
                        own_ref[(block % 4) ^ me] = done

                    @pl.when(ix[DP] != block // 4)
                    def _():
                        far_ref[(block % 4) ^ me] = done


def project_wgrad(ix, first_in, far, back, after=()):
    rows, width = first_in.shape
    whole = lambda i, m: (0, 0)
    return call(
        project_wgrad_kernel, "project_wgrad", ix, (4,), [first_in, *far, *back],
        [ANY] * 5 + [pl.BlockSpec((rows, 384), whole)] * 4,
        [shaped((4, 256, 384))] * 2, [pl.BlockSpec((4, 256, 384), lambda i, m: (0, 0, 0))] * 2,
        [
            pltpu.VMEM((4, rows, width), LOW),
            pltpu.VMEM((width, 384), F32),
            pltpu.SemaphoreType.DMA((4, 4)),
        ],
        after=after,
    )


def project_last_kernel(ix, p0, p1, p2, p3, q_ref, k_ref, v_ref):
    for slot, ref in enumerate((p0, p1, p2, p3)):
        at = pl.ds(pl.multiple_of((slot ^ ix[ME]) * 128, 128), 128)
        for place, out in enumerate((q_ref, k_ref, v_ref)):
            out[:, at] = ref[:, place * 128 : (place + 1) * 128].astype(F32)


def project_last(ix, pieces):
    share = pieces[0].shape[0]
    whole = lambda i, m: (0, 0)
    return call(
        project_last_kernel, "project_last", ix, (1,), list(pieces),
        [pl.BlockSpec((share, 384), whole)] * 4,
        [shaped((share, 512), F32)] * 3, [pl.BlockSpec((share, 512), whole)] * 3,
    )


def over_ctx(slots):
    return [slots[0]] + [swap(slots[k], CTX, k) for k in range(1, 4)]


def per_device(
    dp_size, tokens, attn_gain, w_query, w_key, w_value, w_out, mlp_gain, w_gate, w_up, w_down, cotangent
):
    rows_here, width = tokens.shape
    share = width // (4 * dp_size)
    me, t, d = lax.axis_index(CTX), lax.axis_index(TENSOR), lax.axis_index("dp")
    two_dp = dp_size == 2
    ix = jnp.stack([me, t, d if two_dp else jnp.zeros_like(d)]).astype(jnp.int32)
    order = me ^ jnp.arange(4)
    projections = (w_query, w_key, w_value)
    attn_gain, mlp_gain = attn_gain.reshape(1, -1), mlp_gain.reshape(1, -1)

    cot_mine = lax.dynamic_slice_in_dim(cotangent, t * (rows_here // 4), rows_here // 4, 0)
    tables = rope_tables(me * rows_here + jnp.arange(rows_here, dtype=jnp.int32))
    first_in, *slots = project(ix, tokens, attn_gain, tables, projections)
    pieces = over_ctx(slots)

    back_own = hidden_back(ix, cotangent, rows_here, w_down, (slots[0],))
    all_tables = all_rope_tables(ix, 4 * rows_here, (back_own,))
    (first_mine,) = mine(ix, [first_in], (all_tables[0],))
    cot_mine = tie(ix, cot_mine, (*pieces[1:], first_mine))
    cot_both = lax.all_gather(cot_mine, ("lo", *TENSOR), axis=0, tiled=True)

    *mixed_slots, raw, lse = attend(ix, pieces, (first_mine,))
    mixed = over_ctx(mixed_slots)
    keep, send = join_heads(ix, mixed, w_out, (cot_both,))
    core = swap(send, TENSOR, 1)
    low = sums_to_send(ix, [(keep, 1), (core, 1)])
    middle, second_mine = rows_call(
        middle_kernel, "middle", ix, [(keep, 0), (core, 0), swap(low, TENSOR, 2)], [tokens, mlp_gain], [F32, LOW]
    )

    second_both = lax.all_gather(second_mine, ("lo", *TENSOR), axis=0, tiled=True)
    back_far = hidden_back(ix, cot_both, rows_here, w_down, (second_mine,))
    own_pieces = spread(second_mine, lambda two: tie(ix, two, (back_far,)))
    second_own, hid_own, gb_own, ub_own, keep_own, send = feed(ix, own_pieces, w_gate, w_up, back_own)
    first_all = lax.all_gather(tie(ix, first_mine, (hid_own,)), CTX, axis=0, tiled=False)
    core_own = swap(send, TENSOR, 1)
    second_far, hid_far, gb_far, ub_far, keep, send = feed(ix, [second_both], w_gate, w_up, back_far, (hid_own,))

    seconds = (second_own, second_far)

    def over_pairs(part):
        return lax.psum_scatter(part, ("dp", "hi"), scatter_dimension=0, tiled=True) if two_dp else part

    core = swap(send, TENSOR, 1)
    part_down = wgrad(ix, (cotangent, cot_both), (hid_own, hid_far), "wgrad_down")
    sum_down = over_pairs(part_down)
    low = sums_to_send(ix, [(keep, 1), (core, 1)], (part_down,))
    far_y = swap(low, TENSOR, 2)
    down_far = feed_down(ix, hid_far, w_down, (low,))
    low = sums_to_send(ix, [(keep, 0), (core, 0), far_y], (down_far[0],))
    far_z = swap(low, CTX, 1)
    low = sums_to_send(ix, [(keep_own, 1), (core_own, 1)], (low,))
    own_sums = [(keep_own, 0), (core_own, 0), swap(low, TENSOR, 2)]
    core_far = swap(down_far[1], TENSOR, 1)
    down_own = feed_down(ix, hid_own, w_down, (low,))
    low = sums_to_send(ix, [(down_far[0], 1), (core_far, 1)], (down_own[0],))
    far_down = [(down_far[0], 0), (core_far, 0), swap(low, TENSOR, 2)]
    middle_grad, branch_mine, mlp_gain_part = rows_call(
        middle_back_kernel, "middle_back", ix, [*own_sums, far_z, middle], [cotangent, mlp_gain], [F32, LOW], 1,
        (low,),
    )
    part_gate = wgrad(ix, seconds, (gb_own, gb_far), "wgrad_gate", (branch_mine,))
    sum_gate = over_pairs(part_gate)
    core_own = swap(tie(ix, down_own[1], (branch_mine,)), TENSOR, 1)
    branch_low, *slots = branch_back(
        ix, spread(branch_mine, lambda two: tie(ix, two, (part_gate,))), w_out, (part_gate,)
    )
    upstreams = over_ctx(slots)
    first_far = others(ix, first_all, (branch_low,))
    out_own, out_far = out_wgrad(ix, mixed, branch_low, (first_far,))
    low = sums_to_send(ix, [(down_own[0], 1), (core_own, 1)], (out_own,))
    own_y = swap(low, TENSOR, 2)

    def for_partner(blocks, after):
        return swap(blocks[1:] if after is None else one_block(ix, blocks, 1, after), CTX, 1)

    arrived = [far_down[2], own_y]
    if two_dp:
        out_other = swap(out_far, "dp", 1)
        down_other = for_partner(sum_down, (low,))
        arrived += [out_other, down_other]
    back_slots = attend_back(ix, pieces, upstreams, raw, lse, all_tables, (low,))
    back = over_ctx(back_slots)

    arrived = (back_slots[0], *arrived)
    first_spread = spread(first_far, lambda two: tie(ix, two, arrived), lambda quarter: tie(ix, quarter, arrived))
    qkv_own, qkv_far = project_wgrad(ix, first_in, first_spread, back_slots)
    far_low = sums_to_send(ix, far_down, (qkv_own,))
    part_up = wgrad(ix, seconds, (ub_own, ub_far), "wgrad_up", (far_low,))
    sum_up = over_pairs(tie(ix, part_up, back[1:]))
    token = part_up
    if two_dp:
        out_part = add_blocks(ix, out_own, out_other, 2, (part_up,))
        down_grad = halves(ix, sum_down, down_other, 0, (out_part[0],))
        token = down_grad
    keep, send = project_back(ix, back, projections, (token,))
    core = swap(send, TENSOR, 1)
    low = sums_to_send(ix, [(keep, 1), (core, 1)])
    low_y = swap(low, TENSOR, 2)
    far_z = swap(tie(ix, far_low, (low,)), CTX, 1)
    token = low
    if two_dp:
        gate_low = one_block(ix, sum_gate, 1, (low,))
        token = gate_low
    input_mine = input_back(ix, keep, core, low_y, middle_grad, tokens, attn_gain, mlp_gain_part, (token,))
    input_pieces = spread(input_mine)
    token = input_mine
    if two_dp:
        (qkv_part,) = add_blocks(ix, qkv_own, swap(qkv_far, "dp", 1), 1, (input_mine,))
        out_z = swap(tie(ix, out_part[1], (keep,)), CTX, 2)
        token = qkv_part
    (output_mine,) = rows_call(
        output_kernel, "output", ix, [(down_own[0], 0), (core_own, 0), own_y, far_z, middle], [], [LOW], after=(token,)
    )
    input_grad, gains = join_input(ix, input_pieces, (output_mine,))
    output_pieces = spread(output_mine, late=lambda quarter: tie(ix, quarter, (input_grad,)))
    if two_dp:
        qkv_parts = over_ctx(qkv_part)
        out_part = add_blocks(ix, out_part[0], out_z, 2, (input_grad,))
        out_other = swap(out_part[1], CTX, 1)
        gate_grad = halves(ix, sum_gate, swap(gate_low, CTX, 1), 1, (out_part[0],))
        up_low = one_block(ix, sum_up, 1, (gate_grad,))
        output = join(ix, output_pieces, (up_low,))
        up_grad = halves(ix, sum_up, swap(up_low, CTX, 1), 1, (output,))
        out_grad = out_part[0][0].astype(F32) + out_other[0].astype(F32)
    else:
        output = join(ix, output_pieces)

        def scattered(blocks, axis):
            blocks = jnp.moveaxis(blocks, 0, axis)
            shape = blocks.shape[:axis] + (width,) + blocks.shape[axis + 2 :]
            part = lax.psum_scatter(blocks.reshape(shape), "dp", scatter_dimension=axis, tiled=True)
            shape = part.shape[:axis] + (4, share) + part.shape[axis + 1 :]
            return jnp.moveaxis(part.reshape(shape), axis, 0)

        def in_order(blocks):
            return blocks.reshape(2, 4, *blocks.shape[1:])[:, order].reshape(blocks.shape)

        grads = []
        low_bit = me % 2 ^ jnp.arange(2)
        for k, blocks in enumerate((sum_down, sum_gate, sum_up)):
            blocks = blocks.reshape(4, 2, *blocks.shape[1:])[:, low_bit].reshape(blocks.shape)
            part = scattered(blocks, 0)[order].astype(F32)
            part = (part[:2] + swap(part[2:].astype(LOW), CTX, 2).astype(F32)).astype(LOW)
            grads.append(halves(ix, part, for_partner(part, None), min(k, 1)))
        down_grad, gate_grad, up_grad = grads
        qkv_parts = over_ctx(scattered(in_order(jnp.concatenate([qkv_own, qkv_far])), 0)[order])
        out_part = scattered(in_order(jnp.concatenate([out_own, out_far])), 1)[order]
        out_part = out_part[:2].astype(F32) + swap(out_part[2:], CTX, 2).astype(F32)
        out_grad = out_part[0] + swap(out_part[1].astype(LOW), CTX, 1).astype(F32)
    qkv = project_last(ix, qkv_parts)

    gains = gains[:2]
    if two_dp:
        halved = gains.reshape(2, 2, width // 2)[:, d ^ jnp.arange(2)]
        gains = halved[:, 0] + swap(halved[:, 1], "dp", 1)
    else:
        gains = lax.psum_scatter(gains, "dp", scatter_dimension=1, tiled=True)
    gains = sum(over_ctx(gains.reshape(2, 4, share).transpose(1, 0, 2)[order]))

    return (
        output,
        input_grad,
        gains[0],
        qkv[0],
        qkv[1],
        qkv[2],
        out_grad,
        gains[1],
        gate_grad,
        up_grad,
        down_grad,
    )


def solution(mesh):
    dp_size = mesh.shape["dp"]
    mesh = jax.sharding.Mesh(mesh.devices.reshape(dp_size, 2, 2, 2, 2), ("dp", *CTX, *TENSOR))
    rows, tensor = ("dp", *CTX), TENSOR
    columns = P(None, tensor)
    in_specs = (
        P(rows, None), P(), columns, columns, columns, P(tensor, None),
        P(), columns, columns, P(tensor, None), P(rows, None),
    )
    out_specs = (
        P(rows, None), P(rows, None), P(rows), P(rows, tensor), P(rows, tensor), P(rows, tensor),
        P(tensor, rows), P(rows), P(rows, tensor), P(rows, tensor), P(tensor, rows),
    )
    return jax.shard_map(
        functools.partial(per_device, dp_size),
        mesh=mesh,
        in_specs=in_specs,
        out_specs=out_specs,
        check_vma=False,
    )
```

```python
import functools

import jax
import jax.numpy as jnp
from jax import lax
from jax.experimental import pallas as pl
from jax.experimental.pallas import tpu as pltpu
from jax.sharding import PartitionSpec as P

HEAD_DIM = 64
EPS = 1e-05
THETA = 130000.0
MIB = 1 << 20
MOST = 64
COSTS = {
    "project": 11, "hidden_back": 8.5, "rope_tables": 8, "attend": 28, "quarter": 3,
    "join_heads": 6.5, "sums": 3, "join": 3.5, "middle": 4, "feed": 24, "wgrad_down": 14, "wgrad_gate": 14, "wgrad_up": 14,
    "middle_back": 5, "branch_back": 7, "others": 4, "feed_down": 9, "attend_back": 40, "project_wgrad": 13,
    "out_wgrad": 8.5, "add_pairs": 4, "project_back": 11, "input_back": 5, "output": 4, "halves": 3.5,
    "project_last": 3, "add_blocks": 3, "one_block": 2,
}
SCALE = 2
LOW = jnp.bfloat16
F32 = jnp.float32
ANY = pl.BlockSpec(memory_space=pl.ANY)


CTX, TENSOR = ("hi", "lo"), ("y", "core")


def swap(value, axis, distance):
    size = 2 if axis == "dp" else 4
    return lax.ppermute(value, axis, [(i, i ^ distance) for i in range(size)])


def dot(left, right):
    return jnp.dot(left, right, preferred_element_type=F32)


def against(left, right):
    return lax.dot_general(left, right, (((1,), (1,)), ((), ())), preferred_element_type=F32)


def across(left, right):
    return lax.dot_general(left, right, (((0,), (0,)), ((), ())), preferred_element_type=F32)


def shaped(shape, dtype=LOW):
    return jax.ShapeDtypeStruct(shape, dtype)


def call(kernel, name, index, grid, inputs, in_specs, outs, out_specs, scratch=(), mib=MOST, after=()):
    count = len(inputs)

    def body(index_ref, *refs):
        kernel(index_ref, *refs[:count], *refs[count + len(after) :])

    return pl.pallas_call(
        body,
        grid_spec=pltpu.PrefetchScalarGridSpec(
            num_scalar_prefetch=1,
            grid=grid,
            in_specs=list(in_specs) + [ANY] * len(after),
            out_specs=out_specs,
            scratch_shapes=list(scratch),
        ),
        out_shape=outs,
        compiler_params=pltpu.CompilerParams(
            vmem_limit_bytes=mib * MIB, dimension_semantics=("arbitrary",) * len(grid)
        ),
        cost_estimate=pl.CostEstimate(flops=0, bytes_accessed=int(COSTS.get(name, 0) * SCALE * 3.5 * MIB), transcendentals=0),
        name=name,
    )(index, *inputs, *after)


ME, T, DP = 0, 1, 2


def copy_all(pairs, sems):
    copies = [pltpu.make_async_copy(a, b, sems.at[k]) for k, (a, b) in enumerate(pairs)]
    for copy in copies:
        copy.start()
    for copy in copies:
        copy.wait()


def half_turn(rows):
    lane = lax.broadcasted_iota(jnp.int32, (1, 128), 1)
    first = (lane % HEAD_DIM) < HEAD_DIM // 2
    return jnp.where(first, pltpu.roll(rows, 96, 1), pltpu.roll(rows, 32, 1))


def rope_freq():
    half = HEAD_DIM // 2
    freq = jnp.power(THETA, -jnp.arange(half, dtype=F32) * (2.0 / HEAD_DIM))
    return jnp.concatenate([freq] * 4)


def rope_tables(positions):
    sign = jnp.where((jnp.arange(128) % HEAD_DIM) < HEAD_DIM // 2, -1.0, 1.0)
    angle = positions.astype(F32)[:, None] * rope_freq()[None, :]
    return jnp.cos(angle), jnp.sin(angle) * sign


def project_kernel(ix, tok_ref, gain_ref, cos_ref, sin_ref, wq_ref, wk_ref, wv_ref, first_ref, o0, o1, o2, o3, held):
    me = ix[ME]
    rows = tok_ref[...].astype(F32)
    inverse = lax.rsqrt(jnp.mean(rows * rows, axis=-1, keepdims=True) + EPS)
    first = (rows * inverse * gain_ref[...]).astype(LOW)
    first_ref[...] = first
    cosine, sine = cos_ref[...], sin_ref[...]
    for place, weight in enumerate((wq_ref, wk_ref, wv_ref)):
        flat = dot(first, weight[...])
        for group in range(4):
            part = flat[:, group * 128 : (group + 1) * 128]
            if place < 2:
                part = part * cosine + half_turn(part) * sine
            if place == 0:
                part = part * HEAD_DIM**-0.5
            held[group, :, place * 128 : (place + 1) * 128] = part.astype(LOW)
    for slot, out in enumerate((o0, o1, o2, o3)):
        out[...] = held[slot ^ me]


def project(ix, tokens, gain, tables, weights):
    rows, width = tokens.shape
    local = weights[0].shape[1]
    step = 256
    whole = lambda i, m: (0, 0)
    along = lambda i, m: (i, 0)
    return call(
        project_kernel, "project", ix, (rows // step,),
        [tokens, gain, *tables, *weights],
        [pl.BlockSpec((step, width), along), pl.BlockSpec((1, width), whole)]
        + [pl.BlockSpec((step, 128), along)] * 2 + [pl.BlockSpec((width, local), whole)] * 3,
        [shaped((rows, width))] + [shaped((rows, 384))] * 4,
        [pl.BlockSpec((step, width), along)] + [pl.BlockSpec((step, 384), along)] * 4,
        [pltpu.VMEM((4, step, 384), LOW)],
    )


def own_lanes(rows, head):
    lane = lax.broadcasted_iota(jnp.int32, (1, 128), 1)
    inside = (lane < HEAD_DIM) if head == 0 else (lane >= HEAD_DIM)
    return jnp.where(inside, rows, jnp.zeros_like(rows))


def attend_kernel(ix, r0, r1, r2, r3, o0, o1, o2, o3, raw_ref, lse_ref, held, sems):
    me = ix[ME]
    turn = pl.program_id(0)
    here = turn ^ me
    stretch = r0.shape[0]
    half = stretch // 2
    lane = lax.broadcasted_iota(jnp.int32, (1, 128), 1)

    @pl.when(turn == 0)
    def _():
        copy_all(
            [(ref, held.at[pl.ds((me ^ k) * stretch, stretch)]) for k, ref in enumerate((r0, r1, r2, r3))], sems
        )

    query = held[pl.ds(here * stretch, stretch), 0:128]
    queries = [own_lanes(query, head) for head in range(2)]

    def step(queries, rows, carry, offset):
        keys, values = held[rows, 128:256], held[rows, 256:384]
        out = []
        for head in range(2):
            peak, mass, total = carry[3 * head : 3 * head + 3]
            scores = against(queries[head], keys)
            if offset is not None:
                down = lax.broadcasted_iota(jnp.int32, scores.shape, 0) + offset
                along = lax.broadcasted_iota(jnp.int32, scores.shape, 1)
                scores = jnp.where(down >= along, scores, -1e30)
            top = jnp.maximum(peak, jnp.max(scores, axis=-1, keepdims=True))
            weights = jnp.exp(scores - top)
            fade = jnp.exp(peak - top)
            mass = mass * fade + jnp.sum(weights, axis=-1, keepdims=True)
            out += [top, mass, total * fade + dot(weights.astype(LOW), values)]
        return tuple(out)

    start = (
        jnp.full((stretch, 1), -1e30, F32),
        jnp.zeros((stretch, 1), F32),
        jnp.zeros((stretch, 128), F32),
    ) * 2
    carry = lax.fori_loop(0, here, lambda at, c: step(queries, pl.ds(at * stretch, stretch), c, None), start)
    for part in range(2):
        at = slice(part * half, (part + 1) * half)
        rows = pl.ds(here * stretch, (part + 1) * half)
        done = step([query[at] for query in queries], rows, [c[at] for c in carry], part * half)
        peak0, mass0, total0, peak1, mass1, total1 = done
        mixed = jnp.where(lane < HEAD_DIM, total0 / mass0, total1 / mass1)
        raw_ref[at, :] = mixed
        for slot, out in enumerate((o0, o1, o2, o3)):

            @pl.when(turn == slot)
            def _():
                out[at, :] = mixed.astype(LOW)

        turned = jnp.where(lane < HEAD_DIM, peak0 + jnp.log(mass0), peak1 + jnp.log(mass1)).T
        lse_ref[0, 0:8, at] = turned[0:8]
        lse_ref[0, 8:16, at] = turned[64:72]


def attend(ix, pieces, after):
    stretch = pieces[0].shape[0]
    length = 4 * stretch
    return call(
        attend_kernel, "attend", ix, (4,), list(pieces), [ANY] * 4,
        [shaped((stretch, 128))] * 4 + [shaped((length, 128), F32), shaped((4, 16, stretch), F32)],
        [pl.BlockSpec((stretch, 128), lambda i, m: (0, 0))] * 4
        + [
            pl.BlockSpec((stretch, 128), lambda i, m: (i ^ m[ME], 0)),
            pl.BlockSpec((1, 16, stretch), lambda i, m: (i ^ m[ME], 0, 0)),
        ],
        [pltpu.VMEM((length, 384), LOW), pltpu.SemaphoreType.DMA((4,))], after=after,
    )


def attend_back_kernel(
    ix, p0, p1, p2, p3, u0, u1, u2, u3, raw_ref, lse_ref, cos_ref, sin_ref, o0, o1, o2, o3,
    held, up, query_at, up_at, delta, query_sum, key_sum, value_sum, sems,
):
    me = ix[ME]
    turn = pl.program_id(0)
    count = pl.num_programs(0)
    stretch = p0.shape[0]
    half = stretch // 2
    here = turn ^ me

    @pl.when(turn == 0)
    def _():
        rows = [pl.ds((me ^ k) * stretch, stretch) for k in range(4)]
        copy_all(
            [(ref, held.at[rows[k]]) for k, ref in enumerate((p0, p1, p2, p3))]
            + [(ref, up.at[rows[k]]) for k, ref in enumerate((u0, u1, u2, u3))],
            sems,
        )
        query_sum[...] = jnp.zeros_like(query_sum)

        def prepare(at, _):
            rows = pl.ds(at * stretch, stretch)
            query, upstream = held[rows, 0:128], up[rows, :]
            turned = (upstream.astype(F32) * raw_ref[rows, :]).T
            for head in range(2):
                query_at[head, rows, :] = own_lanes(query, head)
                up_at[head, rows, :] = own_lanes(upstream, head)
                total = jnp.sum(turned[head * 64 : head * 64 + 64], axis=0, keepdims=True)
                delta[at, head * 8 : head * 8 + 8, :] = jnp.broadcast_to(total, (8, stretch))
            return 0

        lax.fori_loop(0, count, prepare, 0)

    here_rows = pl.ds(here * stretch, stretch)
    key, value = held[here_rows, 128:256], held[here_rows, 256:384]
    keys = [own_lanes(key, head) for head in range(2)]
    values = [own_lanes(value, head) for head in range(2)]

    def step(at, queries, kept, diagonal):
        size = queries.stop - queries.start
        rows = pl.ds(at * stretch + queries.start, size)
        query, upstream = held[rows, 0:128], up[rows, :]
        key_total = value_total = query_total = None
        for head in range(2):
            scores = against(keys[head][:kept], query)
            lse = lse_ref[at, head * 8 : head * 8 + 1, queries]
            chance = jnp.exp(scores - lse)
            if diagonal:
                down = lax.broadcasted_iota(jnp.int32, scores.shape, 0)
                along = lax.broadcasted_iota(jnp.int32, scores.shape, 1) + queries.start
                chance = jnp.where(along >= down, chance, 0.0)
            chance_back = against(values[head][:kept], upstream)
            shift = delta[at, head * 8 : head * 8 + 1, queries]
            score_back = (chance * (chance_back - shift)).astype(LOW)
            value_part = dot(chance.astype(LOW), up_at[head, rows, :])
            key_part = dot(score_back, query_at[head, rows, :])
            query_part = across(score_back, keys[head][:kept])
            if head == 0:
                value_total, key_total, query_total = value_part, key_part, query_part
            else:
                value_total += value_part
                key_total += key_part
                query_total += query_part
        query_sum[rows, :] += query_total
        return key_total, value_total

    key_sum[...], value_sum[...] = step(here, slice(half, stretch), stretch, True)
    key_total, value_total = step(here, slice(0, half), half, True)
    key_sum[:half] += key_total
    value_sum[:half] += value_total

    def later(at, _):
        key_total, value_total = step(at, slice(0, stretch), stretch, False)
        key_sum[...] += key_total
        value_sum[...] += value_total
        return 0

    lax.fori_loop(here + 1, count, later, 0)

    def back_rope(rows, at):
        places = pl.ds(at * stretch, stretch)
        return rows * cos_ref[places, :] - half_turn(rows) * sin_ref[places, :]

    key_low, value_low = back_rope(key_sum[...], here).astype(LOW), value_sum[...].astype(LOW)
    for slot, out in enumerate((o0, o1, o2, o3)):

        @pl.when(turn == slot)
        def _():
            out[:, 128:256] = key_low
            out[:, 256:384] = value_low

    @pl.when(turn == count - 1)
    def _():
        for slot, out in enumerate((o0, o1, o2, o3)):
            rows = query_sum[pl.ds((slot ^ me) * stretch, stretch), :] * HEAD_DIM**-0.5
            out[:, 0:128] = back_rope(rows, slot ^ me).astype(LOW)


def attend_back(ix, pieces, upstreams, raw, lse, tables, after):
    stretch = pieces[0].shape[0]
    length = 4 * stretch
    whole = lambda i, m: (0, 0)
    return call(
        attend_back_kernel, "attend_back", ix, (4,), [*pieces, *upstreams, raw, lse, *tables],
        [ANY] * 8
        + [pl.BlockSpec((length, 128), whole), pl.BlockSpec((4, 16, stretch), lambda i, m: (0, 0, 0))]
        + [pl.BlockSpec((length, 128), whole)] * 2,
        [shaped((stretch, 384))] * 4,
        [pl.BlockSpec((stretch, 384), whole)] * 4,
        [
            pltpu.VMEM((length, 384), LOW),
            pltpu.VMEM((length, 128), LOW),
            pltpu.VMEM((2, length, 128), LOW),
            pltpu.VMEM((2, length, 128), LOW),
            pltpu.VMEM((4, 16, stretch), F32),
            pltpu.VMEM((length, 128), F32),
            pltpu.VMEM((stretch, 128), F32),
            pltpu.VMEM((stretch, 128), F32),
            pltpu.SemaphoreType.DMA((8,)),
        ],
        after=after,
    )


def quarter_outs(rows, width, step):
    return (
        [shaped((2, rows // 4, width))] * 2,
        [pl.BlockSpec((2, rows // 4, step), lambda i, m: (0, 0, i))] * 2,
    )


def in_quarters(t, ref, held, columns=slice(None)):
    rows = ref.shape[0] // 4
    return [
        (ref.at[pl.ds((t ^ k) * rows, rows)], held.at[pl.ds(place * rows, rows), columns])
        for place, k in enumerate((0, 2, 1, 3))
    ]


def store_quarters(total, keep_ref, send_ref):
    rows = keep_ref.shape[1]
    for k in range(2):
        keep_ref[k] = total[k * rows : (k + 1) * rows].astype(LOW)
        send_ref[k] = total[(2 + k) * rows : (3 + k) * rows].astype(LOW)


def feed_down_kernel(ix, left_ref, right_ref, keep_ref, send_ref, held, sems):
    @pl.when(pl.program_id(0) == 0)
    def _():
        copy_all(in_quarters(ix[T], left_ref, held), sems)

    store_quarters(dot(held[...], right_ref[...]), keep_ref, send_ref)


def feed_down(ix, hidden, w_down, after=()):
    rows, units = hidden.shape
    width = w_down.shape[1]
    step = 512
    outs, out_specs = quarter_outs(rows, width, step)
    return call(
        feed_down_kernel, "feed_down", ix, (width // step,), [hidden, w_down],
        [ANY, pl.BlockSpec((units, step), lambda i, m: (m[ME] % 2, i))], outs, out_specs,
        [pltpu.VMEM((rows, units), LOW), pltpu.SemaphoreType.DMA((4,))], after=after,
    )


def join_heads_kernel(ix, a0, a1, a2, a3, w0, w1, w2, w3, keep_ref, send_ref, held, sems):
    @pl.when(pl.program_id(0) == 0)
    def _():
        copy_all(
            [
                pair
                for k, ref in enumerate((a0, a1, a2, a3))
                for pair in in_quarters(ix[T], ref, held, slice(k * 128, (k + 1) * 128))
            ],
            sems,
        )

    right = jnp.concatenate([w0[...], w1[...], w2[...], w3[...]], axis=0)
    store_quarters(dot(held[...], right), keep_ref, send_ref)


def join_heads(ix, mixed, w_out, after=()):
    rows = mixed[0].shape[0]
    width = w_out.shape[1]
    step = 1024

    def heads(slot):
        return pl.BlockSpec((128, step), lambda i, m: (m[ME] ^ slot, i))

    outs, out_specs = quarter_outs(rows, width, step)
    return call(
        join_heads_kernel, "join_heads", ix, (width // step,), [*mixed] + [w_out] * 4,
        [ANY] * 4 + [heads(slot) for slot in range(4)], outs, out_specs,
        [pltpu.VMEM((rows, 512), LOW), pltpu.SemaphoreType.DMA((16,))], after=after,
    )


def project_back_kernel(ix, *refs):
    keep_ref, send_ref, held, sems = refs[16:]

    @pl.when(pl.program_id(0) == 0)
    def _():
        copy_all(
            [
                pair
                for k, ref in enumerate(refs[:4])
                for pair in in_quarters(ix[T], ref, held, slice(k * 384, (k + 1) * 384))
            ],
            sems,
        )

    right = jnp.concatenate([ref[...] for ref in refs[4:16]], axis=1)
    store_quarters(against(held[...], right), keep_ref, send_ref)


def project_back(ix, back, weights, after):
    rows = back[0].shape[0]
    width = weights[0].shape[0]
    step = 512

    def heads(slot):
        return pl.BlockSpec((step, 128), lambda i, m: (i, m[ME] ^ slot))

    outs, out_specs = quarter_outs(rows, width, step)
    return call(
        project_back_kernel, "project_back", ix, (width // step,),
        [*back] + [w for slot in range(4) for w in weights],
        [ANY] * 4 + [heads(slot) for slot in range(4) for w in weights], outs, out_specs,
        [pltpu.VMEM((rows, 1536), LOW), pltpu.SemaphoreType.DMA((16,))], after=after,
    )


def rows_call(kernel, name, ix, quarters, others, outs, sums=0, after=()):
    arrays = [a if isinstance(a, tuple) else (a, None) for a in (*quarters, *others)]
    rows, width = arrays[0][0].shape[-2:]
    step = rows // 2

    def spec(array, which):
        if which is not None:
            return pl.BlockSpec((None, step, width), lambda i, m: (which, i, 0))
        if array.shape[0] == 1:
            return pl.BlockSpec((1, width), lambda i, m: (0, 0))
        if array.shape[0] == rows:
            return pl.BlockSpec((step, width), lambda i, m: (i, 0))
        return pl.BlockSpec((step, width), lambda i, m: (2 * m[T] + i, 0))

    return call(
        kernel, name, ix, (2,), [array for array, _ in arrays], [spec(*pair) for pair in arrays],
        [shaped((rows, width), dtype) for dtype in outs] + [shaped((1, width), F32)] * sums,
        [pl.BlockSpec((step, width), lambda i, m: (i, 0))] * len(outs)
        + [pl.BlockSpec((1, width), lambda i, m: (0, 0))] * sums,
        after=after,
    )


def wide_sum(*refs):
    return sum(ref[...].astype(F32) for ref in refs)


def sum_kernel(ix, *refs):
    refs[-1][...] = wide_sum(*refs[:-1]).astype(LOW)


def sums_to_send(ix, arrays, after=()):
    return rows_call(sum_kernel, "sums", ix, arrays, [], [LOW], after=after)[0]


def middle_kernel(ix, one, two, y_ref, tok_ref, gain_ref, middle_ref, second_ref):
    middle = tok_ref[...].astype(F32) + wide_sum(one, two, y_ref)
    middle_ref[...] = middle
    normed, _ = normalize(middle)
    second_ref[...] = (normed * gain_ref[...]).astype(LOW)


def add_rows(out_ref, rows):
    part = jnp.sum(rows, axis=0, keepdims=True)

    @pl.when(pl.program_id(0) == 0)
    def _():
        out_ref[...] = part

    @pl.when(pl.program_id(0) != 0)
    def _():
        out_ref[...] += part


def middle_back_kernel(ix, one, two, y_ref, z_ref, middle_ref, cot_ref, gain_ref, grad_ref, low_ref, sum_ref):
    second_sum = wide_sum(one, two, y_ref, z_ref)
    normed, inverse = normalize(middle_ref[...])
    grad = cot_ref[...].astype(F32) + norm_back(second_sum, normed, inverse, gain_ref[...])
    grad_ref[...] = grad
    low_ref[...] = grad.astype(LOW)
    add_rows(sum_ref, second_sum * normed)


def output_kernel(ix, one, two, y_ref, z_ref, middle_ref, out_ref):
    out_ref[...] = (middle_ref[...] + wide_sum(one, two, y_ref, z_ref)).astype(LOW)


def input_kernel(ix, one, two, y_ref, grad_ref, tok_ref, gain_ref, mlp_ref, out_ref, total):
    here, last = pl.program_id(0), pl.num_programs(0) - 1

    @pl.when(here < last)
    def _():
        first_sum = wide_sum(one, two, y_ref)
        normed, inverse = normalize(tok_ref[...].astype(F32))
        out_ref[...] = (grad_ref[...] + norm_back(first_sum, normed, inverse, gain_ref[...])).astype(LOW)
        add_rows(total, first_sum * normed)

    @pl.when(here == last)
    def _():
        sums = jnp.concatenate([total[...], mlp_ref[...], jnp.zeros((14, total.shape[1]), F32)], axis=0)
        out_ref[0:16, :] = sums.astype(LOW)


def input_back(ix, keep, core, y, grad, tokens, gain, mlp_sum, after):
    rows, width = grad.shape
    step = rows // 2
    at = lambda i: jnp.minimum(i, 1)
    block = pl.BlockSpec((None, step, width), lambda i, m: (0, at(i), 0))
    row = pl.BlockSpec((step, width), lambda i, m: (at(i), 0))
    single = pl.BlockSpec((1, width), lambda i, m: (0, 0))
    return call(
        input_kernel, "input_back", ix, (3,), [keep, core, y, grad, tokens, gain, mlp_sum],
        [block, block, row, row, pl.BlockSpec((step, width), lambda i, m: (2 * m[T] + at(i), 0)), single, single],
        shaped((rows + 16, width)), pl.BlockSpec((step, width), lambda i, m: (i, 0)),
        [pltpu.VMEM((1, width), F32)], after=after,
    )


def join_input_kernel(ix, q0, q1, q2, q3, out_ref, sum_ref, held, sems):
    rows = out_ref.shape[0] // 4
    ins, outs = [], []
    for k, ref in enumerate((q0, q1, q2, q3)):
        ins.append(pltpu.make_async_copy(ref, held.at[k], sems.at[k]))
        at = pl.ds((ix[T] ^ k) * rows, rows)
        outs.append(pltpu.make_async_copy(held.at[k, pl.ds(0, rows)], out_ref.at[at], sems.at[4 + k]))
    for copy in ins:
        copy.start()
    total = jnp.zeros(sum_ref.shape, F32)
    for k, (one, two) in enumerate(zip(ins, outs)):
        one.wait()
        two.start()
        total = total + held[k, rows : rows + 16, :].astype(F32)
    sum_ref[...] = total
    for copy in outs:
        copy.wait()


def join_input(ix, pieces, after):
    rows, width = pieces[0].shape
    rows -= 16
    return call(
        join_input_kernel, "join", ix, (1,), list(pieces), [ANY] * 4,
        [shaped((4 * rows, width)), shaped((16, width), F32)],
        [ANY, pl.BlockSpec((16, width), lambda i, m: (0, 0))],
        [pltpu.VMEM((4, rows + 16, width), LOW), pltpu.SemaphoreType.DMA((8,))], after=after,
    )


def normalize(vector):
    inverse = lax.rsqrt(jnp.mean(vector * vector, axis=-1, keepdims=True) + EPS)
    return (vector * inverse, inverse)


def norm_back(grad_rows, normed, inverse, gain):
    scaled = grad_rows * gain
    return inverse * (scaled - normed * jnp.mean(scaled * normed, axis=-1, keepdims=True))


def tie(ix, value, after):
    return pl.pallas_call(
        lambda *refs: None,
        grid_spec=pltpu.PrefetchScalarGridSpec(
            num_scalar_prefetch=1, grid=(1,), in_specs=[ANY] * (1 + len(after)), out_specs=ANY
        ),
        out_shape=shaped(value.shape, value.dtype),
        input_output_aliases={1: 0},
        cost_estimate=pl.CostEstimate(flops=0, bytes_accessed=0, transcendentals=0),
        name="tie",
    )(ix, value, *after)


def spread(quarter, hold=lambda two: two, late=lambda quarter: quarter):
    two = hold(swap(quarter, TENSOR, 2))
    one = swap(late(quarter), TENSOR, 1)
    three = swap(two, TENSOR, 1)
    return (quarter, one, two, three)


def quarter_copies(t, pieces, held):
    rows = pieces[0].shape[0]
    return [(ref, held.at[pl.ds((t ^ k) * rows, rows)]) for k, ref in enumerate(pieces)]


def join_kernel(ix, q0, q1, q2, q3, out_ref, held, sems):
    rows = q0.shape[0]
    ins, outs = [], []
    for k, ref in enumerate((q0, q1, q2, q3)):
        ins.append(pltpu.make_async_copy(ref, held.at[k], sems.at[k]))
        at = pl.ds((ix[T] ^ k) * rows, rows)
        outs.append(pltpu.make_async_copy(held.at[k], out_ref.at[at], sems.at[4 + k]))
    for copy in ins:
        copy.start()
    for one, two in zip(ins, outs):
        one.wait()
        two.start()
    for copy in outs:
        copy.wait()


def join(ix, pieces, after=()):
    rows, width = pieces[0].shape
    return call(
        join_kernel, "join", ix, (1,), list(pieces), [ANY] * 4,
        shaped((4 * rows, width)), ANY,
        [pltpu.VMEM((4, rows, width), LOW), pltpu.SemaphoreType.DMA((8,))], after=after,
    )


def mine_kernel(ix, *refs):
    count = len(refs) // 2
    rows = refs[count].shape[0]
    at = pl.ds(ix[T] * rows, rows)
    copy_all([(refs[k].at[at], refs[count + k]) for k in range(count)], refs[-1])


def mine(ix, arrays, after):
    count, width = arrays[0].shape
    size = len(arrays)
    return call(
        mine_kernel, "quarter", ix, (1,), list(arrays), [ANY] * size, [shaped((count // 4, width))] * size,
        [pl.BlockSpec((count // 4, width), lambda i, m: (0, 0))] * size, [pltpu.SemaphoreType.DMA((size,))],
        after=after,
    )


def others_kernel(ix, rows_ref, out_ref, sems):
    copy_all([(rows_ref.at[ix[ME] ^ k], out_ref.at[k - 1]) for k in range(1, 4)], sems)


def others(ix, rows, after):
    shape = (3,) + rows.shape[1:]
    return call(
        others_kernel, "others", ix, (1,), [rows], [ANY], shaped(shape),
        pl.BlockSpec(shape, lambda i, m: (0, 0, 0)), [pltpu.SemaphoreType.DMA((3,))], after=after,
    )


def tables_kernel(ix, freq_ref, cos_ref, sin_ref):
    rows = cos_ref.shape[0]
    lane = lax.broadcasted_iota(jnp.int32, (1, 128), 1)
    place = pl.program_id(0) * rows + lax.broadcasted_iota(jnp.int32, (rows, 128), 0)
    angle = place.astype(F32) * freq_ref[0:1, :]
    cos_ref[...] = jnp.cos(angle)
    sin_ref[...] = jnp.where((lane % HEAD_DIM) < HEAD_DIM // 2, -1.0, 1.0) * jnp.sin(angle)


def all_rope_tables(ix, count, after):
    step = 768
    return call(
        tables_kernel, "rope_tables", ix, (count // step,), [rope_freq().reshape(1, 128)],
        [pl.BlockSpec((1, 128), lambda i, m: (0, 0))], [shaped((count, 128), F32)] * 2,
        [pl.BlockSpec((step, 128), lambda i, m: (i, 0))] * 2, after=after,
    )


def hidden_back_kernel(ix, cot_ref, w_ref, out_ref):
    out_ref[...] = against(cot_ref[...], w_ref[...])


def far_rows(array, rows):
    return (lambda m: (m[ME] % 2) ^ 1) if array.shape[0] > rows else (lambda m: 0)


def hidden_back(ix, cotangent, rows, w_down, after=()):
    width = cotangent.shape[1]
    units = w_down.shape[0] // 2
    step = 512
    block = far_rows(cotangent, rows)
    return call(
        hidden_back_kernel, "hidden_back", ix, (units // step,), [cotangent, w_down],
        [
            pl.BlockSpec((rows, width), lambda i, m: (block(m), 0)),
            pl.BlockSpec((step, width), lambda i, m: ((m[ME] % 2) * (units // step) + i, 0)),
        ],
        shaped((rows, units), F32), pl.BlockSpec((rows, step), lambda i, m: (0, i)), after=after,
    )


def feed_kernel(ix, *refs, count):
    pieces = refs[:count]
    wg_ref, wu_ref, hb_ref, wg_rows, wu_rows, rows_ref, hid_ref, gb_ref, ub_ref, keep_ref, send_ref = refs[count:-4]
    held, gate_back, up_back, sems = refs[-4:]
    t = ix[T]
    here = pl.program_id(0)
    rows, units = gate_back.shape
    step = wg_ref.shape[1]
    forward = units // step
    quarter = rows // 4

    @pl.when(here == 0)
    def _():
        if count == 1:
            copy_all([(pieces[0].at[pl.ds((1 - ix[ME] % 2) * rows, rows)], held)], sems)
        else:
            copy_all(quarter_copies(t, pieces, held), sems)
        pltpu.make_async_copy(held, rows_ref, sems.at[4]).start()

    @pl.when(here < forward)
    def _():
        second = held[...]
        gate = dot(second, wg_ref[...])
        up = dot(second, wu_ref[...])
        back = hb_ref[...]
        sig = 0.5 + 0.5 * jnp.tanh(0.5 * gate)
        swish = gate * sig
        hid_ref[...] = (swish * up).astype(LOW)
        gate_low = (back * up * (sig + swish * (1.0 - sig))).astype(LOW)
        up_low = (back * swish).astype(LOW)
        gb_ref[...] = gate_low
        ub_ref[...] = up_low
        columns = pl.ds(pl.multiple_of(here * step, step), step)
        for k in range(4):
            slot = k ^ t
            place = pl.ds(pl.multiple_of(((slot & 1) * 2 + (slot >> 1)) * quarter, quarter), quarter)
            gate_back[place, columns] = gate_low[k * quarter : (k + 1) * quarter]
            up_back[place, columns] = up_low[k * quarter : (k + 1) * quarter]

    @pl.when(here >= forward)
    def _():
        total = against(gate_back[...], wg_rows[...]) + against(up_back[...], wu_rows[...])
        store_quarters(total, keep_ref, send_ref)

    @pl.when(here == pl.num_programs(0) - 1)
    def _():
        pltpu.make_async_copy(held, rows_ref, sems.at[4]).wait()


def feed(ix, pieces, w_gate, w_up, back, after=()):
    rows, width = back.shape[0], pieces[0].shape[1]
    units = w_gate.shape[1] // 2
    step, wide = 256, 512
    forward = units // step
    first = lambda i: jnp.minimum(i, forward - 1)
    then = lambda i: jnp.maximum(i - forward, 0)
    weight = pl.BlockSpec((width, step), lambda i, m: (0, (m[ME] % 2) * forward + first(i)))
    weight_rows = pl.BlockSpec((wide, units), lambda i, m: (then(i), m[ME] % 2))
    block = pl.BlockSpec((rows, step), lambda i, m: (0, first(i)))
    return call(
        functools.partial(feed_kernel, count=len(pieces)), "feed", ix, (forward + width // wide,),
        [*pieces, w_gate, w_up, back, w_gate, w_up],
        [ANY] * len(pieces) + [weight] * 2 + [block] + [weight_rows] * 2,
        [shaped((rows, width))] + [shaped((rows, units))] * 3 + [shaped((2, rows // 4, width))] * 2,
        [ANY, block, block, block] + [pl.BlockSpec((2, rows // 4, wide), lambda i, m: (0, 0, then(i)))] * 2,
        [
            pltpu.VMEM((rows, width), LOW),
            pltpu.VMEM((rows, units), LOW),
            pltpu.VMEM((rows, units), LOW),
            pltpu.SemaphoreType.DMA((5,)),
        ],
        after=after,
    )


def branch_back_kernel(ix, q0, q1, q2, q3, w0, w1, w2, w3, rows_ref, o0, o1, o2, o3, held, sems):
    copy_all(quarter_copies(ix[T], (q0, q1, q2, q3), held), sems)
    keep = pltpu.make_async_copy(held, rows_ref, sems.at[4])
    keep.start()
    weight = jnp.concatenate([w0[...], w1[...], w2[...], w3[...]], axis=0)
    for part in range(3):
        at = slice(part * 256, (part + 1) * 256)
        flat = against(held[at, :], weight).astype(LOW)
        for slot, out in enumerate((o0, o1, o2, o3)):
            out[at, :] = flat[:, slot * 128 : (slot + 1) * 128]
    keep.wait()


def branch_back(ix, pieces, w_out, after):
    rows, width = pieces[0].shape
    rows = 4 * rows

    def heads(slot):
        return pl.BlockSpec((128, width), lambda i, m: (m[ME] ^ slot, 0))

    return call(
        branch_back_kernel, "branch_back", ix, (1,), [*pieces] + [w_out] * 4,
        [ANY] * 4 + [heads(slot) for slot in range(4)],
        [shaped((rows, width))] + [shaped((rows, 128))] * 4,
        [ANY] + [pl.BlockSpec((rows, 128), lambda i, m: (0, 0))] * 4,
        [pltpu.VMEM((rows, width), LOW), pltpu.SemaphoreType.DMA((5,))], after=after,
    )


def wgrad_kernel(ix, l0, l1, r0, r1, out_ref):
    out_ref[0] = (across(l0[...], r0[...]) + across(l1[...], r1[...])).astype(LOW)


def wgrad_kernel(ix, l0, l1, r0, r1, out_ref):
    out_ref[0] = (across(l0[...], r0[...]) + across(l1[...], r1[...])).astype(LOW)


def wgrad(ix, wide, free, name, after=()):
    rows, units = free[0].shape
    share = 256

    def wide_spec(array):
        block = far_rows(array, rows)
        return pl.BlockSpec((rows, share), lambda i, m: (block(m), i ^ (m[ME] % 2)))

    return call(
        wgrad_kernel, name, ix, (8,), [*wide, *free],
        [wide_spec(array) for array in wide] + [pl.BlockSpec((rows, units), lambda i, m: (0, 0))] * 2,
        shaped((8, share, units)), pl.BlockSpec((1, share, units), lambda i, m: (i, 0, 0)), after=after,
    )


def add_blocks_kernel(ix, a_ref, b_ref, *refs):
    total = (a_ref[...].astype(F32) + b_ref[...].astype(F32)).astype(LOW)
    size = refs[0].shape[0]
    for k, ref in enumerate(refs):
        ref[...] = total[k * size : (k + 1) * size]


def add_blocks(ix, one, two, parts, after=()):
    shape = (one.shape[0] // parts,) + one.shape[1:]
    whole = pl.BlockSpec(one.shape, lambda i, m: (0, 0, 0))
    return call(
        add_blocks_kernel, "add_blocks", ix, (1,), [one, two], [whole] * 2,
        [shaped(shape)] * parts, [pl.BlockSpec(shape, lambda i, m: (0, 0, 0))] * parts, after=after,
    )


def one_block_kernel(ix, in_ref, out_ref):
    out_ref[...] = in_ref[...]


def one_block(ix, blocks, which, after=()):
    shape = (1,) + blocks.shape[1:]
    return call(
        one_block_kernel, "one_block", ix, (1,), [blocks],
        [pl.BlockSpec(shape, lambda i, m: (which, 0, 0))], shaped(shape),
        pl.BlockSpec(shape, lambda i, m: (0, 0, 0)), after=after,
    )


def halves_kernel(ix, own_ref, other_ref, out_ref, *, axis):
    which = ix[ME] % 2
    for place, ref in ((which, own_ref), (1 - which, other_ref)):
        value = ref[...].astype(F32)
        if axis == 0:
            value = value.T
        size = value.shape[axis]
        at = pl.ds(pl.multiple_of(place * size, size), size)
        if axis == 0:
            out_ref[at, :] = value
        else:
            out_ref[:, at] = value


def halves(ix, blocks, other, axis, after=()):
    share, units = blocks.shape[1:]
    shape = (2 * units, share) if axis == 0 else (share, 2 * units)
    whole = lambda i, m: (0, 0)
    return call(
        functools.partial(halves_kernel, axis=axis), "halves", ix, (1,), [blocks, other],
        [pl.BlockSpec((None, share, units), lambda i, m: (0, 0, 0))] * 2,
        shaped(shape, F32), pl.BlockSpec(shape, whole), after=after,
    )


def out_wgrad_kernel(ix, a0, a1, a2, a3, rows_ref, own_ref, far_ref, held):
    for slot, ref in enumerate((a0, a1, a2, a3)):
        at = pl.ds(pl.multiple_of((slot ^ ix[ME]) * 128, 128), 128)
        held[at, :] = across(ref[...], rows_ref[...]).astype(LOW)
    for half, out in enumerate((own_ref, far_ref)):

        @pl.when(pl.program_id(0) // 4 == half)
        def _():
            out[0] = held[...]


def out_wgrad(ix, mixed, rows, after=()):
    count, width = rows.shape
    share = 256
    return call(
        out_wgrad_kernel, "out_wgrad", ix, (width // share,), [*mixed, rows],
        [pl.BlockSpec((count, 128), lambda i, m: (0, 0))] * 4
        + [pl.BlockSpec((count, share), lambda i, m: (0, i ^ (m[DP] * 4 + m[ME])))],
        [shaped((4, 512, share))] * 2,
        [
            pl.BlockSpec((1, 512, share), lambda i, m: (jnp.minimum(i, 3), 0, 0)),
            pl.BlockSpec((1, 512, share), lambda i, m: (jnp.maximum(i - 4, 0), 0, 0)),
        ],
        [pltpu.VMEM((512, share), LOW)], after=after,
    )


def project_wgrad_kernel(ix, first_ref, f0, f1, f2, f3, b0, b1, b2, b3, own_ref, far_ref, held, total, sems):
    me, t = ix[ME], ix[T]
    turn = pl.program_id(0)
    quarter = f0.shape[1]

    def copies(slot):
        if slot == 0:
            return [pltpu.make_async_copy(first_ref, held.at[0], sems.at[0, 0])]
        return [
            pltpu.make_async_copy(
                ref.at[slot - 1], held.at[slot, pl.ds((t ^ k) * quarter, quarter)], sems.at[slot, k]
            )
            for k, ref in enumerate((f0, f1, f2, f3))
        ]

    @pl.when(turn == 0)
    def _():
        for slot in range(4):
            for copy in copies(slot):
                copy.start()

    for slot, back in enumerate((b0, b1, b2, b3)):

        @pl.when(turn == slot)
        def _():
            for copy in copies(slot):
                copy.wait()
            for block in range(8):
                at = slice(block * 256, (block + 1) * 256)
                part = across(held[slot, :, at], back[...])
                if slot == 0:
                    total[at, :] = part
                elif slot < 3:
                    total[at, :] += part
                else:
                    done = (total[at, :] + part).astype(LOW)

                    @pl.when(ix[DP] == block // 4)
                    def _():
                        own_ref[(block % 4) ^ me] = done

                    @pl.when(ix[DP] != block // 4)
                    def _():
                        far_ref[(block % 4) ^ me] = done


def project_wgrad(ix, first_in, far, back, after=()):
    rows, width = first_in.shape
    whole = lambda i, m: (0, 0)
    return call(
        project_wgrad_kernel, "project_wgrad", ix, (4,), [first_in, *far, *back],
        [ANY] * 5 + [pl.BlockSpec((rows, 384), whole)] * 4,
        [shaped((4, 256, 384))] * 2, [pl.BlockSpec((4, 256, 384), lambda i, m: (0, 0, 0))] * 2,
        [
            pltpu.VMEM((4, rows, width), LOW),
            pltpu.VMEM((width, 384), F32),
            pltpu.SemaphoreType.DMA((4, 4)),
        ],
        after=after,
    )


def add_parts_kernel(ix, a_ref, b_ref, gain_ref, *refs):
    rows = a_ref.shape[1]
    for k, out in enumerate(refs):
        out[0:rows, :] = (a_ref[k].astype(F32) + b_ref[k].astype(F32)).astype(LOW)
        gains = jnp.concatenate([gain_ref[k], jnp.zeros((14, gain_ref.shape[2]), F32)], axis=0)
        out[rows : rows + 16, 0 : gains.shape[1]] = gains.astype(LOW)
        out[rows : rows + 16, gains.shape[1] :] = jnp.zeros((16, out.shape[1] - gains.shape[1]), LOW)


def add_parts(ix, one, two, gains, after=()):
    count, rows, width = one.shape
    whole = lambda shape: pl.BlockSpec(shape, lambda i, m: (0,) * len(shape))
    shape = (rows + 16, width)
    return call(
        add_parts_kernel, "add_blocks", ix, (1,), [one, two, gains], [whole(a.shape) for a in (one, two, gains)],
        [shaped(shape)] * count, [whole(shape)] * count, after=after,
    )


def add_last_kernel(ix, a_ref, b_ref, out_ref):
    out_ref[...] = a_ref[...].astype(F32) + b_ref[...].astype(F32)


def add_last(ix, one, two, after):
    shape = one.shape[1:]
    block = pl.BlockSpec((None, *shape), lambda i, m: (0, 0, 0))
    return call(
        add_last_kernel, "add_last", ix, (1,), [one, two], [block] * 2, shaped(shape, F32),
        pl.BlockSpec(shape, lambda i, m: (0, 0)), after=after,
    )


def project_last_kernel(ix, p0, p1, p2, p3, q_ref, k_ref, v_ref, *gain_refs):
    share = q_ref.shape[0]
    for slot, ref in enumerate((p0, p1, p2, p3)):
        at = pl.ds(pl.multiple_of((slot ^ ix[ME]) * 128, 128), 128)
        for place, out in enumerate((q_ref, k_ref, v_ref)):
            out[:, at] = ref[0:share, place * 128 : (place + 1) * 128].astype(F32)
    for out in gain_refs:
        out[...] = sum(ref[share : share + 16, 0 : out.shape[1]].astype(F32) for ref in (p0, p1, p2, p3))


def project_last(ix, pieces, share, after=()):
    whole = lambda i, m: (0, 0)
    shapes = [(share, 512)] * 3 + ([(16, share)] if pieces[0].shape[0] > share else [])
    return call(
        project_last_kernel, "project_last", ix, (1,), list(pieces), [pl.BlockSpec(pieces[0].shape, whole)] * 4,
        [shaped(shape, F32) for shape in shapes], [pl.BlockSpec(shape, whole) for shape in shapes], after=after,
    )


def over_ctx(slots):
    return [slots[0]] + [swap(slots[k], CTX, k) for k in range(1, 4)]


def per_device(
    dp_size, tokens, attn_gain, w_query, w_key, w_value, w_out, mlp_gain, w_gate, w_up, w_down, cotangent
):
    rows_here, width = tokens.shape
    share = width // (4 * dp_size)
    me, t, d = lax.axis_index(CTX), lax.axis_index(TENSOR), lax.axis_index("dp")
    two_dp = dp_size == 2
    ix = jnp.stack([me, t, d if two_dp else jnp.zeros_like(d)]).astype(jnp.int32)
    order = me ^ jnp.arange(4)
    projections = (w_query, w_key, w_value)
    attn_gain, mlp_gain = attn_gain.reshape(1, -1), mlp_gain.reshape(1, -1)

    cot_mine = lax.dynamic_slice_in_dim(cotangent, t * (rows_here // 4), rows_here // 4, 0)
    tables = rope_tables(me * rows_here + jnp.arange(rows_here, dtype=jnp.int32))
    first_in, *slots = project(ix, tokens, attn_gain, tables, projections)
    pieces = over_ctx(slots)

    back_own = hidden_back(ix, cotangent, rows_here, w_down, (slots[0],))
    all_tables = all_rope_tables(ix, 4 * rows_here, (back_own,))
    (first_mine,) = mine(ix, [first_in], (all_tables[0],))
    cot_mine = tie(ix, cot_mine, (*pieces[1:], first_mine))
    cot_both = lax.all_gather(cot_mine, ("lo", *TENSOR), axis=0, tiled=True)

    *mixed_slots, raw, lse = attend(ix, pieces, (first_mine,))
    mixed = over_ctx(mixed_slots)
    keep, send = join_heads(ix, mixed, w_out, (cot_both,))
    core = swap(send, TENSOR, 1)
    low = sums_to_send(ix, [(keep, 1), (core, 1)])
    middle, second_mine = rows_call(
        middle_kernel, "middle", ix, [(keep, 0), (core, 0), swap(low, TENSOR, 2)], [tokens, mlp_gain], [F32, LOW]
    )

    second_both = lax.all_gather(second_mine, ("lo", *TENSOR), axis=0, tiled=True)
    back_far = hidden_back(ix, cot_both, rows_here, w_down, (second_mine,))
    own_pieces = spread(second_mine, lambda two: tie(ix, two, (back_far,)))
    second_own, hid_own, gb_own, ub_own, keep_own, send = feed(ix, own_pieces, w_gate, w_up, back_own)
    first_all = lax.all_gather(tie(ix, first_mine, (hid_own,)), CTX, axis=0, tiled=False)
    core_own = swap(send, TENSOR, 1)
    second_far, hid_far, gb_far, ub_far, keep, send = feed(ix, [second_both], w_gate, w_up, back_far, (hid_own,))

    seconds = (second_own, second_far)

    def over_pairs(part):
        return lax.psum_scatter(part, ("dp", "hi"), scatter_dimension=0, tiled=True) if two_dp else part

    core = swap(send, TENSOR, 1)
    part_down = wgrad(ix, (cotangent, cot_both), (hid_own, hid_far), "wgrad_down")
    low = sums_to_send(ix, [(keep, 1), (core, 1)])
    far_y = swap(low, TENSOR, 2)
    down_far = feed_down(ix, hid_far, w_down, (low,))
    low = sums_to_send(ix, [(keep, 0), (core, 0), far_y], (down_far[0],))
    far_z = swap(low, CTX, 1)
    sum_down = over_pairs(tie(ix, part_down, (far_z,)))
    low = sums_to_send(ix, [(keep_own, 1), (core_own, 1)], (low,))
    own_sums = [(keep_own, 0), (core_own, 0), swap(low, TENSOR, 2)]
    core_far = swap(down_far[1], TENSOR, 1)
    down_own = feed_down(ix, hid_own, w_down, (low,))
    low = sums_to_send(ix, [(down_far[0], 1), (core_far, 1)], (down_own[0],))
    far_down = [(down_far[0], 0), (core_far, 0), swap(low, TENSOR, 2)]
    middle_grad, branch_mine, mlp_gain_part = rows_call(
        middle_back_kernel, "middle_back", ix, [*own_sums, far_z, middle], [cotangent, mlp_gain], [F32, LOW], 1,
        (low,),
    )
    core_own = swap(down_own[1], TENSOR, 1)
    low = sums_to_send(ix, [(down_own[0], 1), (core_own, 1)], (branch_mine,))
    own_y = swap(low, TENSOR, 2)
    branch_low, *slots = branch_back(ix, spread(branch_mine), w_out, (low,))
    upstreams = over_ctx(slots)
    first_far = others(ix, first_all, (branch_low,))
    out_own, out_far = out_wgrad(ix, mixed, branch_low, (first_far,))
    part_gate = wgrad(ix, seconds, (gb_own, gb_far), "wgrad_gate", (out_own, own_y))
    sum_gate = over_pairs(tie(ix, part_gate, upstreams[1:]))

    def for_partner(blocks, after):
        return swap(blocks[1:] if after is None else one_block(ix, blocks, 1, after), CTX, 1)

    token, arrived = own_y, []
    if two_dp:
        out_other = swap(out_far, "dp", 1)
        token = one_block(ix, sum_down, 1, (out_own, *upstreams[1:]))
        down_other = swap(token, CTX, 1)
        arrived = [out_other, down_other]
    back_slots = attend_back(ix, pieces, upstreams, raw, lse, all_tables, (token, out_own, own_y))
    back = over_ctx(back_slots)

    arrived = (back_slots[0], *arrived)
    first_spread = spread(first_far, lambda two: tie(ix, two, arrived))
    qkv_own, qkv_far = project_wgrad(ix, first_in, first_spread, back_slots)
    far_low = sums_to_send(ix, far_down, (qkv_own,))
    token = far_low
    if two_dp:
        qkv_other = swap(qkv_far, "dp", 1)
        out_part = add_blocks(ix, out_own, out_other, 2, (far_low,))
        down_grad = halves(ix, sum_down, down_other, 0, (out_part[0],))
        token = down_grad
    part_up = wgrad(ix, seconds, (ub_own, ub_far), "wgrad_up", (token,))
    part_up = tie(ix, part_up, back[1:])
    sum_up = over_pairs(part_up)
    keep, send = project_back(ix, back, projections, (part_up,))
    core = swap(send, TENSOR, 1)
    low = sums_to_send(ix, [(keep, 1), (core, 1)])
    low_y = swap(low, TENSOR, 2)
    far_z = swap(tie(ix, far_low, (low,)), CTX, 1)
    token = low
    if two_dp:
        gate_low = one_block(ix, sum_gate, 1, (low,))
        gate_other = swap(gate_low, CTX, 1)
        token = gate_low
    input_mine = input_back(ix, keep, core, low_y, middle_grad, tokens, attn_gain, mlp_gain_part, (token,))
    arrived = (far_z,)
    if two_dp:
        out_z = swap(tie(ix, out_part[1], (keep,)), CTX, 2)
        arrived = (far_z, qkv_other, out_z)
    input_grad, gains = join_input(ix, spread(input_mine, lambda two: tie(ix, two, arrived)), (input_mine,))
    gains = gains[:2]
    if two_dp:
        halved = gains.reshape(2, 2, width // 2)[:, d ^ jnp.arange(2)]
        gains = halved[:, 0] + swap(halved[:, 1], "dp", 1)
        gains = gains.reshape(2, 4, share).transpose(1, 0, 2)[order]
    (output_mine,) = rows_call(
        output_kernel, "output", ix, [(down_own[0], 0), (core_own, 0), own_y, far_z, middle], [], [LOW],
        after=(input_grad,),
    )
    output = lax.all_gather(output_mine, TENSOR, axis=0, tiled=True)
    if two_dp:
        up_low = one_block(ix, sum_up, 1, (output_mine,))
        up_other = swap(up_low, CTX, 1)
        out_part = add_blocks(ix, out_part[0], out_z, 2, (up_low,))
        out_other = swap(out_part[1], CTX, 1)
        qkv_parts = over_ctx(add_parts(ix, qkv_own, qkv_other, gains, (out_part[0],)))
        gate_grad = halves(ix, sum_gate, gate_other, 1, (qkv_parts[0],))
        up_grad = halves(ix, sum_up, up_other, 1, (gate_grad,))
        *qkv, gains = project_last(ix, qkv_parts, share, (up_grad,))
        out_grad = add_last(ix, out_part[0], out_other, (qkv[0],))
    else:
        def scattered(blocks, axis):
            blocks = jnp.moveaxis(blocks, 0, axis)
            shape = blocks.shape[:axis] + (width,) + blocks.shape[axis + 2 :]
            part = lax.psum_scatter(blocks.reshape(shape), "dp", scatter_dimension=axis, tiled=True)
            shape = part.shape[:axis] + (4, share) + part.shape[axis + 1 :]
            return jnp.moveaxis(part.reshape(shape), axis, 0)

        def in_order(blocks):
            return blocks.reshape(2, 4, *blocks.shape[1:])[:, order].reshape(blocks.shape)

        grads = []
        own_first = me % 2 ^ jnp.arange(2)
        for k, blocks in enumerate((sum_down, sum_gate, sum_up)):
            blocks = blocks.reshape(4, 2, *blocks.shape[1:])[:, own_first].reshape(blocks.shape)
            part = scattered(blocks, 0)[order].astype(F32)
            part = (part[:2] + swap(part[2:].astype(LOW), CTX, 2).astype(F32)).astype(LOW)
            grads.append(halves(ix, part, for_partner(part, None), min(k, 1)))
        down_grad, gate_grad, up_grad = grads
        qkv_parts = over_ctx(scattered(in_order(jnp.concatenate([qkv_own, qkv_far])), 0)[order])
        out_part = scattered(in_order(jnp.concatenate([out_own, out_far])), 1)[order]
        out_part = out_part[:2].astype(F32) + swap(out_part[2:], CTX, 2).astype(F32)
        out_grad = out_part[0] + swap(out_part[1].astype(LOW), CTX, 1).astype(F32)
        qkv = project_last(ix, qkv_parts, share)
        gains = lax.psum_scatter(gains, "dp", scatter_dimension=1, tiled=True)
        gains = sum(over_ctx(gains.reshape(2, 4, share).transpose(1, 0, 2)[order]))

    return (
        output,
        input_grad,
        gains[0],
        qkv[0],
        qkv[1],
        qkv[2],
        out_grad,
        gains[1],
        gate_grad,
        up_grad,
        down_grad,
    )


def solution(mesh):
    dp_size = mesh.shape["dp"]
    mesh = jax.sharding.Mesh(mesh.devices.reshape(dp_size, 2, 2, 2, 2), ("dp", *CTX, *TENSOR))
    rows, tensor = ("dp", *CTX), TENSOR
    columns = P(None, tensor)
    in_specs = (
        P(rows, None), P(), columns, columns, columns, P(tensor, None),
        P(), columns, columns, P(tensor, None), P(rows, None),
    )
    out_specs = (
        P(rows, None), P(rows, None), P(rows), P(rows, tensor), P(rows, tensor), P(rows, tensor),
        P(tensor, rows), P(rows), P(rows, tensor), P(rows, tensor), P(tensor, rows),
    )
    return jax.shard_map(
        functools.partial(per_device, dp_size),
        mesh=mesh,
        in_specs=in_specs,
        out_specs=out_specs,
        check_vma=False,
    )
```

```python
import functools

import jax
import jax.numpy as jnp
from jax import lax
from jax.experimental import pallas as pl
from jax.experimental.pallas import tpu as pltpu
from jax.sharding import PartitionSpec as P

HEAD_DIM = 64
EPS = 1e-05
THETA = 130000.0
MIB = 1 << 20
MOST = 64
COSTS = {
    "project": 11, "hidden_back": 8.5, "rope_tables": 8, "attend": 28, "quarter": 3,
    "join_heads": 6.5, "sums": 3, "join": 3.5, "middle": 4, "feed": 24, "wgrad_down": 14, "wgrad_gate": 14, "wgrad_up": 14,
    "middle_back": 5, "branch_back": 7, "others": 4, "feed_down": 9, "attend_back": 40, "project_wgrad": 13,
    "out_wgrad": 8.5, "add_pairs": 4, "project_back": 11, "input_back": 5, "output": 4, "halves": 3.5,
    "project_last": 3, "add_blocks": 3, "one_block": 2,
}
SCALE = 2
LOW = jnp.bfloat16
F32 = jnp.float32
ANY = pl.BlockSpec(memory_space=pl.ANY)


CTX, TENSOR = ("hi", "lo"), ("y", "core")


def swap(value, axis, distance):
    size = 2 if axis == "dp" else 4
    return lax.ppermute(value, axis, [(i, i ^ distance) for i in range(size)])


def dot(left, right):
    return jnp.dot(left, right, preferred_element_type=F32)


def against(left, right):
    return lax.dot_general(left, right, (((1,), (1,)), ((), ())), preferred_element_type=F32)


def across(left, right):
    return lax.dot_general(left, right, (((0,), (0,)), ((), ())), preferred_element_type=F32)


def shaped(shape, dtype=LOW):
    return jax.ShapeDtypeStruct(shape, dtype)


def call(kernel, name, index, grid, inputs, in_specs, outs, out_specs, scratch=(), mib=MOST, after=()):
    count = len(inputs)

    def body(index_ref, *refs):
        kernel(index_ref, *refs[:count], *refs[count + len(after) :])

    return pl.pallas_call(
        body,
        grid_spec=pltpu.PrefetchScalarGridSpec(
            num_scalar_prefetch=1,
            grid=grid,
            in_specs=list(in_specs) + [ANY] * len(after),
            out_specs=out_specs,
            scratch_shapes=list(scratch),
        ),
        out_shape=outs,
        compiler_params=pltpu.CompilerParams(
            vmem_limit_bytes=mib * MIB, dimension_semantics=("arbitrary",) * len(grid)
        ),
        cost_estimate=pl.CostEstimate(flops=0, bytes_accessed=int(COSTS.get(name, 0) * SCALE * 3.5 * MIB), transcendentals=0),
        name=name,
    )(index, *inputs, *after)


ME, T, DP = 0, 1, 2


def copy_all(pairs, sems):
    copies = [pltpu.make_async_copy(a, b, sems.at[k]) for k, (a, b) in enumerate(pairs)]
    for copy in copies:
        copy.start()
    for copy in copies:
        copy.wait()


def half_turn(rows):
    lane = lax.broadcasted_iota(jnp.int32, (1, 128), 1)
    first = (lane % HEAD_DIM) < HEAD_DIM // 2
    return jnp.where(first, pltpu.roll(rows, 96, 1), pltpu.roll(rows, 32, 1))


def rope_freq():
    half = HEAD_DIM // 2
    freq = jnp.power(THETA, -jnp.arange(half, dtype=F32) * (2.0 / HEAD_DIM))
    return jnp.concatenate([freq] * 4)


def rope_tables(positions):
    angle = rope_freq()[: HEAD_DIM // 2, None] * positions.astype(F32)[None, :]
    return jnp.cos(angle), jnp.sin(angle)


def project_kernel(ix, tok_ref, gain_ref, cos_ref, sin_ref, wq_ref, wk_ref, wv_ref, first_ref, o0, o1, o2, o3, held):
    me = ix[ME]
    rows = tok_ref[...].astype(F32)
    inverse = lax.rsqrt(jnp.mean(rows * rows, axis=-1, keepdims=True) + EPS)
    first = (rows * inverse * gain_ref[...]).astype(LOW)
    first_ref[...] = first
    half_cos, half_sin = cos_ref[...].T, sin_ref[...].T
    cosine = jnp.concatenate([half_cos] * 4, axis=1)
    sine = jnp.concatenate([-half_sin, half_sin] * 2, axis=1)
    for place, weight in enumerate((wq_ref, wk_ref, wv_ref)):
        flat = dot(first, weight[...])
        for group in range(4):
            part = flat[:, group * 128 : (group + 1) * 128]
            if place < 2:
                part = part * cosine + half_turn(part) * sine
            if place == 0:
                part = part * HEAD_DIM**-0.5
            held[group, :, place * 128 : (place + 1) * 128] = part.astype(LOW)
    for slot, out in enumerate((o0, o1, o2, o3)):
        out[...] = held[slot ^ me]


def project(ix, tokens, gain, tables, weights):
    rows, width = tokens.shape
    local = weights[0].shape[1]
    step = 256
    whole = lambda i, m: (0, 0)
    along = lambda i, m: (i, 0)
    return call(
        project_kernel, "project", ix, (rows // step,),
        [tokens, gain, *tables, *weights],
        [pl.BlockSpec((step, width), along), pl.BlockSpec((1, width), whole)]
        + [pl.BlockSpec((HEAD_DIM // 2, step), lambda i, m: (0, i))] * 2 + [pl.BlockSpec((width, local), whole)] * 3,
        [shaped((rows, width))] + [shaped((rows, 384))] * 4,
        [pl.BlockSpec((step, width), along)] + [pl.BlockSpec((step, 384), along)] * 4,
        [pltpu.VMEM((4, step, 384), LOW)],
    )


def own_lanes(rows, head):
    lane = lax.broadcasted_iota(jnp.int32, (1, 128), 1)
    inside = (lane < HEAD_DIM) if head == 0 else (lane >= HEAD_DIM)
    return jnp.where(inside, rows, jnp.zeros_like(rows))


def attend_kernel(ix, r0, r1, r2, r3, o0, o1, o2, o3, raw_ref, lse_ref, held, sems):
    me = ix[ME]
    turn = pl.program_id(0)
    here = turn ^ me
    stretch = r0.shape[0]
    half = stretch // 2
    lane = lax.broadcasted_iota(jnp.int32, (1, 128), 1)

    @pl.when(turn == 0)
    def _():
        copy_all(
            [(ref, held.at[pl.ds((me ^ k) * stretch, stretch)]) for k, ref in enumerate((r0, r1, r2, r3))], sems
        )

    query = held[pl.ds(here * stretch, stretch), 0:128]
    queries = [own_lanes(query, head) for head in range(2)]

    def step(queries, rows, carry, offset):
        keys, values = held[rows, 128:256], held[rows, 256:384]
        out = []
        for head in range(2):
            peak, mass, total = carry[3 * head : 3 * head + 3]
            scores = against(queries[head], keys)
            if offset is not None:
                down = lax.broadcasted_iota(jnp.int32, scores.shape, 0) + offset
                along = lax.broadcasted_iota(jnp.int32, scores.shape, 1)
                scores = jnp.where(down >= along, scores, -1e30)
            top = jnp.maximum(peak, jnp.max(scores, axis=-1, keepdims=True))
            weights = jnp.exp(scores - top)
            fade = jnp.exp(peak - top)
            mass = mass * fade + jnp.sum(weights, axis=-1, keepdims=True)
            out += [top, mass, total * fade + dot(weights.astype(LOW), values)]
        return tuple(out)

    start = (
        jnp.full((stretch, 1), -1e30, F32),
        jnp.zeros((stretch, 1), F32),
        jnp.zeros((stretch, 128), F32),
    ) * 2
    carry = lax.fori_loop(0, here, lambda at, c: step(queries, pl.ds(at * stretch, stretch), c, None), start)
    for part in range(2):
        at = slice(part * half, (part + 1) * half)
        rows = pl.ds(here * stretch, (part + 1) * half)
        done = step([query[at] for query in queries], rows, [c[at] for c in carry], part * half)
        peak0, mass0, total0, peak1, mass1, total1 = done
        mixed = jnp.where(lane < HEAD_DIM, total0 / mass0, total1 / mass1)
        raw_ref[at, :] = mixed
        for slot, out in enumerate((o0, o1, o2, o3)):

            @pl.when(turn == slot)
            def _():
                out[at, :] = mixed.astype(LOW)

        turned = jnp.where(lane < HEAD_DIM, peak0 + jnp.log(mass0), peak1 + jnp.log(mass1)).T
        lse_ref[0, 0:8, at] = turned[0:8]
        lse_ref[0, 8:16, at] = turned[64:72]


def attend(ix, pieces, after):
    stretch = pieces[0].shape[0]
    length = 4 * stretch
    return call(
        attend_kernel, "attend", ix, (4,), list(pieces), [ANY] * 4,
        [shaped((stretch, 128))] * 4 + [shaped((length, 128), F32), shaped((4, 16, stretch), F32)],
        [pl.BlockSpec((stretch, 128), lambda i, m: (0, 0))] * 4
        + [
            pl.BlockSpec((stretch, 128), lambda i, m: (i ^ m[ME], 0)),
            pl.BlockSpec((1, 16, stretch), lambda i, m: (i ^ m[ME], 0, 0)),
        ],
        [pltpu.VMEM((length, 384), LOW), pltpu.SemaphoreType.DMA((4,))], after=after,
    )


def attend_back_kernel(
    ix, p0, p1, p2, p3, u0, u1, u2, u3, raw_ref, lse_ref, cos_ref, sin_ref, o0, o1, o2, o3,
    held, up, query_at, up_at, delta, query_sum, key_sum, value_sum, sems,
):
    me = ix[ME]
    turn = pl.program_id(0)
    count = pl.num_programs(0)
    stretch = p0.shape[0]
    half = stretch // 2
    here = turn ^ me

    @pl.when(turn == 0)
    def _():
        rows = [pl.ds((me ^ k) * stretch, stretch) for k in range(4)]
        copy_all(
            [(ref, held.at[rows[k]]) for k, ref in enumerate((p0, p1, p2, p3))]
            + [(ref, up.at[rows[k]]) for k, ref in enumerate((u0, u1, u2, u3))],
            sems,
        )
        query_sum[...] = jnp.zeros_like(query_sum)

        def prepare(at, _):
            rows = pl.ds(at * stretch, stretch)
            query, upstream = held[rows, 0:128], up[rows, :]
            turned = (upstream.astype(F32) * raw_ref[rows, :]).T
            for head in range(2):
                query_at[head, rows, :] = own_lanes(query, head)
                up_at[head, rows, :] = own_lanes(upstream, head)
                total = jnp.sum(turned[head * 64 : head * 64 + 64], axis=0, keepdims=True)
                delta[at, head * 8 : head * 8 + 8, :] = jnp.broadcast_to(total, (8, stretch))
            return 0

        lax.fori_loop(0, count, prepare, 0)

    here_rows = pl.ds(here * stretch, stretch)
    key, value = held[here_rows, 128:256], held[here_rows, 256:384]
    keys = [own_lanes(key, head) for head in range(2)]
    values = [own_lanes(value, head) for head in range(2)]
    keys_turned = [own.T for own in keys]

    def step(at, queries, kept, diagonal):
        size = queries.stop - queries.start
        rows = pl.ds(at * stretch + queries.start, size)
        query, upstream = held[rows, 0:128], up[rows, :]
        key_total = value_total = query_total = None
        for head in range(2):
            scores = against(keys[head][:kept], query)
            lse = lse_ref[at, head * 8 : head * 8 + 1, queries]
            chance = jnp.exp(scores - lse)
            if diagonal:
                down = lax.broadcasted_iota(jnp.int32, scores.shape, 0)
                along = lax.broadcasted_iota(jnp.int32, scores.shape, 1) + queries.start
                chance = jnp.where(along >= down, chance, 0.0)
            chance_back = against(values[head][:kept], upstream)
            shift = delta[at, head * 8 : head * 8 + 1, queries]
            score_back = (chance * (chance_back - shift)).astype(LOW)
            value_part = dot(chance.astype(LOW), up_at[head, rows, :])
            key_part = dot(score_back, query_at[head, rows, :])
            query_part = dot(keys_turned[head][:, :kept], score_back)
            if head == 0:
                value_total, key_total, query_total = value_part, key_part, query_part
            else:
                value_total += value_part
                key_total += key_part
                query_total += query_part
        columns = pl.ds(pl.multiple_of(at * stretch + queries.start, 128), size)
        query_sum[:, columns] += query_total
        return key_total, value_total

    key_sum[...], value_sum[...] = step(here, slice(half, stretch), stretch, True)
    key_total, value_total = step(here, slice(0, half), half, True)
    key_sum[:half] += key_total
    value_sum[:half] += value_total

    def later(at, _):
        key_total, value_total = step(at, slice(0, stretch), stretch, False)
        key_sum[...] += key_total
        value_sum[...] += value_total
        return 0

    lax.fori_loop(here + 1, count, later, 0)

    def back_rope(rows, at):
        places = pl.ds(at * stretch, stretch)
        return rows * cos_ref[places, :] - half_turn(rows) * sin_ref[places, :]

    key_low, value_low = back_rope(key_sum[...], here).astype(LOW), value_sum[...].astype(LOW)
    for slot, out in enumerate((o0, o1, o2, o3)):

        @pl.when(turn == slot)
        def _():
            out[:, 128:256] = key_low
            out[:, 256:384] = value_low

    @pl.when(turn == count - 1)
    def _():
        for slot, out in enumerate((o0, o1, o2, o3)):
            columns = pl.ds(pl.multiple_of((slot ^ me) * stretch, 128), stretch)
            rows = query_sum[:, columns].T * HEAD_DIM**-0.5
            out[:, 0:128] = back_rope(rows, slot ^ me).astype(LOW)


def attend_back(ix, pieces, upstreams, raw, lse, tables, after):
    stretch = pieces[0].shape[0]
    length = 4 * stretch
    whole = lambda i, m: (0, 0)
    return call(
        attend_back_kernel, "attend_back", ix, (4,), [*pieces, *upstreams, raw, lse, *tables],
        [ANY] * 8
        + [pl.BlockSpec((length, 128), whole), pl.BlockSpec((4, 16, stretch), lambda i, m: (0, 0, 0))]
        + [pl.BlockSpec((length, 128), whole)] * 2,
        [shaped((stretch, 384))] * 4,
        [pl.BlockSpec((stretch, 384), whole)] * 4,
        [
            pltpu.VMEM((length, 384), LOW),
            pltpu.VMEM((length, 128), LOW),
            pltpu.VMEM((2, length, 128), LOW),
            pltpu.VMEM((2, length, 128), LOW),
            pltpu.VMEM((4, 16, stretch), F32),
            pltpu.VMEM((128, length), F32),
            pltpu.VMEM((stretch, 128), F32),
            pltpu.VMEM((stretch, 128), F32),
            pltpu.SemaphoreType.DMA((8,)),
        ],
        after=after,
    )


def quarter_outs(rows, width, step):
    return (
        [shaped((2, rows // 4, width))] * 2,
        [pl.BlockSpec((2, rows // 4, step), lambda i, m: (0, 0, i))] * 2,
    )


def in_quarters(t, ref, held, columns=slice(None)):
    rows = ref.shape[0] // 4
    return [
        (ref.at[pl.ds((t ^ k) * rows, rows)], held.at[pl.ds(place * rows, rows), columns])
        for place, k in enumerate((0, 2, 1, 3))
    ]


def store_quarters(total, keep_ref, send_ref):
    rows = keep_ref.shape[1]
    for k in range(2):
        keep_ref[k] = total[k * rows : (k + 1) * rows].astype(LOW)
        send_ref[k] = total[(2 + k) * rows : (3 + k) * rows].astype(LOW)


def feed_down_kernel(ix, left_ref, right_ref, keep_ref, send_ref, held, sems):
    @pl.when(pl.program_id(0) == 0)
    def _():
        copy_all(in_quarters(ix[T], left_ref, held), sems)

    store_quarters(dot(held[...], right_ref[...]), keep_ref, send_ref)


def feed_down(ix, hidden, w_down, after=()):
    rows, units = hidden.shape
    width = w_down.shape[1]
    step = 512
    outs, out_specs = quarter_outs(rows, width, step)
    return call(
        feed_down_kernel, "feed_down", ix, (width // step,), [hidden, w_down],
        [ANY, pl.BlockSpec((units, step), lambda i, m: (m[ME] % 2, i))], outs, out_specs,
        [pltpu.VMEM((rows, units), LOW), pltpu.SemaphoreType.DMA((4,))], after=after,
    )


def join_heads_kernel(ix, a0, a1, a2, a3, w0, w1, w2, w3, keep_ref, send_ref, held, sems):
    @pl.when(pl.program_id(0) == 0)
    def _():
        copy_all(
            [
                pair
                for k, ref in enumerate((a0, a1, a2, a3))
                for pair in in_quarters(ix[T], ref, held, slice(k * 128, (k + 1) * 128))
            ],
            sems,
        )

    right = jnp.concatenate([w0[...], w1[...], w2[...], w3[...]], axis=0)
    store_quarters(dot(held[...], right), keep_ref, send_ref)


def join_heads(ix, mixed, w_out, after=()):
    rows = mixed[0].shape[0]
    width = w_out.shape[1]
    step = 1024

    def heads(slot):
        return pl.BlockSpec((128, step), lambda i, m: (m[ME] ^ slot, i))

    outs, out_specs = quarter_outs(rows, width, step)
    return call(
        join_heads_kernel, "join_heads", ix, (width // step,), [*mixed] + [w_out] * 4,
        [ANY] * 4 + [heads(slot) for slot in range(4)], outs, out_specs,
        [pltpu.VMEM((rows, 512), LOW), pltpu.SemaphoreType.DMA((16,))], after=after,
    )


def project_back_kernel(ix, *refs):
    keep_ref, send_ref, held, sems = refs[16:]

    @pl.when(pl.program_id(0) == 0)
    def _():
        copy_all(
            [
                pair
                for k, ref in enumerate(refs[:4])
                for pair in in_quarters(ix[T], ref, held, slice(k * 384, (k + 1) * 384))
            ],
            sems,
        )

    right = jnp.concatenate([ref[...] for ref in refs[4:16]], axis=1)
    store_quarters(against(held[...], right), keep_ref, send_ref)


def project_back(ix, back, weights, after):
    rows = back[0].shape[0]
    width = weights[0].shape[0]
    step = 512

    def heads(slot):
        return pl.BlockSpec((step, 128), lambda i, m: (i, m[ME] ^ slot))

    outs, out_specs = quarter_outs(rows, width, step)
    return call(
        project_back_kernel, "project_back", ix, (width // step,),
        [*back] + [w for slot in range(4) for w in weights],
        [ANY] * 4 + [heads(slot) for slot in range(4) for w in weights], outs, out_specs,
        [pltpu.VMEM((rows, 1536), LOW), pltpu.SemaphoreType.DMA((16,))], after=after,
    )


def rows_call(kernel, name, ix, quarters, others, outs, sums=0, after=()):
    arrays = [a if isinstance(a, tuple) else (a, None) for a in (*quarters, *others)]
    rows, width = arrays[0][0].shape[-2:]
    step = rows // 2

    def spec(array, which):
        if which is not None:
            return pl.BlockSpec((None, step, width), lambda i, m: (which, i, 0))
        if array.shape[0] == 1:
            return pl.BlockSpec((1, width), lambda i, m: (0, 0))
        if array.shape[0] == rows:
            return pl.BlockSpec((step, width), lambda i, m: (i, 0))
        return pl.BlockSpec((step, width), lambda i, m: (2 * m[T] + i, 0))

    return call(
        kernel, name, ix, (2,), [array for array, _ in arrays], [spec(*pair) for pair in arrays],
        [shaped((rows, width), dtype) for dtype in outs] + [shaped((1, width), F32)] * sums,
        [pl.BlockSpec((step, width), lambda i, m: (i, 0))] * len(outs)
        + [pl.BlockSpec((1, width), lambda i, m: (0, 0))] * sums,
        after=after,
    )


def wide_sum(*refs):
    return sum(ref[...].astype(F32) for ref in refs)


def sum_kernel(ix, *refs):
    refs[-1][...] = wide_sum(*refs[:-1]).astype(LOW)


def sums_to_send(ix, arrays, after=()):
    return rows_call(sum_kernel, "sums", ix, arrays, [], [LOW], after=after)[0]


def middle_kernel(ix, one, two, y_ref, tok_ref, gain_ref, middle_ref, second_ref):
    middle = tok_ref[...].astype(F32) + wide_sum(one, two, y_ref)
    middle_ref[...] = middle
    normed, _ = normalize(middle)
    second_ref[...] = (normed * gain_ref[...]).astype(LOW)


def add_rows(out_ref, rows):
    part = jnp.sum(rows, axis=0, keepdims=True)

    @pl.when(pl.program_id(0) == 0)
    def _():
        out_ref[...] = part

    @pl.when(pl.program_id(0) != 0)
    def _():
        out_ref[...] += part


def middle_back_kernel(ix, one, two, y_ref, z_ref, middle_ref, cot_ref, gain_ref, grad_ref, low_ref, sum_ref):
    second_sum = wide_sum(one, two, y_ref, z_ref)
    normed, inverse = normalize(middle_ref[...])
    grad = cot_ref[...].astype(F32) + norm_back(second_sum, normed, inverse, gain_ref[...])
    grad_ref[...] = grad
    low_ref[...] = grad.astype(LOW)
    add_rows(sum_ref, second_sum * normed)


def output_kernel(ix, one, two, y_ref, z_ref, middle_ref, out_ref):
    out_ref[...] = (middle_ref[...] + wide_sum(one, two, y_ref, z_ref)).astype(LOW)


def input_kernel(ix, one, two, y_ref, grad_ref, tok_ref, gain_ref, mlp_ref, out_ref, total):
    here, last = pl.program_id(0), pl.num_programs(0) - 1

    @pl.when(here < last)
    def _():
        first_sum = wide_sum(one, two, y_ref)
        normed, inverse = normalize(tok_ref[...].astype(F32))
        out_ref[...] = (grad_ref[...] + norm_back(first_sum, normed, inverse, gain_ref[...])).astype(LOW)
        add_rows(total, first_sum * normed)

    @pl.when(here == last)
    def _():
        sums = jnp.concatenate([total[...], mlp_ref[...], jnp.zeros((14, total.shape[1]), F32)], axis=0)
        out_ref[0:16, :] = sums.astype(LOW)


def input_back(ix, keep, core, y, grad, tokens, gain, mlp_sum, after):
    rows, width = grad.shape
    step = rows // 2
    at = lambda i: jnp.minimum(i, 1)
    block = pl.BlockSpec((None, step, width), lambda i, m: (0, at(i), 0))
    row = pl.BlockSpec((step, width), lambda i, m: (at(i), 0))
    single = pl.BlockSpec((1, width), lambda i, m: (0, 0))
    return call(
        input_kernel, "input_back", ix, (3,), [keep, core, y, grad, tokens, gain, mlp_sum],
        [block, block, row, row, pl.BlockSpec((step, width), lambda i, m: (2 * m[T] + at(i), 0)), single, single],
        shaped((rows + 16, width)), pl.BlockSpec((step, width), lambda i, m: (i, 0)),
        [pltpu.VMEM((1, width), F32)], after=after,
    )


def copied_kernel(ix, in_ref, out_ref):
    out_ref[...] = in_ref[...]


def copied(ix, rows, after=()):
    count, width = rows.shape
    spec = pl.BlockSpec((count // 2, width), lambda i, m: (i, 0))
    return call(copied_kernel, "copied", ix, (2,), [rows], [spec], shaped((count, width)), spec, after=after)


def join_input_kernel(ix, q0, q1, q2, q3, out_ref, sum_ref, held, sems):
    rows = out_ref.shape[0] // 4
    ins, outs = [], []
    for k, ref in enumerate((q0, q1, q2, q3)):
        ins.append(pltpu.make_async_copy(ref, held.at[k], sems.at[k]))
        at = pl.ds((ix[T] ^ k) * rows, rows)
        outs.append(pltpu.make_async_copy(held.at[k, pl.ds(0, rows)], out_ref.at[at], sems.at[4 + k]))
    for copy in ins:
        copy.start()
    total = jnp.zeros(sum_ref.shape, F32)
    for k, (one, two) in enumerate(zip(ins, outs)):
        one.wait()
        two.start()
        total = total + held[k, rows : rows + 16, :].astype(F32)
    sum_ref[...] = total
    for copy in outs:
        copy.wait()


def join_input(ix, pieces, after):
    rows, width = pieces[0].shape
    rows -= 16
    return call(
        join_input_kernel, "join", ix, (1,), list(pieces), [ANY] * 4,
        [shaped((4 * rows, width)), shaped((16, width), F32)],
        [ANY, pl.BlockSpec((16, width), lambda i, m: (0, 0))],
        [pltpu.VMEM((4, rows + 16, width), LOW), pltpu.SemaphoreType.DMA((8,))], after=after,
    )


def normalize(vector):
    inverse = lax.rsqrt(jnp.mean(vector * vector, axis=-1, keepdims=True) + EPS)
    return (vector * inverse, inverse)


def norm_back(grad_rows, normed, inverse, gain):
    scaled = grad_rows * gain
    return inverse * (scaled - normed * jnp.mean(scaled * normed, axis=-1, keepdims=True))


def tie(ix, value, after):
    return pl.pallas_call(
        lambda *refs: None,
        grid_spec=pltpu.PrefetchScalarGridSpec(
            num_scalar_prefetch=1, grid=(1,), in_specs=[ANY] * (1 + len(after)), out_specs=ANY
        ),
        out_shape=shaped(value.shape, value.dtype),
        input_output_aliases={1: 0},
        cost_estimate=pl.CostEstimate(flops=0, bytes_accessed=0, transcendentals=0),
        name="tie",
    )(ix, value, *after)


def spread(quarter, hold=lambda two: two, late=lambda quarter: quarter):
    two = hold(swap(quarter, TENSOR, 2))
    one = swap(late(quarter), TENSOR, 1)
    three = swap(two, TENSOR, 1)
    return (quarter, one, two, three)


def quarter_copies(t, pieces, held):
    rows = pieces[0].shape[0]
    return [(ref, held.at[pl.ds((t ^ k) * rows, rows)]) for k, ref in enumerate(pieces)]


def join_kernel(ix, q0, q1, q2, q3, out_ref, held, sems):
    rows = q0.shape[0]
    ins, outs = [], []
    for k, ref in enumerate((q0, q1, q2, q3)):
        ins.append(pltpu.make_async_copy(ref, held.at[k], sems.at[k]))
        at = pl.ds((ix[T] ^ k) * rows, rows)
        outs.append(pltpu.make_async_copy(held.at[k], out_ref.at[at], sems.at[4 + k]))
    for copy in ins:
        copy.start()
    for one, two in zip(ins, outs):
        one.wait()
        two.start()
    for copy in outs:
        copy.wait()


def join(ix, pieces, after=()):
    rows, width = pieces[0].shape
    return call(
        join_kernel, "join", ix, (1,), list(pieces), [ANY] * 4,
        shaped((4 * rows, width)), ANY,
        [pltpu.VMEM((4, rows, width), LOW), pltpu.SemaphoreType.DMA((8,))], after=after,
    )


def mine_kernel(ix, *refs):
    count = len(refs) // 2
    rows = refs[count].shape[0]
    at = pl.ds(ix[T] * rows, rows)
    copy_all([(refs[k].at[at], refs[count + k]) for k in range(count)], refs[-1])


def mine(ix, arrays, after):
    count, width = arrays[0].shape
    size = len(arrays)
    return call(
        mine_kernel, "quarter", ix, (1,), list(arrays), [ANY] * size, [shaped((count // 4, width))] * size,
        [pl.BlockSpec((count // 4, width), lambda i, m: (0, 0))] * size, [pltpu.SemaphoreType.DMA((size,))],
        after=after,
    )


def others_kernel(ix, rows_ref, out_ref, sems):
    copy_all([(rows_ref.at[ix[ME] ^ k], out_ref.at[k - 1]) for k in range(1, 4)], sems)


def others(ix, rows, after):
    shape = (3,) + rows.shape[1:]
    return call(
        others_kernel, "others", ix, (1,), [rows], [ANY], shaped(shape),
        pl.BlockSpec(shape, lambda i, m: (0, 0, 0)), [pltpu.SemaphoreType.DMA((3,))], after=after,
    )


def tables_kernel(ix, freq_ref, cos_ref, sin_ref):
    rows = cos_ref.shape[0]
    lane = lax.broadcasted_iota(jnp.int32, (1, 128), 1)
    place = pl.program_id(0) * rows + lax.broadcasted_iota(jnp.int32, (rows, 128), 0)
    angle = place.astype(F32) * freq_ref[0:1, :]
    cos_ref[...] = jnp.cos(angle)
    sin_ref[...] = jnp.where((lane % HEAD_DIM) < HEAD_DIM // 2, -1.0, 1.0) * jnp.sin(angle)


def all_rope_tables(ix, count, after):
    step = 768
    return call(
        tables_kernel, "rope_tables", ix, (count // step,), [rope_freq().reshape(1, 128)],
        [pl.BlockSpec((1, 128), lambda i, m: (0, 0))], [shaped((count, 128), F32)] * 2,
        [pl.BlockSpec((step, 128), lambda i, m: (i, 0))] * 2, after=after,
    )


def hidden_back_kernel(ix, cot_ref, w_ref, out_ref):
    out_ref[...] = against(cot_ref[...], w_ref[...])


def far_rows(array, rows):
    return (lambda m: (m[ME] % 2) ^ 1) if array.shape[0] > rows else (lambda m: 0)


def hidden_back(ix, cotangent, rows, w_down, after=()):
    width = cotangent.shape[1]
    units = w_down.shape[0] // 2
    step = 512
    block = far_rows(cotangent, rows)
    return call(
        hidden_back_kernel, "hidden_back", ix, (units // step,), [cotangent, w_down],
        [
            pl.BlockSpec((rows, width), lambda i, m: (block(m), 0)),
            pl.BlockSpec((step, width), lambda i, m: ((m[ME] % 2) * (units // step) + i, 0)),
        ],
        shaped((rows, units), F32), pl.BlockSpec((rows, step), lambda i, m: (0, i)), after=after,
    )


def feed_kernel(ix, *refs, count):
    pieces = refs[:count]
    wg_ref, wu_ref, hb_ref, wg_rows, wu_rows, rows_ref, hid_ref, gb_ref, ub_ref, keep_ref, send_ref = refs[count:-4]
    held, gate_back, up_back, sems = refs[-4:]
    t = ix[T]
    here = pl.program_id(0)
    rows, units = gate_back.shape
    step = wg_ref.shape[1]
    forward = units // step
    quarter = rows // 4

    @pl.when(here == 0)
    def _():
        if count == 1:
            copy_all([(pieces[0].at[pl.ds((1 - ix[ME] % 2) * rows, rows)], held)], sems)
        else:
            copy_all(quarter_copies(t, pieces, held), sems)
        pltpu.make_async_copy(held, rows_ref, sems.at[4]).start()

    @pl.when(here < forward)
    def _():
        second = held[...]
        gate = dot(second, wg_ref[...])
        up = dot(second, wu_ref[...])
        back = hb_ref[...]
        sig = 0.5 + 0.5 * jnp.tanh(0.5 * gate)
        swish = gate * sig
        hid_ref[...] = (swish * up).astype(LOW)
        gate_low = (back * up * (sig + swish * (1.0 - sig))).astype(LOW)
        up_low = (back * swish).astype(LOW)
        gb_ref[...] = gate_low
        ub_ref[...] = up_low
        columns = pl.ds(pl.multiple_of(here * step, step), step)
        for k in range(4):
            slot = k ^ t
            place = pl.ds(pl.multiple_of(((slot & 1) * 2 + (slot >> 1)) * quarter, quarter), quarter)
            gate_back[place, columns] = gate_low[k * quarter : (k + 1) * quarter]
            up_back[place, columns] = up_low[k * quarter : (k + 1) * quarter]

    @pl.when(here >= forward)
    def _():
        total = against(gate_back[...], wg_rows[...]) + against(up_back[...], wu_rows[...])
        store_quarters(total, keep_ref, send_ref)

    @pl.when(here == pl.num_programs(0) - 1)
    def _():
        pltpu.make_async_copy(held, rows_ref, sems.at[4]).wait()


def feed(ix, pieces, w_gate, w_up, back, after=()):
    rows, width = back.shape[0], pieces[0].shape[1]
    units = w_gate.shape[1] // 2
    step, wide = 256, 512
    forward = units // step
    first = lambda i: jnp.minimum(i, forward - 1)
    then = lambda i: jnp.maximum(i - forward, 0)
    weight = pl.BlockSpec((width, step), lambda i, m: (0, (m[ME] % 2) * forward + first(i)))
    weight_rows = pl.BlockSpec((wide, units), lambda i, m: (then(i), m[ME] % 2))
    block = pl.BlockSpec((rows, step), lambda i, m: (0, first(i)))
    return call(
        functools.partial(feed_kernel, count=len(pieces)), "feed", ix, (forward + width // wide,),
        [*pieces, w_gate, w_up, back, w_gate, w_up],
        [ANY] * len(pieces) + [weight] * 2 + [block] + [weight_rows] * 2,
        [shaped((rows, width))] + [shaped((rows, units))] * 3 + [shaped((2, rows // 4, width))] * 2,
        [ANY, block, block, block] + [pl.BlockSpec((2, rows // 4, wide), lambda i, m: (0, 0, then(i)))] * 2,
        [
            pltpu.VMEM((rows, width), LOW),
            pltpu.VMEM((rows, units), LOW),
            pltpu.VMEM((rows, units), LOW),
            pltpu.SemaphoreType.DMA((5,)),
        ],
        after=after,
    )


def branch_back_kernel(ix, q0, q1, q2, q3, w0, w1, w2, w3, rows_ref, o0, o1, o2, o3, held, sems):
    copy_all(quarter_copies(ix[T], (q0, q1, q2, q3), held), sems)
    keep = pltpu.make_async_copy(held, rows_ref, sems.at[4])
    keep.start()
    weight = jnp.concatenate([w0[...], w1[...], w2[...], w3[...]], axis=0)
    for part in range(3):
        at = slice(part * 256, (part + 1) * 256)
        flat = against(held[at, :], weight).astype(LOW)
        for slot, out in enumerate((o0, o1, o2, o3)):
            out[at, :] = flat[:, slot * 128 : (slot + 1) * 128]
    keep.wait()


def branch_back(ix, pieces, w_out, after):
    rows, width = pieces[0].shape
    rows = 4 * rows

    def heads(slot):
        return pl.BlockSpec((128, width), lambda i, m: (m[ME] ^ slot, 0))

    return call(
        branch_back_kernel, "branch_back", ix, (1,), [*pieces] + [w_out] * 4,
        [ANY] * 4 + [heads(slot) for slot in range(4)],
        [shaped((rows, width))] + [shaped((rows, 128))] * 4,
        [ANY] + [pl.BlockSpec((rows, 128), lambda i, m: (0, 0))] * 4,
        [pltpu.VMEM((rows, width), LOW), pltpu.SemaphoreType.DMA((5,))], after=after,
    )


def wgrad_kernel(ix, l0, l1, r0, r1, out_ref):
    out_ref[0] = (across(l0[...], r0[...]) + across(l1[...], r1[...])).astype(LOW)


def wgrad_kernel(ix, l0, l1, r0, r1, out_ref):
    out_ref[0] = (across(l0[...], r0[...]) + across(l1[...], r1[...])).astype(LOW)


def wgrad(ix, wide, free, name, after=()):
    rows, units = free[0].shape
    share = 256

    def wide_spec(array):
        block = far_rows(array, rows)
        return pl.BlockSpec((rows, share), lambda i, m: (block(m), i ^ (m[ME] % 2)))

    return call(
        wgrad_kernel, name, ix, (8,), [*wide, *free],
        [wide_spec(array) for array in wide] + [pl.BlockSpec((rows, units), lambda i, m: (0, 0))] * 2,
        shaped((8, share, units)), pl.BlockSpec((1, share, units), lambda i, m: (i, 0, 0)), after=after,
    )


def add_blocks_kernel(ix, a_ref, b_ref, *refs):
    total = (a_ref[...].astype(F32) + b_ref[...].astype(F32)).astype(LOW)
    size = refs[0].shape[0]
    for k, ref in enumerate(refs):
        ref[...] = total[k * size : (k + 1) * size]


def add_blocks(ix, one, two, parts, after=()):
    shape = (one.shape[0] // parts,) + one.shape[1:]
    whole = pl.BlockSpec(one.shape, lambda i, m: (0, 0, 0))
    return call(
        add_blocks_kernel, "add_blocks", ix, (1,), [one, two], [whole] * 2,
        [shaped(shape)] * parts, [pl.BlockSpec(shape, lambda i, m: (0, 0, 0))] * parts, after=after,
    )


def one_block_kernel(ix, in_ref, out_ref):
    out_ref[...] = in_ref[...]


def one_block(ix, blocks, which, after=()):
    shape = (1,) + blocks.shape[1:]
    return call(
        one_block_kernel, "one_block", ix, (1,), [blocks],
        [pl.BlockSpec(shape, lambda i, m: (which, 0, 0))], shaped(shape),
        pl.BlockSpec(shape, lambda i, m: (0, 0, 0)), after=after,
    )


def halves_kernel(ix, own_ref, other_ref, out_ref, *, axis):
    which = ix[ME] % 2
    for place, ref in ((which, own_ref), (1 - which, other_ref)):
        value = ref[...].astype(F32)
        if axis == 0:
            value = value.T
        size = value.shape[axis]
        at = pl.ds(pl.multiple_of(place * size, size), size)
        if axis == 0:
            out_ref[at, :] = value
        else:
            out_ref[:, at] = value


def halves(ix, blocks, other, axis, after=()):
    share, units = blocks.shape[1:]
    shape = (2 * units, share) if axis == 0 else (share, 2 * units)
    whole = lambda i, m: (0, 0)
    return call(
        functools.partial(halves_kernel, axis=axis), "halves", ix, (1,), [blocks, other],
        [pl.BlockSpec((None, share, units), lambda i, m: (0, 0, 0))] * 2,
        shaped(shape, F32), pl.BlockSpec(shape, whole), after=after,
    )


def out_wgrad_kernel(ix, a0, a1, a2, a3, rows_ref, own_ref, far_ref, held):
    for slot, ref in enumerate((a0, a1, a2, a3)):
        at = pl.ds(pl.multiple_of((slot ^ ix[ME]) * 128, 128), 128)
        held[at, :] = across(ref[...], rows_ref[...]).astype(LOW)
    for half, out in enumerate((own_ref, far_ref)):

        @pl.when(pl.program_id(0) // 4 == half)
        def _():
            out[0] = held[...]


def out_wgrad(ix, mixed, rows, after=()):
    count, width = rows.shape
    share = 256
    return call(
        out_wgrad_kernel, "out_wgrad", ix, (width // share,), [*mixed, rows],
        [pl.BlockSpec((count, 128), lambda i, m: (0, 0))] * 4
        + [pl.BlockSpec((count, share), lambda i, m: (0, i ^ (m[DP] * 4 + m[ME])))],
        [shaped((4, 512, share))] * 2,
        [
            pl.BlockSpec((1, 512, share), lambda i, m: (jnp.minimum(i, 3), 0, 0)),
            pl.BlockSpec((1, 512, share), lambda i, m: (jnp.maximum(i - 4, 0), 0, 0)),
        ],
        [pltpu.VMEM((512, share), LOW)], after=after,
    )


def project_wgrad_kernel(ix, first_ref, f0, f1, f2, f3, b0, b1, b2, b3, own_ref, far_ref, held, total, sems):
    me, t = ix[ME], ix[T]
    turn = pl.program_id(0)
    quarter = f0.shape[1]

    def copies(slot):
        if slot == 0:
            return [pltpu.make_async_copy(first_ref, held.at[0], sems.at[0, 0])]
        return [
            pltpu.make_async_copy(
                ref.at[slot - 1], held.at[slot, pl.ds((t ^ k) * quarter, quarter)], sems.at[slot, k]
            )
            for k, ref in enumerate((f0, f1, f2, f3))
        ]

    @pl.when(turn == 0)
    def _():
        for slot in range(4):
            for copy in copies(slot):
                copy.start()

    for slot, back in enumerate((b0, b1, b2, b3)):

        @pl.when(turn == slot)
        def _():
            for copy in copies(slot):
                copy.wait()
            for block in range(8):
                at = slice(block * 256, (block + 1) * 256)
                part = across(held[slot, :, at], back[...])
                if slot == 0:
                    total[at, :] = part
                elif slot < 3:
                    total[at, :] += part
                else:
                    done = (total[at, :] + part).astype(LOW)

                    @pl.when(ix[DP] == block // 4)
                    def _():
                        own_ref[(block % 4) ^ me] = done

                    @pl.when(ix[DP] != block // 4)
                    def _():
                        far_ref[(block % 4) ^ me] = done


def project_wgrad(ix, first_in, far, back, after=()):
    rows, width = first_in.shape
    whole = lambda i, m: (0, 0)
    return call(
        project_wgrad_kernel, "project_wgrad", ix, (4,), [first_in, *far, *back],
        [ANY] * 5 + [pl.BlockSpec((rows, 384), whole)] * 4,
        [shaped((4, 256, 384))] * 2, [pl.BlockSpec((4, 256, 384), lambda i, m: (0, 0, 0))] * 2,
        [
            pltpu.VMEM((4, rows, width), LOW),
            pltpu.VMEM((width, 384), F32),
            pltpu.SemaphoreType.DMA((4, 4)),
        ],
        after=after,
    )


def add_parts_kernel(ix, a_ref, b_ref, gain_ref, *refs):
    rows = a_ref.shape[1]
    for k, out in enumerate(refs):
        out[0:rows, :] = (a_ref[k].astype(F32) + b_ref[k].astype(F32)).astype(LOW)
        gains = jnp.concatenate([gain_ref[k], jnp.zeros((14, gain_ref.shape[2]), F32)], axis=0)
        out[rows : rows + 16, 0 : gains.shape[1]] = gains.astype(LOW)
        out[rows : rows + 16, gains.shape[1] :] = jnp.zeros((16, out.shape[1] - gains.shape[1]), LOW)


def add_parts(ix, one, two, gains, after=()):
    count, rows, width = one.shape
    whole = lambda shape: pl.BlockSpec(shape, lambda i, m: (0,) * len(shape))
    shape = (rows + 16, width)
    return call(
        add_parts_kernel, "add_blocks", ix, (1,), [one, two, gains], [whole(a.shape) for a in (one, two, gains)],
        [shaped(shape)] * count, [whole(shape)] * count, after=after,
    )


def add_last_kernel(ix, a_ref, b_ref, out_ref):
    out_ref[...] = a_ref[...].astype(F32) + b_ref[...].astype(F32)


def add_last(ix, one, two, after):
    shape = one.shape[1:]
    block = pl.BlockSpec((None, *shape), lambda i, m: (0, 0, 0))
    return call(
        add_last_kernel, "add_last", ix, (1,), [one, two], [block] * 2, shaped(shape, F32),
        pl.BlockSpec(shape, lambda i, m: (0, 0)), after=after,
    )


def project_last_kernel(ix, p0, p1, p2, p3, q_ref, k_ref, v_ref, *gain_refs):
    share = q_ref.shape[0]
    for slot, ref in enumerate((p0, p1, p2, p3)):
        at = pl.ds(pl.multiple_of((slot ^ ix[ME]) * 128, 128), 128)
        for place, out in enumerate((q_ref, k_ref, v_ref)):
            out[:, at] = ref[0:share, place * 128 : (place + 1) * 128].astype(F32)
    for out in gain_refs:
        out[...] = sum(ref[share : share + 16, 0 : out.shape[1]].astype(F32) for ref in (p0, p1, p2, p3))


def project_last(ix, pieces, share, after=()):
    whole = lambda i, m: (0, 0)
    shapes = [(share, 512)] * 3 + ([(16, share)] if pieces[0].shape[0] > share else [])
    return call(
        project_last_kernel, "project_last", ix, (1,), list(pieces), [pl.BlockSpec(pieces[0].shape, whole)] * 4,
        [shaped(shape, F32) for shape in shapes], [pl.BlockSpec(shape, whole) for shape in shapes], after=after,
    )


def over_ctx(slots):
    return [slots[0]] + [swap(slots[k], CTX, k) for k in range(1, 4)]


def per_device(
    dp_size, tokens, attn_gain, w_query, w_key, w_value, w_out, mlp_gain, w_gate, w_up, w_down, cotangent
):
    rows_here, width = tokens.shape
    share = width // (4 * dp_size)
    me, t, d = lax.axis_index(CTX), lax.axis_index(TENSOR), lax.axis_index("dp")
    two_dp = dp_size == 2
    ix = jnp.stack([me, t, d if two_dp else jnp.zeros_like(d)]).astype(jnp.int32)
    order = me ^ jnp.arange(4)
    projections = (w_query, w_key, w_value)
    attn_gain, mlp_gain = attn_gain.reshape(1, -1), mlp_gain.reshape(1, -1)

    cot_mine = lax.dynamic_slice_in_dim(cotangent, t * (rows_here // 4), rows_here // 4, 0)
    tables = rope_tables(me * rows_here + jnp.arange(rows_here, dtype=jnp.int32))
    first_in, *slots = project(ix, tokens, attn_gain, tables, projections)
    pieces = over_ctx(slots)

    back_own = hidden_back(ix, cotangent, rows_here, w_down, (slots[0],))
    all_tables = all_rope_tables(ix, 4 * rows_here, (back_own,))
    (first_mine,) = mine(ix, [first_in], (all_tables[0],))
    cot_mine = tie(ix, cot_mine, (*pieces[1:], first_mine))
    cot_both = lax.all_gather(cot_mine, ("lo", *TENSOR), axis=0, tiled=True)

    *mixed_slots, raw, lse = attend(ix, pieces, (first_mine,))
    mixed = over_ctx(mixed_slots)
    keep, send = join_heads(ix, mixed, w_out, (cot_both,))
    core = swap(send, TENSOR, 1)
    low = sums_to_send(ix, [(keep, 1), (core, 1)])
    middle, second_mine = rows_call(
        middle_kernel, "middle", ix, [(keep, 0), (core, 0), swap(low, TENSOR, 2)], [tokens, mlp_gain], [F32, LOW]
    )

    second_both = lax.all_gather(second_mine, ("lo", *TENSOR), axis=0, tiled=True)
    back_far = hidden_back(ix, cot_both, rows_here, w_down, (second_mine,))
    own_pieces = spread(second_mine, lambda two: tie(ix, two, (back_far,)))
    second_own, hid_own, gb_own, ub_own, keep_own, send = feed(ix, own_pieces, w_gate, w_up, back_own)
    first_all = lax.all_gather(tie(ix, first_mine, (hid_own,)), CTX, axis=0, tiled=False)
    core_own = swap(send, TENSOR, 1)
    second_far, hid_far, gb_far, ub_far, keep, send = feed(ix, [second_both], w_gate, w_up, back_far, (hid_own,))

    seconds = (second_own, second_far)

    def over_pairs(part):
        return lax.psum_scatter(part, ("dp", "hi"), scatter_dimension=0, tiled=True) if two_dp else part

    core = swap(send, TENSOR, 1)
    part_down = wgrad(ix, (cotangent, cot_both), (hid_own, hid_far), "wgrad_down")
    low = sums_to_send(ix, [(keep, 1), (core, 1)])
    far_y = swap(low, TENSOR, 2)
    down_far = feed_down(ix, hid_far, w_down, (low,))
    low = sums_to_send(ix, [(keep, 0), (core, 0), far_y], (down_far[0],))
    far_z = swap(low, CTX, 1)
    sum_down = over_pairs(tie(ix, part_down, (far_z,)))
    low = sums_to_send(ix, [(keep_own, 1), (core_own, 1)], (low,))
    own_sums = [(keep_own, 0), (core_own, 0), swap(low, TENSOR, 2)]
    core_far = swap(down_far[1], TENSOR, 1)
    down_own = feed_down(ix, hid_own, w_down, (low,))
    low = sums_to_send(ix, [(down_far[0], 1), (core_far, 1)], (down_own[0],))
    far_down = [(down_far[0], 0), (core_far, 0), swap(low, TENSOR, 2)]
    middle_grad, branch_mine, mlp_gain_part = rows_call(
        middle_back_kernel, "middle_back", ix, [*own_sums, far_z, middle], [cotangent, mlp_gain], [F32, LOW], 1,
        (low,),
    )
    core_own = swap(down_own[1], TENSOR, 1)
    low = sums_to_send(ix, [(down_own[0], 1), (core_own, 1)], (branch_mine,))
    own_y = swap(low, TENSOR, 2)
    branch_low, *slots = branch_back(ix, spread(branch_mine), w_out, (low,))
    upstreams = over_ctx(slots)
    first_far = others(ix, first_all, (branch_low,))
    out_own, out_far = out_wgrad(ix, mixed, branch_low, (first_far,))
    part_gate = wgrad(ix, seconds, (gb_own, gb_far), "wgrad_gate", (out_own, own_y))
    sum_gate = over_pairs(tie(ix, part_gate, upstreams[1:]))

    def for_partner(blocks, after):
        return swap(blocks[1:] if after is None else one_block(ix, blocks, 1, after), CTX, 1)

    token, arrived = own_y, []
    if two_dp:
        out_other = swap(out_far, "dp", 1)
        token = one_block(ix, sum_down, 1, (out_own, *upstreams[1:]))
        down_other = swap(token, CTX, 1)
        arrived = [out_other, down_other]
    back_slots = attend_back(ix, pieces, upstreams, raw, lse, all_tables, (token, out_own, own_y))
    back = over_ctx(back_slots)

    arrived = (back_slots[0], *arrived)
    first_spread = spread(first_far, lambda two: tie(ix, two, arrived))
    qkv_own, qkv_far = project_wgrad(ix, first_in, first_spread, back_slots)
    far_low = sums_to_send(ix, far_down, (qkv_own,))
    token = far_low
    if two_dp:
        qkv_other = swap(qkv_far, "dp", 1)
        out_part = add_blocks(ix, out_own, out_other, 2, (far_low,))
        down_grad = halves(ix, sum_down, down_other, 0, (out_part[0],))
        token = down_grad
    part_up = wgrad(ix, seconds, (ub_own, ub_far), "wgrad_up", (token,))
    part_up = tie(ix, part_up, back[1:])
    sum_up = over_pairs(part_up)
    keep, send = project_back(ix, back, projections, (part_up,))
    core = swap(send, TENSOR, 1)
    low = sums_to_send(ix, [(keep, 1), (core, 1)])
    low_y = swap(low, TENSOR, 2)
    far_z = swap(tie(ix, far_low, (low,)), CTX, 1)
    token = low
    if two_dp:
        gate_low = one_block(ix, sum_gate, 1, (low,))
        gate_other = swap(gate_low, CTX, 1)
        token = gate_low
    input_mine = input_back(ix, keep, core, low_y, middle_grad, tokens, attn_gain, mlp_gain_part, (token,))
    arrived = (far_z,)
    if two_dp:
        out_z = swap(tie(ix, out_part[1], (keep,)), CTX, 2)
        arrived = (far_z, qkv_other, out_z)
    input_grad, gains = join_input(ix, spread(input_mine, lambda two: tie(ix, two, arrived)), (input_mine,))
    gains = gains[:2]
    if two_dp:
        halved = gains.reshape(2, 2, width // 2)[:, d ^ jnp.arange(2)]
        gains = halved[:, 0] + swap(halved[:, 1], "dp", 1)
        gains = gains.reshape(2, 4, share).transpose(1, 0, 2)[order]
    (output_mine,) = rows_call(
        output_kernel, "output", ix, [(down_own[0], 0), (core_own, 0), own_y, far_z, middle], [], [LOW],
        after=(input_grad,),
    )
    output = lax.all_gather(output_mine, TENSOR, axis=0, tiled=True)
    if not two_dp:
        output = copied(ix, output)
    if two_dp:
        up_low = one_block(ix, sum_up, 1, (output_mine,))
        up_other = swap(up_low, CTX, 1)
        out_part = add_blocks(ix, out_part[0], out_z, 2, (up_low,))
        out_other = swap(out_part[1], CTX, 1)
        qkv_parts = over_ctx(add_parts(ix, qkv_own, qkv_other, gains, (out_part[0],)))
        gate_grad = halves(ix, sum_gate, gate_other, 1, (qkv_parts[0],))
        up_grad = halves(ix, sum_up, up_other, 1, (gate_grad,))
        output = copied(ix, output, (up_grad,))
        *qkv, gains = project_last(ix, qkv_parts, share, (output,))
        out_grad = add_last(ix, out_part[0], out_other, (qkv[0],))
    else:
        def scattered(blocks, axis):
            blocks = jnp.moveaxis(blocks, 0, axis)
            shape = blocks.shape[:axis] + (width,) + blocks.shape[axis + 2 :]
            part = lax.psum_scatter(blocks.reshape(shape), "dp", scatter_dimension=axis, tiled=True)
            shape = part.shape[:axis] + (4, share) + part.shape[axis + 1 :]
            return jnp.moveaxis(part.reshape(shape), axis, 0)

        def in_order(blocks):
            return blocks.reshape(2, 4, *blocks.shape[1:])[:, order].reshape(blocks.shape)

        grads = []
        own_first = me % 2 ^ jnp.arange(2)
        for k, blocks in enumerate((sum_down, sum_gate, sum_up)):
            blocks = blocks.reshape(4, 2, *blocks.shape[1:])[:, own_first].reshape(blocks.shape)
            part = scattered(blocks, 0)[order].astype(F32)
            part = (part[:2] + swap(part[2:].astype(LOW), CTX, 2).astype(F32)).astype(LOW)
            grads.append(halves(ix, part, for_partner(part, None), min(k, 1)))
        down_grad, gate_grad, up_grad = grads
        qkv_parts = over_ctx(scattered(in_order(jnp.concatenate([qkv_own, qkv_far])), 0)[order])
        out_part = scattered(in_order(jnp.concatenate([out_own, out_far])), 1)[order]
        out_part = out_part[:2].astype(F32) + swap(out_part[2:], CTX, 2).astype(F32)
        out_grad = out_part[0] + swap(out_part[1].astype(LOW), CTX, 1).astype(F32)
        qkv = project_last(ix, qkv_parts, share)
        gains = lax.psum_scatter(gains, "dp", scatter_dimension=1, tiled=True)
        gains = sum(over_ctx(gains.reshape(2, 4, share).transpose(1, 0, 2)[order]))

    return (
        output,
        input_grad,
        gains[0],
        qkv[0],
        qkv[1],
        qkv[2],
        out_grad,
        gains[1],
        gate_grad,
        up_grad,
        down_grad,
    )


def solution(mesh):
    dp_size = mesh.shape["dp"]
    mesh = jax.sharding.Mesh(mesh.devices.reshape(dp_size, 2, 2, 2, 2), ("dp", *CTX, *TENSOR))
    rows, tensor = ("dp", *CTX), TENSOR
    columns = P(None, tensor)
    in_specs = (
        P(rows, None), P(), columns, columns, columns, P(tensor, None),
        P(), columns, columns, P(tensor, None), P(rows, None),
    )
    out_specs = (
        P(rows, None), P(rows, None), P(rows), P(rows, tensor), P(rows, tensor), P(rows, tensor),
        P(tensor, rows), P(rows), P(rows, tensor), P(rows, tensor), P(tensor, rows),
    )
    return jax.shard_map(
        functools.partial(per_device, dp_size),
        mesh=mesh,
        in_specs=in_specs,
        out_specs=out_specs,
        check_vma=False,
    )
```

```python
import functools

import jax
import jax.numpy as jnp
from jax import lax
from jax.experimental import pallas as pl
from jax.experimental.pallas import tpu as pltpu
from jax.sharding import PartitionSpec as P

HEAD_DIM = 64
EPS = 1e-05
THETA = 130000.0
MIB = 1 << 20
MOST = 64
COSTS = {
    "project": 11, "hidden_back": 8.5, "rope_tables": 8, "attend": 28, "quarter": 3,
    "join_heads": 6.5, "sums": 3, "join": 3.5, "middle": 4, "feed": 24, "wgrad_down": 14, "wgrad_gate": 14, "wgrad_up": 14,
    "middle_back": 5, "branch_back": 7, "others": 4, "feed_down": 9, "attend_back": 40, "project_wgrad": 13,
    "out_wgrad": 8.5, "add_pairs": 4, "project_back": 11, "input_back": 5, "output": 4, "halves": 3.5,
    "project_last": 3, "add_blocks": 3, "one_block": 2,
}
SCALE = 2
LOW = jnp.bfloat16
F32 = jnp.float32
ANY = pl.BlockSpec(memory_space=pl.ANY)


CTX, TENSOR = ("hi", "lo"), ("y", "core")


def swap(value, axis, distance):
    size = 2 if axis == "dp" else 4
    return lax.ppermute(value, axis, [(i, i ^ distance) for i in range(size)])


def dot(left, right):
    return jnp.dot(left, right, preferred_element_type=F32)


def against(left, right):
    return lax.dot_general(left, right, (((1,), (1,)), ((), ())), preferred_element_type=F32)


def across(left, right):
    return lax.dot_general(left, right, (((0,), (0,)), ((), ())), preferred_element_type=F32)


def shaped(shape, dtype=LOW):
    return jax.ShapeDtypeStruct(shape, dtype)


def call(kernel, name, index, grid, inputs, in_specs, outs, out_specs, scratch=(), mib=MOST, after=()):
    count = len(inputs)

    def body(index_ref, *refs):
        kernel(index_ref, *refs[:count], *refs[count + len(after) :])

    return pl.pallas_call(
        body,
        grid_spec=pltpu.PrefetchScalarGridSpec(
            num_scalar_prefetch=1,
            grid=grid,
            in_specs=list(in_specs) + [ANY] * len(after),
            out_specs=out_specs,
            scratch_shapes=list(scratch),
        ),
        out_shape=outs,
        compiler_params=pltpu.CompilerParams(
            vmem_limit_bytes=mib * MIB, dimension_semantics=("arbitrary",) * len(grid)
        ),
        cost_estimate=pl.CostEstimate(flops=0, bytes_accessed=int(COSTS.get(name, 0) * SCALE * 3.5 * MIB), transcendentals=0),
        name=name,
    )(index, *inputs, *after)


ME, T, DP = 0, 1, 2


def copy_all(pairs, sems):
    copies = [pltpu.make_async_copy(a, b, sems.at[k]) for k, (a, b) in enumerate(pairs)]
    for copy in copies:
        copy.start()
    for copy in copies:
        copy.wait()


def half_turn(rows):
    lane = lax.broadcasted_iota(jnp.int32, (1, 128), 1)
    first = (lane % HEAD_DIM) < HEAD_DIM // 2
    return jnp.where(first, pltpu.roll(rows, 96, 1), pltpu.roll(rows, 32, 1))


def rope_freq():
    half = HEAD_DIM // 2
    freq = jnp.power(THETA, -jnp.arange(half, dtype=F32) * (2.0 / HEAD_DIM))
    return jnp.concatenate([freq] * 4)


def rope_tables(positions):
    angle = rope_freq()[: HEAD_DIM // 2, None] * positions.astype(F32)[None, :]
    return jnp.cos(angle), jnp.sin(angle)


def project_kernel(ix, tok_ref, gain_ref, cos_ref, sin_ref, wq_ref, wk_ref, wv_ref, first_ref, o0, o1, o2, o3, held):
    me = ix[ME]
    rows = tok_ref[...].astype(F32)
    inverse = lax.rsqrt(jnp.mean(rows * rows, axis=-1, keepdims=True) + EPS)
    first = (rows * inverse * gain_ref[...]).astype(LOW)
    first_ref[...] = first
    half_cos, half_sin = cos_ref[...].T, sin_ref[...].T
    cosine = jnp.concatenate([half_cos] * 4, axis=1)
    sine = jnp.concatenate([-half_sin, half_sin] * 2, axis=1)
    for place, weight in enumerate((wq_ref, wk_ref, wv_ref)):
        flat = dot(first, weight[...])
        for group in range(4):
            part = flat[:, group * 128 : (group + 1) * 128]
            if place < 2:
                part = part * cosine + half_turn(part) * sine
            if place == 0:
                part = part * HEAD_DIM**-0.5
            held[group, :, place * 128 : (place + 1) * 128] = part.astype(LOW)
    for slot, out in enumerate((o0, o1, o2, o3)):
        out[...] = held[slot ^ me]


def project(ix, tokens, gain, tables, weights):
    rows, width = tokens.shape
    local = weights[0].shape[1]
    step = 256
    whole = lambda i, m: (0, 0)
    along = lambda i, m: (i, 0)
    return call(
        project_kernel, "project", ix, (rows // step,),
        [tokens, gain, *tables, *weights],
        [pl.BlockSpec((step, width), along), pl.BlockSpec((1, width), whole)]
        + [pl.BlockSpec((HEAD_DIM // 2, step), lambda i, m: (0, i))] * 2 + [pl.BlockSpec((width, local), whole)] * 3,
        [shaped((rows, width))] + [shaped((rows, 384))] * 4,
        [pl.BlockSpec((step, width), along)] + [pl.BlockSpec((step, 384), along)] * 4,
        [pltpu.VMEM((4, step, 384), LOW)],
    )


def own_lanes(rows, head):
    lane = lax.broadcasted_iota(jnp.int32, (1, 128), 1)
    inside = (lane < HEAD_DIM) if head == 0 else (lane >= HEAD_DIM)
    return jnp.where(inside, rows, jnp.zeros_like(rows))


def attend_kernel(ix, r0, r1, r2, r3, o0, o1, o2, o3, raw_ref, lse_ref, held, sems):
    me = ix[ME]
    turn = pl.program_id(0)
    here = turn ^ me
    stretch = r0.shape[0]
    half = stretch // 2
    lane = lax.broadcasted_iota(jnp.int32, (1, 128), 1)

    @pl.when(turn == 0)
    def _():
        copy_all(
            [(ref, held.at[pl.ds((me ^ k) * stretch, stretch)]) for k, ref in enumerate((r0, r1, r2, r3))], sems
        )

    query = held[pl.ds(here * stretch, stretch), 0:128]
    queries = [own_lanes(query, head) for head in range(2)]

    def step(queries, rows, carry, offset):
        keys, values = held[rows, 128:256], held[rows, 256:384]
        out = []
        for head in range(2):
            peak, mass, total = carry[3 * head : 3 * head + 3]
            scores = against(queries[head], keys)
            if offset is not None:
                down = lax.broadcasted_iota(jnp.int32, scores.shape, 0) + offset
                along = lax.broadcasted_iota(jnp.int32, scores.shape, 1)
                scores = jnp.where(down >= along, scores, -1e30)
            top = jnp.maximum(peak, jnp.max(scores, axis=-1, keepdims=True))
            weights = jnp.exp(scores - top)
            fade = jnp.exp(peak - top)
            mass = mass * fade + jnp.sum(weights, axis=-1, keepdims=True)
            out += [top, mass, total * fade + dot(weights.astype(LOW), values)]
        return tuple(out)

    start = (
        jnp.full((stretch, 1), -1e30, F32),
        jnp.zeros((stretch, 1), F32),
        jnp.zeros((stretch, 128), F32),
    ) * 2
    carry = lax.fori_loop(0, here, lambda at, c: step(queries, pl.ds(at * stretch, stretch), c, None), start)
    for part in range(2):
        at = slice(part * half, (part + 1) * half)
        rows = pl.ds(here * stretch, (part + 1) * half)
        done = step([query[at] for query in queries], rows, [c[at] for c in carry], part * half)
        peak0, mass0, total0, peak1, mass1, total1 = done
        mixed = jnp.where(lane < HEAD_DIM, total0 / mass0, total1 / mass1)
        raw_ref[at, :] = mixed
        for slot, out in enumerate((o0, o1, o2, o3)):

            @pl.when(turn == slot)
            def _():
                out[at, :] = mixed.astype(LOW)

        turned = jnp.where(lane < HEAD_DIM, peak0 + jnp.log(mass0), peak1 + jnp.log(mass1)).T
        lse_ref[0, 0:8, at] = turned[0:8]
        lse_ref[0, 8:16, at] = turned[64:72]


def attend(ix, pieces, after):
    stretch = pieces[0].shape[0]
    length = 4 * stretch
    return call(
        attend_kernel, "attend", ix, (4,), list(pieces), [ANY] * 4,
        [shaped((stretch, 128))] * 4 + [shaped((length, 128), F32), shaped((4, 16, stretch), F32)],
        [pl.BlockSpec((stretch, 128), lambda i, m: (0, 0))] * 4
        + [
            pl.BlockSpec((stretch, 128), lambda i, m: (i ^ m[ME], 0)),
            pl.BlockSpec((1, 16, stretch), lambda i, m: (i ^ m[ME], 0, 0)),
        ],
        [pltpu.VMEM((length, 384), LOW), pltpu.SemaphoreType.DMA((4,))], after=after,
    )


def attend_back_kernel(
    ix, p0, p1, p2, p3, u0, u1, u2, u3, raw_ref, lse_ref, cos_ref, sin_ref, o0, o1, o2, o3,
    held, up, query_at, up_at, delta, query_sum, key_sum, value_sum, sems,
):
    me = ix[ME]
    turn = pl.program_id(0)
    count = pl.num_programs(0)
    stretch = p0.shape[0]
    half = stretch // 2
    here = turn ^ me

    @pl.when(turn == 0)
    def _():
        rows = [pl.ds((me ^ k) * stretch, stretch) for k in range(4)]
        copy_all(
            [(ref, held.at[rows[k]]) for k, ref in enumerate((p0, p1, p2, p3))]
            + [(ref, up.at[rows[k]]) for k, ref in enumerate((u0, u1, u2, u3))],
            sems,
        )
        query_sum[...] = jnp.zeros_like(query_sum)

        def prepare(at, _):
            rows = pl.ds(at * stretch, stretch)
            query, upstream = held[rows, 0:128], up[rows, :]
            turned = (upstream.astype(F32) * raw_ref[rows, :]).T
            for head in range(2):
                query_at[head, rows, :] = own_lanes(query, head)
                up_at[head, rows, :] = own_lanes(upstream, head)
                total = jnp.sum(turned[head * 64 : head * 64 + 64], axis=0, keepdims=True)
                delta[at, head * 8 : head * 8 + 8, :] = jnp.broadcast_to(total, (8, stretch))
            return 0

        lax.fori_loop(0, count, prepare, 0)

    here_rows = pl.ds(here * stretch, stretch)
    key, value = held[here_rows, 128:256], held[here_rows, 256:384]
    keys = [own_lanes(key, head) for head in range(2)]
    values = [own_lanes(value, head) for head in range(2)]
    keys_turned = [own.T for own in keys]

    def step(at, queries, kept, diagonal):
        size = queries.stop - queries.start
        rows = pl.ds(at * stretch + queries.start, size)
        query, upstream = held[rows, 0:128], up[rows, :]
        key_total = value_total = query_total = None
        for head in range(2):
            scores = against(keys[head][:kept], query)
            lse = lse_ref[at, head * 8 : head * 8 + 1, queries]
            chance = jnp.exp(scores - lse)
            if diagonal:
                down = lax.broadcasted_iota(jnp.int32, scores.shape, 0)
                along = lax.broadcasted_iota(jnp.int32, scores.shape, 1) + queries.start
                chance = jnp.where(along >= down, chance, 0.0)
            chance_back = against(values[head][:kept], upstream)
            shift = delta[at, head * 8 : head * 8 + 1, queries]
            score_back = (chance * (chance_back - shift)).astype(LOW)
            value_part = dot(chance.astype(LOW), up_at[head, rows, :])
            key_part = dot(score_back, query_at[head, rows, :])
            query_part = dot(keys_turned[head][:, :kept], score_back)
            if head == 0:
                value_total, key_total, query_total = value_part, key_part, query_part
            else:
                value_total += value_part
                key_total += key_part
                query_total += query_part
        columns = pl.ds(pl.multiple_of(at * stretch + queries.start, 128), size)
        query_sum[:, columns] += query_total
        return key_total, value_total

    key_sum[...], value_sum[...] = step(here, slice(half, stretch), stretch, True)
    key_total, value_total = step(here, slice(0, half), half, True)
    key_sum[:half] += key_total
    value_sum[:half] += value_total

    def later(at, _):
        key_total, value_total = step(at, slice(0, stretch), stretch, False)
        key_sum[...] += key_total
        value_sum[...] += value_total
        return 0

    lax.fori_loop(here + 1, count, later, 0)

    def back_rope(rows, at):
        places = pl.ds(at * stretch, stretch)
        return rows * cos_ref[places, :] - half_turn(rows) * sin_ref[places, :]

    key_low, value_low = back_rope(key_sum[...], here).astype(LOW), value_sum[...].astype(LOW)
    for slot, out in enumerate((o0, o1, o2, o3)):

        @pl.when(turn == slot)
        def _():
            out[:, 128:256] = key_low
            out[:, 256:384] = value_low

    @pl.when(turn == count - 1)
    def _():
        for slot, out in enumerate((o0, o1, o2, o3)):
            columns = pl.ds(pl.multiple_of((slot ^ me) * stretch, 128), stretch)
            rows = query_sum[:, columns].T * HEAD_DIM**-0.5
            out[:, 0:128] = back_rope(rows, slot ^ me).astype(LOW)


def attend_back(ix, pieces, upstreams, raw, lse, tables, after):
    stretch = pieces[0].shape[0]
    length = 4 * stretch
    whole = lambda i, m: (0, 0)
    return call(
        attend_back_kernel, "attend_back", ix, (4,), [*pieces, *upstreams, raw, lse, *tables],
        [ANY] * 8
        + [pl.BlockSpec((length, 128), whole), pl.BlockSpec((4, 16, stretch), lambda i, m: (0, 0, 0))]
        + [pl.BlockSpec((length, 128), whole)] * 2,
        [shaped((stretch, 384))] * 4,
        [pl.BlockSpec((stretch, 384), whole)] * 4,
        [
            pltpu.VMEM((length, 384), LOW),
            pltpu.VMEM((length, 128), LOW),
            pltpu.VMEM((2, length, 128), LOW),
            pltpu.VMEM((2, length, 128), LOW),
            pltpu.VMEM((4, 16, stretch), F32),
            pltpu.VMEM((128, length), F32),
            pltpu.VMEM((stretch, 128), F32),
            pltpu.VMEM((stretch, 128), F32),
            pltpu.SemaphoreType.DMA((8,)),
        ],
        after=after,
    )


def quarter_outs(rows, width, step):
    return (
        [shaped((2, rows // 4, width))] * 2,
        [pl.BlockSpec((2, rows // 4, step), lambda i, m: (0, 0, i))] * 2,
    )


def in_quarters(t, ref, held, columns=slice(None)):
    rows = ref.shape[0] // 4
    return [
        (ref.at[pl.ds((t ^ k) * rows, rows)], held.at[pl.ds(place * rows, rows), columns])
        for place, k in enumerate((0, 2, 1, 3))
    ]


def store_quarters(total, keep_ref, send_ref):
    rows = keep_ref.shape[1]
    for k in range(2):
        keep_ref[k] = total[k * rows : (k + 1) * rows].astype(LOW)
        send_ref[k] = total[(2 + k) * rows : (3 + k) * rows].astype(LOW)


def feed_down_kernel(ix, left_ref, right_ref, keep_ref, send_ref, held, sems):
    @pl.when(pl.program_id(0) == 0)
    def _():
        copy_all(in_quarters(ix[T], left_ref, held), sems)

    store_quarters(dot(held[...], right_ref[...]), keep_ref, send_ref)


def feed_down(ix, hidden, w_down, after=()):
    rows, units = hidden.shape
    width = w_down.shape[1]
    step = 512
    outs, out_specs = quarter_outs(rows, width, step)
    return call(
        feed_down_kernel, "feed_down", ix, (width // step,), [hidden, w_down],
        [ANY, pl.BlockSpec((units, step), lambda i, m: (m[ME] % 2, i))], outs, out_specs,
        [pltpu.VMEM((rows, units), LOW), pltpu.SemaphoreType.DMA((4,))], after=after,
    )


def join_heads_kernel(ix, a0, a1, a2, a3, w0, w1, w2, w3, keep_ref, send_ref, held, sems):
    @pl.when(pl.program_id(0) == 0)
    def _():
        copy_all(
            [
                pair
                for k, ref in enumerate((a0, a1, a2, a3))
                for pair in in_quarters(ix[T], ref, held, slice(k * 128, (k + 1) * 128))
            ],
            sems,
        )

    right = jnp.concatenate([w0[...], w1[...], w2[...], w3[...]], axis=0)
    store_quarters(dot(held[...], right), keep_ref, send_ref)


def join_heads(ix, mixed, w_out, after=()):
    rows = mixed[0].shape[0]
    width = w_out.shape[1]
    step = 1024

    def heads(slot):
        return pl.BlockSpec((128, step), lambda i, m: (m[ME] ^ slot, i))

    outs, out_specs = quarter_outs(rows, width, step)
    return call(
        join_heads_kernel, "join_heads", ix, (width // step,), [*mixed] + [w_out] * 4,
        [ANY] * 4 + [heads(slot) for slot in range(4)], outs, out_specs,
        [pltpu.VMEM((rows, 512), LOW), pltpu.SemaphoreType.DMA((16,))], after=after,
    )


def project_back_kernel(ix, *refs):
    keep_ref, send_ref, held, sems = refs[16:]

    @pl.when(pl.program_id(0) == 0)
    def _():
        copy_all(
            [
                pair
                for k, ref in enumerate(refs[:4])
                for pair in in_quarters(ix[T], ref, held, slice(k * 384, (k + 1) * 384))
            ],
            sems,
        )

    right = jnp.concatenate([ref[...] for ref in refs[4:16]], axis=1)
    store_quarters(against(held[...], right), keep_ref, send_ref)


def project_back(ix, back, weights, after):
    rows = back[0].shape[0]
    width = weights[0].shape[0]
    step = 512

    def heads(slot):
        return pl.BlockSpec((step, 128), lambda i, m: (i, m[ME] ^ slot))

    outs, out_specs = quarter_outs(rows, width, step)
    return call(
        project_back_kernel, "project_back", ix, (width // step,),
        [*back] + [w for slot in range(4) for w in weights],
        [ANY] * 4 + [heads(slot) for slot in range(4) for w in weights], outs, out_specs,
        [pltpu.VMEM((rows, 1536), LOW), pltpu.SemaphoreType.DMA((16,))], after=after,
    )


def rows_call(kernel, name, ix, quarters, others, outs, sums=0, after=()):
    arrays = [a if isinstance(a, tuple) else (a, None) for a in (*quarters, *others)]
    rows, width = arrays[0][0].shape[-2:]
    step = rows // 2

    def spec(array, which):
        if which is not None:
            return pl.BlockSpec((None, step, width), lambda i, m: (which, i, 0))
        if array.shape[0] == 1:
            return pl.BlockSpec((1, width), lambda i, m: (0, 0))
        if array.shape[0] == rows:
            return pl.BlockSpec((step, width), lambda i, m: (i, 0))
        return pl.BlockSpec((step, width), lambda i, m: (2 * m[T] + i, 0))

    return call(
        kernel, name, ix, (2,), [array for array, _ in arrays], [spec(*pair) for pair in arrays],
        [shaped((rows, width), dtype) for dtype in outs] + [shaped((1, width), F32)] * sums,
        [pl.BlockSpec((step, width), lambda i, m: (i, 0))] * len(outs)
        + [pl.BlockSpec((1, width), lambda i, m: (0, 0))] * sums,
        after=after,
    )


def wide_sum(*refs):
    return sum(ref[...].astype(F32) for ref in refs)


def sum_kernel(ix, *refs):
    refs[-1][...] = wide_sum(*refs[:-1]).astype(LOW)


def sums_to_send(ix, arrays, after=()):
    return rows_call(sum_kernel, "sums", ix, arrays, [], [LOW], after=after)[0]


def middle_kernel(ix, one, two, y_ref, tok_ref, gain_ref, middle_ref, second_ref):
    middle = tok_ref[...].astype(F32) + wide_sum(one, two, y_ref)
    middle_ref[...] = middle
    normed, _ = normalize(middle)
    second_ref[...] = (normed * gain_ref[...]).astype(LOW)


def add_rows(out_ref, rows):
    part = jnp.sum(rows, axis=0, keepdims=True)

    @pl.when(pl.program_id(0) == 0)
    def _():
        out_ref[...] = part

    @pl.when(pl.program_id(0) != 0)
    def _():
        out_ref[...] += part


def middle_back_kernel(ix, one, two, y_ref, z_ref, middle_ref, cot_ref, gain_ref, grad_ref, low_ref, sum_ref):
    second_sum = wide_sum(one, two, y_ref, z_ref)
    normed, inverse = normalize(middle_ref[...])
    grad = cot_ref[...].astype(F32) + norm_back(second_sum, normed, inverse, gain_ref[...])
    grad_ref[...] = grad
    low_ref[...] = grad.astype(LOW)
    add_rows(sum_ref, second_sum * normed)


def output_kernel(ix, one, two, y_ref, z_ref, middle_ref, out_ref):
    out_ref[...] = (middle_ref[...] + wide_sum(one, two, y_ref, z_ref)).astype(LOW)


def input_kernel(ix, one, two, y_ref, grad_ref, tok_ref, gain_ref, mlp_ref, out_ref, total):
    here, last = pl.program_id(0), pl.num_programs(0) - 1

    @pl.when(here < last)
    def _():
        first_sum = wide_sum(one, two, y_ref)
        normed, inverse = normalize(tok_ref[...].astype(F32))
        out_ref[...] = (grad_ref[...] + norm_back(first_sum, normed, inverse, gain_ref[...])).astype(LOW)
        add_rows(total, first_sum * normed)

    @pl.when(here == last)
    def _():
        sums = jnp.concatenate([total[...], mlp_ref[...], jnp.zeros((14, total.shape[1]), F32)], axis=0)
        out_ref[0:16, :] = sums.astype(LOW)


def input_back(ix, keep, core, y, grad, tokens, gain, mlp_sum, after):
    rows, width = grad.shape
    step = rows // 2
    at = lambda i: jnp.minimum(i, 1)
    block = pl.BlockSpec((None, step, width), lambda i, m: (0, at(i), 0))
    row = pl.BlockSpec((step, width), lambda i, m: (at(i), 0))
    single = pl.BlockSpec((1, width), lambda i, m: (0, 0))
    return call(
        input_kernel, "input_back", ix, (3,), [keep, core, y, grad, tokens, gain, mlp_sum],
        [block, block, row, row, pl.BlockSpec((step, width), lambda i, m: (2 * m[T] + at(i), 0)), single, single],
        shaped((rows + 16, width)), pl.BlockSpec((step, width), lambda i, m: (i, 0)),
        [pltpu.VMEM((1, width), F32)], after=after,
    )


def copied_kernel(ix, in_ref, out_ref):
    out_ref[...] = in_ref[...]


def copied(ix, rows, after=()):
    count, width = rows.shape
    spec = pl.BlockSpec((count // 2, width), lambda i, m: (i, 0))
    return call(copied_kernel, "copied", ix, (2,), [rows], [spec], shaped((count, width)), spec, after=after)


def join_input_kernel(ix, q0, q1, q2, q3, out_ref, sum_ref, held, sems):
    rows = out_ref.shape[0] // 4
    ins, outs = [], []
    for k, ref in enumerate((q0, q1, q2, q3)):
        ins.append(pltpu.make_async_copy(ref, held.at[k], sems.at[k]))
        at = pl.ds((ix[T] ^ k) * rows, rows)
        outs.append(pltpu.make_async_copy(held.at[k, pl.ds(0, rows)], out_ref.at[at], sems.at[4 + k]))
    for copy in ins:
        copy.start()
    total = jnp.zeros(sum_ref.shape, F32)
    for k, (one, two) in enumerate(zip(ins, outs)):
        one.wait()
        two.start()
        total = total + held[k, rows : rows + 16, :].astype(F32)
    sum_ref[...] = total
    for copy in outs:
        copy.wait()


def join_input(ix, pieces, after):
    rows, width = pieces[0].shape
    rows -= 16
    return call(
        join_input_kernel, "join", ix, (1,), list(pieces), [ANY] * 4,
        [shaped((4 * rows, width)), shaped((16, width), F32)],
        [ANY, pl.BlockSpec((16, width), lambda i, m: (0, 0))],
        [pltpu.VMEM((4, rows + 16, width), LOW), pltpu.SemaphoreType.DMA((8,))], after=after,
    )


def normalize(vector):
    inverse = lax.rsqrt(jnp.mean(vector * vector, axis=-1, keepdims=True) + EPS)
    return (vector * inverse, inverse)


def norm_back(grad_rows, normed, inverse, gain):
    scaled = grad_rows * gain
    return inverse * (scaled - normed * jnp.mean(scaled * normed, axis=-1, keepdims=True))


def tie(ix, value, after):
    return pl.pallas_call(
        lambda *refs: None,
        grid_spec=pltpu.PrefetchScalarGridSpec(
            num_scalar_prefetch=1, grid=(1,), in_specs=[ANY] * (1 + len(after)), out_specs=ANY
        ),
        out_shape=shaped(value.shape, value.dtype),
        input_output_aliases={1: 0},
        cost_estimate=pl.CostEstimate(flops=0, bytes_accessed=0, transcendentals=0),
        name="tie",
    )(ix, value, *after)


def spread(quarter, hold=lambda two: two, late=lambda quarter: quarter):
    two = hold(swap(quarter, TENSOR, 2))
    one = swap(late(quarter), TENSOR, 1)
    three = swap(two, TENSOR, 1)
    return (quarter, one, two, three)


def quarter_copies(t, pieces, held):
    rows = pieces[0].shape[0]
    return [(ref, held.at[pl.ds((t ^ k) * rows, rows)]) for k, ref in enumerate(pieces)]


def join_kernel(ix, q0, q1, q2, q3, out_ref, held, sems):
    rows = q0.shape[0]
    ins, outs = [], []
    for k, ref in enumerate((q0, q1, q2, q3)):
        ins.append(pltpu.make_async_copy(ref, held.at[k], sems.at[k]))
        at = pl.ds((ix[T] ^ k) * rows, rows)
        outs.append(pltpu.make_async_copy(held.at[k], out_ref.at[at], sems.at[4 + k]))
    for copy in ins:
        copy.start()
    for one, two in zip(ins, outs):
        one.wait()
        two.start()
    for copy in outs:
        copy.wait()


def join(ix, pieces, after=()):
    rows, width = pieces[0].shape
    return call(
        join_kernel, "join", ix, (1,), list(pieces), [ANY] * 4,
        shaped((4 * rows, width)), ANY,
        [pltpu.VMEM((4, rows, width), LOW), pltpu.SemaphoreType.DMA((8,))], after=after,
    )


def mine_kernel(ix, *refs):
    count = len(refs) // 2
    rows = refs[count].shape[0]
    at = pl.ds(ix[T] * rows, rows)
    copy_all([(refs[k].at[at], refs[count + k]) for k in range(count)], refs[-1])


def mine(ix, arrays, after):
    count, width = arrays[0].shape
    size = len(arrays)
    return call(
        mine_kernel, "quarter", ix, (1,), list(arrays), [ANY] * size, [shaped((count // 4, width))] * size,
        [pl.BlockSpec((count // 4, width), lambda i, m: (0, 0))] * size, [pltpu.SemaphoreType.DMA((size,))],
        after=after,
    )


def others_kernel(ix, rows_ref, out_ref, sems):
    copy_all([(rows_ref.at[ix[ME] ^ k], out_ref.at[k - 1]) for k in range(1, 4)], sems)


def others(ix, rows, after):
    shape = (3,) + rows.shape[1:]
    return call(
        others_kernel, "others", ix, (1,), [rows], [ANY], shaped(shape),
        pl.BlockSpec(shape, lambda i, m: (0, 0, 0)), [pltpu.SemaphoreType.DMA((3,))], after=after,
    )


def tables_kernel(ix, freq_ref, cos_ref, sin_ref):
    rows = cos_ref.shape[0]
    lane = lax.broadcasted_iota(jnp.int32, (1, 128), 1)
    place = pl.program_id(0) * rows + lax.broadcasted_iota(jnp.int32, (rows, 128), 0)
    angle = place.astype(F32) * freq_ref[0:1, :]
    cos_ref[...] = jnp.cos(angle)
    sin_ref[...] = jnp.where((lane % HEAD_DIM) < HEAD_DIM // 2, -1.0, 1.0) * jnp.sin(angle)


def all_rope_tables(ix, count, after):
    step = 768
    return call(
        tables_kernel, "rope_tables", ix, (count // step,), [rope_freq().reshape(1, 128)],
        [pl.BlockSpec((1, 128), lambda i, m: (0, 0))], [shaped((count, 128), F32)] * 2,
        [pl.BlockSpec((step, 128), lambda i, m: (i, 0))] * 2, after=after,
    )


def hidden_back_kernel(ix, cot_ref, w_ref, out_ref):
    out_ref[...] = against(cot_ref[...], w_ref[...])


def far_rows(array, rows):
    return (lambda m: (m[ME] % 2) ^ 1) if array.shape[0] > rows else (lambda m: 0)


def hidden_back(ix, cotangent, rows, w_down, after=()):
    width = cotangent.shape[1]
    units = w_down.shape[0] // 2
    step = 512
    block = far_rows(cotangent, rows)
    return call(
        hidden_back_kernel, "hidden_back", ix, (units // step,), [cotangent, w_down],
        [
            pl.BlockSpec((rows, width), lambda i, m: (block(m), 0)),
            pl.BlockSpec((step, width), lambda i, m: ((m[ME] % 2) * (units // step) + i, 0)),
        ],
        shaped((rows, units), F32), pl.BlockSpec((rows, step), lambda i, m: (0, i)), after=after,
    )


def feed_kernel(ix, *refs, count):
    pieces = refs[:count]
    wg_ref, wu_ref, hb_ref, wg_rows, wu_rows, rows_ref, hid_ref, gb_ref, ub_ref, keep_ref, send_ref = refs[count:-4]
    held, gate_back, up_back, sems = refs[-4:]
    t = ix[T]
    here = pl.program_id(0)
    rows, units = gate_back.shape
    step = wg_ref.shape[1]
    forward = units // step
    quarter = rows // 4

    @pl.when(here == 0)
    def _():
        if count == 1:
            copy_all([(pieces[0].at[pl.ds((1 - ix[ME] % 2) * rows, rows)], held)], sems)
        else:
            copy_all(quarter_copies(t, pieces, held), sems)
        pltpu.make_async_copy(held, rows_ref, sems.at[4]).start()

    @pl.when(here < forward)
    def _():
        second = held[...]
        gate = dot(second, wg_ref[...])
        up = dot(second, wu_ref[...])
        back = hb_ref[...]
        sig = 0.5 + 0.5 * jnp.tanh(0.5 * gate)
        swish = gate * sig
        hid_ref[...] = (swish * up).astype(LOW)
        gate_low = (back * up * (sig + swish * (1.0 - sig))).astype(LOW)
        up_low = (back * swish).astype(LOW)
        gb_ref[...] = gate_low
        ub_ref[...] = up_low
        columns = pl.ds(pl.multiple_of(here * step, step), step)
        for k in range(4):
            slot = k ^ t
            place = pl.ds(pl.multiple_of(((slot & 1) * 2 + (slot >> 1)) * quarter, quarter), quarter)
            gate_back[place, columns] = gate_low[k * quarter : (k + 1) * quarter]
            up_back[place, columns] = up_low[k * quarter : (k + 1) * quarter]

    @pl.when(here >= forward)
    def _():
        total = against(gate_back[...], wg_rows[...]) + against(up_back[...], wu_rows[...])
        store_quarters(total, keep_ref, send_ref)

    @pl.when(here == pl.num_programs(0) - 1)
    def _():
        pltpu.make_async_copy(held, rows_ref, sems.at[4]).wait()


def feed(ix, pieces, w_gate, w_up, back, after=()):
    rows, width = back.shape[0], pieces[0].shape[1]
    units = w_gate.shape[1] // 2
    step, wide = 256, 512
    forward = units // step
    first = lambda i: jnp.minimum(i, forward - 1)
    then = lambda i: jnp.maximum(i - forward, 0)
    weight = pl.BlockSpec((width, step), lambda i, m: (0, (m[ME] % 2) * forward + first(i)))
    weight_rows = pl.BlockSpec((wide, units), lambda i, m: (then(i), m[ME] % 2))
    block = pl.BlockSpec((rows, step), lambda i, m: (0, first(i)))
    return call(
        functools.partial(feed_kernel, count=len(pieces)), "feed", ix, (forward + width // wide,),
        [*pieces, w_gate, w_up, back, w_gate, w_up],
        [ANY] * len(pieces) + [weight] * 2 + [block] + [weight_rows] * 2,
        [shaped((rows, width))] + [shaped((rows, units))] * 3 + [shaped((2, rows // 4, width))] * 2,
        [ANY, block, block, block] + [pl.BlockSpec((2, rows // 4, wide), lambda i, m: (0, 0, then(i)))] * 2,
        [
            pltpu.VMEM((rows, width), LOW),
            pltpu.VMEM((rows, units), LOW),
            pltpu.VMEM((rows, units), LOW),
            pltpu.SemaphoreType.DMA((5,)),
        ],
        after=after,
    )


def branch_back_kernel(ix, q0, q1, q2, q3, w0, w1, w2, w3, rows_ref, o0, o1, o2, o3, held, sems):
    rows = q0.shape[0]
    copies = [
        pltpu.make_async_copy(a, b, sems.at[k])
        for k, (a, b) in enumerate(quarter_copies(ix[T], (q0, q1, q2, q3), held))
    ]
    for copy in copies:
        copy.start()
    weight = jnp.concatenate([w0[...], w1[...], w2[...], w3[...]], axis=0)
    for k, copy in enumerate(copies):
        copy.wait()
        at = pl.ds(pl.multiple_of((ix[T] ^ k) * rows, rows), rows)
        flat = against(held[at, :], weight).astype(LOW)
        for slot, out in enumerate((o0, o1, o2, o3)):
            out[at, :] = flat[:, slot * 128 : (slot + 1) * 128]
    keep = pltpu.make_async_copy(held, rows_ref, sems.at[4])
    keep.start()
    keep.wait()


def branch_back(ix, pieces, w_out, after):
    rows, width = pieces[0].shape
    rows = 4 * rows

    def heads(slot):
        return pl.BlockSpec((128, width), lambda i, m: (m[ME] ^ slot, 0))

    return call(
        branch_back_kernel, "branch_back", ix, (1,), [*pieces] + [w_out] * 4,
        [ANY] * 4 + [heads(slot) for slot in range(4)],
        [shaped((rows, width))] + [shaped((rows, 128))] * 4,
        [ANY] + [pl.BlockSpec((rows, 128), lambda i, m: (0, 0))] * 4,
        [pltpu.VMEM((rows, width), LOW), pltpu.SemaphoreType.DMA((5,))], after=after,
    )


def wgrad_kernel(ix, l0, l1, r0, r1, out_ref):
    out_ref[0] = (across(l0[...], r0[...]) + across(l1[...], r1[...])).astype(LOW)


def wgrad_kernel(ix, l0, l1, r0, r1, out_ref):
    out_ref[0] = (across(l0[...], r0[...]) + across(l1[...], r1[...])).astype(LOW)


def wgrad(ix, wide, free, name, after=()):
    rows, units = free[0].shape
    share = 256

    def wide_spec(array):
        block = far_rows(array, rows)
        return pl.BlockSpec((rows, share), lambda i, m: (block(m), i ^ (m[ME] % 2)))

    return call(
        wgrad_kernel, name, ix, (8,), [*wide, *free],
        [wide_spec(array) for array in wide] + [pl.BlockSpec((rows, units), lambda i, m: (0, 0))] * 2,
        shaped((8, share, units)), pl.BlockSpec((1, share, units), lambda i, m: (i, 0, 0)), after=after,
    )


def add_blocks_kernel(ix, a_ref, b_ref, *refs):
    total = (a_ref[...].astype(F32) + b_ref[...].astype(F32)).astype(LOW)
    size = refs[0].shape[0]
    for k, ref in enumerate(refs):
        ref[...] = total[k * size : (k + 1) * size]


def add_blocks(ix, one, two, parts, after=()):
    shape = (one.shape[0] // parts,) + one.shape[1:]
    whole = pl.BlockSpec(one.shape, lambda i, m: (0, 0, 0))
    return call(
        add_blocks_kernel, "add_blocks", ix, (1,), [one, two], [whole] * 2,
        [shaped(shape)] * parts, [pl.BlockSpec(shape, lambda i, m: (0, 0, 0))] * parts, after=after,
    )


def one_block_kernel(ix, in_ref, out_ref):
    out_ref[...] = in_ref[...]


def one_block(ix, blocks, which, after=()):
    shape = (1,) + blocks.shape[1:]
    return call(
        one_block_kernel, "one_block", ix, (1,), [blocks],
        [pl.BlockSpec(shape, lambda i, m: (which, 0, 0))], shaped(shape),
        pl.BlockSpec(shape, lambda i, m: (0, 0, 0)), after=after,
    )


def halves_kernel(ix, own_ref, other_ref, out_ref, *, axis):
    which = ix[ME] % 2
    for place, ref in ((which, own_ref), (1 - which, other_ref)):
        value = ref[...].astype(F32)
        if axis == 0:
            value = value.T
        size = value.shape[axis]
        at = pl.ds(pl.multiple_of(place * size, size), size)
        if axis == 0:
            out_ref[at, :] = value
        else:
            out_ref[:, at] = value


def halves(ix, blocks, other, axis, after=()):
    share, units = blocks.shape[1:]
    shape = (2 * units, share) if axis == 0 else (share, 2 * units)
    whole = lambda i, m: (0, 0)
    return call(
        functools.partial(halves_kernel, axis=axis), "halves", ix, (1,), [blocks, other],
        [pl.BlockSpec((None, share, units), lambda i, m: (0, 0, 0))] * 2,
        shaped(shape, F32), pl.BlockSpec(shape, whole), after=after,
    )


def out_wgrad_kernel(ix, a0, a1, a2, a3, rows_ref, own_ref, far_ref, held):
    for slot, ref in enumerate((a0, a1, a2, a3)):
        at = pl.ds(pl.multiple_of((slot ^ ix[ME]) * 128, 128), 128)
        held[at, :] = across(ref[...], rows_ref[...]).astype(LOW)
    for half, out in enumerate((own_ref, far_ref)):

        @pl.when(pl.program_id(0) // 4 == half)
        def _():
            out[0] = held[...]


def out_wgrad(ix, mixed, rows, after=()):
    count, width = rows.shape
    share = 256
    return call(
        out_wgrad_kernel, "out_wgrad", ix, (width // share,), [*mixed, rows],
        [pl.BlockSpec((count, 128), lambda i, m: (0, 0))] * 4
        + [pl.BlockSpec((count, share), lambda i, m: (0, i ^ (m[DP] * 4 + m[ME])))],
        [shaped((4, 512, share))] * 2,
        [
            pl.BlockSpec((1, 512, share), lambda i, m: (jnp.minimum(i, 3), 0, 0)),
            pl.BlockSpec((1, 512, share), lambda i, m: (jnp.maximum(i - 4, 0), 0, 0)),
        ],
        [pltpu.VMEM((512, share), LOW)], after=after,
    )


def project_wgrad_kernel(ix, first_ref, f0, f1, f2, f3, b0, b1, b2, b3, own_ref, far_ref, held, total, sems):
    me, t = ix[ME], ix[T]
    turn = pl.program_id(0)
    quarter = f0.shape[1]

    def copies(slot):
        if slot == 0:
            return [pltpu.make_async_copy(first_ref, held.at[0], sems.at[0, 0])]
        return [
            pltpu.make_async_copy(
                ref.at[slot - 1], held.at[slot, pl.ds((t ^ k) * quarter, quarter)], sems.at[slot, k]
            )
            for k, ref in enumerate((f0, f1, f2, f3))
        ]

    @pl.when(turn == 0)
    def _():
        for slot in range(4):
            for copy in copies(slot):
                copy.start()

    for slot, back in enumerate((b0, b1, b2, b3)):

        @pl.when(turn == slot)
        def _():
            for copy in copies(slot):
                copy.wait()
            for block in range(8):
                at = slice(block * 256, (block + 1) * 256)
                part = across(held[slot, :, at], back[...])
                if slot == 0:
                    total[at, :] = part
                elif slot < 3:
                    total[at, :] += part
                else:
                    done = (total[at, :] + part).astype(LOW)

                    @pl.when(ix[DP] == block // 4)
                    def _():
                        own_ref[(block % 4) ^ me] = done

                    @pl.when(ix[DP] != block // 4)
                    def _():
                        far_ref[(block % 4) ^ me] = done


def project_wgrad(ix, first_in, far, back, after=()):
    rows, width = first_in.shape
    whole = lambda i, m: (0, 0)
    return call(
        project_wgrad_kernel, "project_wgrad", ix, (4,), [first_in, *far, *back],
        [ANY] * 5 + [pl.BlockSpec((rows, 384), whole)] * 4,
        [shaped((4, 256, 384))] * 2, [pl.BlockSpec((4, 256, 384), lambda i, m: (0, 0, 0))] * 2,
        [
            pltpu.VMEM((4, rows, width), LOW),
            pltpu.VMEM((width, 384), F32),
            pltpu.SemaphoreType.DMA((4, 4)),
        ],
        after=after,
    )


def add_parts_kernel(ix, a_ref, b_ref, gain_ref, *refs):
    rows = a_ref.shape[1]
    for k, out in enumerate(refs):
        out[0:rows, :] = (a_ref[k].astype(F32) + b_ref[k].astype(F32)).astype(LOW)
        gains = jnp.concatenate([gain_ref[k], jnp.zeros((14, gain_ref.shape[2]), F32)], axis=0)
        out[rows : rows + 16, 0 : gains.shape[1]] = gains.astype(LOW)
        out[rows : rows + 16, gains.shape[1] :] = jnp.zeros((16, out.shape[1] - gains.shape[1]), LOW)


def add_parts(ix, one, two, gains, after=()):
    count, rows, width = one.shape
    whole = lambda shape: pl.BlockSpec(shape, lambda i, m: (0,) * len(shape))
    shape = (rows + 16, width)
    return call(
        add_parts_kernel, "add_blocks", ix, (1,), [one, two, gains], [whole(a.shape) for a in (one, two, gains)],
        [shaped(shape)] * count, [whole(shape)] * count, after=after,
    )


def add_last_kernel(ix, a_ref, b_ref, out_ref):
    out_ref[...] = a_ref[...].astype(F32) + b_ref[...].astype(F32)


def add_last(ix, one, two, after):
    shape = one.shape[1:]
    block = pl.BlockSpec((None, *shape), lambda i, m: (0, 0, 0))
    return call(
        add_last_kernel, "add_last", ix, (1,), [one, two], [block] * 2, shaped(shape, F32),
        pl.BlockSpec(shape, lambda i, m: (0, 0)), after=after,
    )


def project_last_kernel(ix, p0, p1, p2, p3, q_ref, k_ref, v_ref, *gain_refs):
    share = q_ref.shape[0]
    for slot, ref in enumerate((p0, p1, p2, p3)):
        at = pl.ds(pl.multiple_of((slot ^ ix[ME]) * 128, 128), 128)
        for place, out in enumerate((q_ref, k_ref, v_ref)):
            out[:, at] = ref[0:share, place * 128 : (place + 1) * 128].astype(F32)
    for out in gain_refs:
        out[...] = sum(ref[share : share + 16, 0 : out.shape[1]].astype(F32) for ref in (p0, p1, p2, p3))


def project_last(ix, pieces, share, after=()):
    whole = lambda i, m: (0, 0)
    shapes = [(share, 512)] * 3 + ([(16, share)] if pieces[0].shape[0] > share else [])
    return call(
        project_last_kernel, "project_last", ix, (1,), list(pieces), [pl.BlockSpec(pieces[0].shape, whole)] * 4,
        [shaped(shape, F32) for shape in shapes], [pl.BlockSpec(shape, whole) for shape in shapes], after=after,
    )


def over_ctx(slots):
    return [slots[0]] + [swap(slots[k], CTX, k) for k in range(1, 4)]


def per_device(
    dp_size, tokens, attn_gain, w_query, w_key, w_value, w_out, mlp_gain, w_gate, w_up, w_down, cotangent
):
    rows_here, width = tokens.shape
    share = width // (4 * dp_size)
    me, t, d = lax.axis_index(CTX), lax.axis_index(TENSOR), lax.axis_index("dp")
    two_dp = dp_size == 2
    ix = jnp.stack([me, t, d if two_dp else jnp.zeros_like(d)]).astype(jnp.int32)
    order = me ^ jnp.arange(4)
    projections = (w_query, w_key, w_value)
    attn_gain, mlp_gain = attn_gain.reshape(1, -1), mlp_gain.reshape(1, -1)

    cot_mine = lax.dynamic_slice_in_dim(cotangent, t * (rows_here // 4), rows_here // 4, 0)
    tables = rope_tables(me * rows_here + jnp.arange(rows_here, dtype=jnp.int32))
    first_in, *slots = project(ix, tokens, attn_gain, tables, projections)
    pieces = over_ctx(slots)

    back_own = hidden_back(ix, cotangent, rows_here, w_down, (slots[0],))
    all_tables = all_rope_tables(ix, 4 * rows_here, (back_own,))
    (first_mine,) = mine(ix, [first_in], (all_tables[0],))
    cot_mine = tie(ix, cot_mine, (*pieces[1:], first_mine))
    cot_both = lax.all_gather(cot_mine, ("lo", *TENSOR), axis=0, tiled=True)

    *mixed_slots, raw, lse = attend(ix, pieces, (first_mine,))
    mixed = over_ctx(mixed_slots)
    keep, send = join_heads(ix, mixed, w_out, (cot_both,))
    core = swap(send, TENSOR, 1)
    low = sums_to_send(ix, [(keep, 1), (core, 1)])
    middle, second_mine = rows_call(
        middle_kernel, "middle", ix, [(keep, 0), (core, 0), swap(low, TENSOR, 2)], [tokens, mlp_gain], [F32, LOW]
    )

    second_both = lax.all_gather(second_mine, ("lo", *TENSOR), axis=0, tiled=True)
    back_far = hidden_back(ix, cot_both, rows_here, w_down, (second_mine,))
    own_pieces = spread(second_mine, lambda two: tie(ix, two, (back_far,)))
    second_own, hid_own, gb_own, ub_own, keep_own, send = feed(ix, own_pieces, w_gate, w_up, back_own)
    first_all = lax.all_gather(tie(ix, first_mine, (hid_own,)), CTX, axis=0, tiled=False)
    core_own = swap(send, TENSOR, 1)
    second_far, hid_far, gb_far, ub_far, keep, send = feed(ix, [second_both], w_gate, w_up, back_far, (hid_own,))

    seconds = (second_own, second_far)

    def over_pairs(part):
        return lax.psum_scatter(part, ("dp", "hi"), scatter_dimension=0, tiled=True) if two_dp else part

    core = swap(send, TENSOR, 1)
    part_down = wgrad(ix, (cotangent, cot_both), (hid_own, hid_far), "wgrad_down")
    low = sums_to_send(ix, [(keep, 1), (core, 1)])
    far_y = swap(low, TENSOR, 2)
    down_far = feed_down(ix, hid_far, w_down, (low,))
    low = sums_to_send(ix, [(keep, 0), (core, 0), far_y], (down_far[0],))
    far_z = swap(low, CTX, 1)
    sum_down = over_pairs(tie(ix, part_down, (far_z,)))
    low = sums_to_send(ix, [(keep_own, 1), (core_own, 1)], (low,))
    own_sums = [(keep_own, 0), (core_own, 0), swap(low, TENSOR, 2)]
    core_far = swap(down_far[1], TENSOR, 1)
    down_own = feed_down(ix, hid_own, w_down, (low,))
    low = sums_to_send(ix, [(down_far[0], 1), (core_far, 1)], (down_own[0],))
    far_down = [(down_far[0], 0), (core_far, 0), swap(low, TENSOR, 2)]
    middle_grad, branch_mine, mlp_gain_part = rows_call(
        middle_back_kernel, "middle_back", ix, [*own_sums, far_z, middle], [cotangent, mlp_gain], [F32, LOW], 1,
        (low,),
    )
    core_own = swap(down_own[1], TENSOR, 1)
    low = sums_to_send(ix, [(down_own[0], 1), (core_own, 1)], (branch_mine,))
    own_y = swap(low, TENSOR, 2)
    branch_low, *slots = branch_back(ix, spread(branch_mine), w_out, (low,))
    upstreams = over_ctx(slots)
    first_far = others(ix, first_all, (branch_low,))
    out_own, out_far = out_wgrad(ix, mixed, branch_low, (first_far,))
    part_gate = wgrad(ix, seconds, (gb_own, gb_far), "wgrad_gate", (out_own, own_y))
    sum_gate = over_pairs(tie(ix, part_gate, upstreams[1:]))

    def for_partner(blocks, after):
        return swap(blocks[1:] if after is None else one_block(ix, blocks, 1, after), CTX, 1)

    token, arrived = own_y, []
    if two_dp:
        out_other = swap(out_far, "dp", 1)
        token = one_block(ix, sum_down, 1, (out_own, *upstreams[1:]))
        down_other = swap(token, CTX, 1)
        arrived = [out_other, down_other]
    back_slots = attend_back(ix, pieces, upstreams, raw, lse, all_tables, (token, out_own, own_y))
    back = over_ctx(back_slots)

    arrived = (back_slots[0], *arrived)
    first_spread = spread(first_far, lambda two: tie(ix, two, arrived))
    qkv_own, qkv_far = project_wgrad(ix, first_in, first_spread, back_slots)
    far_low = sums_to_send(ix, far_down, (qkv_own,))
    token = far_low
    if two_dp:
        qkv_other = swap(qkv_far, "dp", 1)
        out_part = add_blocks(ix, out_own, out_other, 2, (far_low,))
        down_grad = halves(ix, sum_down, down_other, 0, (out_part[0],))
        token = down_grad
    part_up = wgrad(ix, seconds, (ub_own, ub_far), "wgrad_up", (token,))
    part_up = tie(ix, part_up, back[1:])
    sum_up = over_pairs(part_up)
    keep, send = project_back(ix, back, projections, (part_up,))
    core = swap(send, TENSOR, 1)
    low = sums_to_send(ix, [(keep, 1), (core, 1)])
    low_y = swap(low, TENSOR, 2)
    far_z = swap(tie(ix, far_low, (low,)), CTX, 1)
    token = low
    if two_dp:
        gate_low = one_block(ix, sum_gate, 1, (low,))
        gate_other = swap(gate_low, CTX, 1)
        token = gate_low
    input_mine = input_back(ix, keep, core, low_y, middle_grad, tokens, attn_gain, mlp_gain_part, (token,))
    arrived = (far_z,)
    if two_dp:
        out_z = swap(tie(ix, out_part[1], (keep,)), CTX, 2)
        arrived = (far_z, qkv_other, out_z)
    input_grad, gains = join_input(ix, spread(input_mine, lambda two: tie(ix, two, arrived)), (input_mine,))
    gains = gains[:2]
    if two_dp:
        halved = gains.reshape(2, 2, width // 2)[:, d ^ jnp.arange(2)]
        gains = halved[:, 0] + swap(halved[:, 1], "dp", 1)
        gains = gains.reshape(2, 4, share).transpose(1, 0, 2)[order]
    (output_mine,) = rows_call(
        output_kernel, "output", ix, [(down_own[0], 0), (core_own, 0), own_y, far_z, middle], [], [LOW],
        after=(input_grad,),
    )
    output = lax.all_gather(output_mine, TENSOR, axis=0, tiled=True)
    if not two_dp:
        output = copied(ix, output)
    if two_dp:
        up_low = one_block(ix, sum_up, 1, (output_mine,))
        up_other = swap(up_low, CTX, 1)
        out_part = add_blocks(ix, out_part[0], out_z, 2, (up_low,))
        out_other = swap(out_part[1], CTX, 1)
        qkv_parts = over_ctx(add_parts(ix, qkv_own, qkv_other, gains, (out_part[0],)))
        gate_grad = halves(ix, sum_gate, gate_other, 1, (qkv_parts[0],))
        up_grad = halves(ix, sum_up, up_other, 1, (gate_grad,))
        output = copied(ix, output, (up_grad,))
        *qkv, gains = project_last(ix, qkv_parts, share, (output,))
        out_grad = add_last(ix, out_part[0], out_other, (qkv[0],))
    else:
        def scattered(blocks, axis):
            blocks = jnp.moveaxis(blocks, 0, axis)
            shape = blocks.shape[:axis] + (width,) + blocks.shape[axis + 2 :]
            part = lax.psum_scatter(blocks.reshape(shape), "dp", scatter_dimension=axis, tiled=True)
            shape = part.shape[:axis] + (4, share) + part.shape[axis + 1 :]
            return jnp.moveaxis(part.reshape(shape), axis, 0)

        def in_order(blocks):
            return blocks.reshape(2, 4, *blocks.shape[1:])[:, order].reshape(blocks.shape)

        grads = []
        own_first = me % 2 ^ jnp.arange(2)
        for k, blocks in enumerate((sum_down, sum_gate, sum_up)):
            blocks = blocks.reshape(4, 2, *blocks.shape[1:])[:, own_first].reshape(blocks.shape)
            part = scattered(blocks, 0)[order].astype(F32)
            part = (part[:2] + swap(part[2:].astype(LOW), CTX, 2).astype(F32)).astype(LOW)
            grads.append(halves(ix, part, for_partner(part, None), min(k, 1)))
        down_grad, gate_grad, up_grad = grads
        qkv_parts = over_ctx(scattered(in_order(jnp.concatenate([qkv_own, qkv_far])), 0)[order])
        out_part = scattered(in_order(jnp.concatenate([out_own, out_far])), 1)[order]
        out_part = out_part[:2].astype(F32) + swap(out_part[2:], CTX, 2).astype(F32)
        out_grad = out_part[0] + swap(out_part[1].astype(LOW), CTX, 1).astype(F32)
        qkv = project_last(ix, qkv_parts, share)
        gains = lax.psum_scatter(gains, "dp", scatter_dimension=1, tiled=True)
        gains = sum(over_ctx(gains.reshape(2, 4, share).transpose(1, 0, 2)[order]))

    return (
        output,
        input_grad,
        gains[0],
        qkv[0],
        qkv[1],
        qkv[2],
        out_grad,
        gains[1],
        gate_grad,
        up_grad,
        down_grad,
    )


def solution(mesh):
    dp_size = mesh.shape["dp"]
    mesh = jax.sharding.Mesh(mesh.devices.reshape(dp_size, 2, 2, 2, 2), ("dp", *CTX, *TENSOR))
    rows, tensor = ("dp", *CTX), TENSOR
    columns = P(None, tensor)
    in_specs = (
        P(rows, None), P(), columns, columns, columns, P(tensor, None),
        P(), columns, columns, P(tensor, None), P(rows, None),
    )
    out_specs = (
        P(rows, None), P(rows, None), P(rows), P(rows, tensor), P(rows, tensor), P(rows, tensor),
        P(tensor, rows), P(rows), P(rows, tensor), P(rows, tensor), P(tensor, rows),
    )
    return jax.shard_map(
        functools.partial(per_device, dp_size),
        mesh=mesh,
        in_specs=in_specs,
        out_specs=out_specs,
        check_vma=False,
    )
```
